32 devices in a mesh: clip: 4 (over x, core), seq: 8 (over z, y).
Axes of the slice: x: 2, y: 2, z: 4, core: 2. Of those that a mesh axis runs over, the one named last changes fastest.
Arguments:
- frames_in: bfloat16 [8, 4096, 1024], P('clip', 'seq')
- noise_level: int32 [8, 16], P('clip'), may hold values from 0 to 999
- frame_time: int32 [8, 16], P('clip'), may hold values from 0 to 45, as said below
- cotangent: bfloat16 [8, 4096, 1024], P('clip', 'seq'), may hold values from -6 to 6
- joint_weight: float32 [1024, 3072], P(('clip', 'seq')), may hold values from -0.1875 to 0.1875
- output_weight: float32 [1024, 1024], P(('clip', 'seq')), may hold values from -6 to 6
- up_weight: float32 [1024, 4096], P(('clip', 'seq')), may hold values from -0.1875 to 0.1875
- down_weight: float32 [4096, 1024], P(('clip', 'seq')), may hold values from -0.09375 to 0.09375
- modulation: float32 [1024, 6144], P(('clip', 'seq')), may hold values from -0.1875 to 0.1875
- modulation_bias: float32 [6144], P(('clip', 'seq')), may hold values from -3 to 3
- first_joint: float32 [1024, 3072], P(('clip', 'seq')), may hold values from -0.0014648438 to 0.0014648438
- first_output: float32 [1024, 1024], P(('clip', 'seq')), may hold values from -0.00024414062 to 0.00024414062
- first_up: float32 [1024, 4096], P(('clip', 'seq')), may hold values from -0.00030517578 to 0.00030517578
- first_down: float32 [4096, 1024], P(('clip', 'seq')), may hold values from -0.00036621094 to 0.00036621094
- first_modulation: float32 [1024, 6144], P(('clip', 'seq')), may hold values from -0.0014648438 to 0.0014648438
- first_bias: float32 [6144], P(('clip', 'seq')), may hold values from -0.005859375 to 0.005859375
- second_joint: float32 [1024, 3072], P(('clip', 'seq')), may hold values from 5.2964666e-08 to 2.1185866e-07
- second_output: float32 [1024, 1024], P(('clip', 'seq')), may hold values from 1.58894e-09 to 6.35576e-09
- second_up: float32 [1024, 4096], P(('clip', 'seq')), may hold values from 2.3304452e-09 to 9.321781e-09
- second_down: float32 [4096, 1024], P(('clip', 'seq')), may hold values from 4.2371733e-09 to 1.6948693e-08
- second_modulation: float32 [1024, 6144], P(('clip', 'seq')), may hold values from 5.2964666e-08 to 2.1185866e-07
- second_bias: float32 [6144], P(('clip', 'seq')), may hold values from 8.4743465e-07 to 3.3897386e-06
Outputs:
- mixed: bfloat16 [8, 4096, 1024], P('clip', 'seq')
- input_grad: float32 [8, 4096, 1024], P('clip', 'seq')
- grad_joint: float32 [1024, 3072], P(('clip', 'seq'))
- grad_output: float32 [1024, 1024], P(('clip', 'seq'))
- grad_up: float32 [1024, 4096], P(('clip', 'seq'))
- grad_down: float32 [4096, 1024], P(('clip', 'seq'))
- grad_modulation: float32 [1024, 6144], P(('clip', 'seq'))
- grad_bias: float32 [6144], P(('clip', 'seq'))
- grad_norm: float32 [], replicated
- new_first_joint: float32 [1024, 3072], P(('clip', 'seq'))
- new_first_output: float32 [1024, 1024], P(('clip', 'seq'))
- new_first_up: float32 [1024, 4096], P(('clip', 'seq'))
- new_first_down: float32 [4096, 1024], P(('clip', 'seq'))
- new_first_modulation: float32 [1024, 6144], P(('clip', 'seq'))
- new_first_bias: float32 [6144], P(('clip', 'seq'))
- new_second_joint: float32 [1024, 3072], P(('clip', 'seq'))
- new_second_output: float32 [1024, 1024], P(('clip', 'seq'))
- new_second_up: float32 [1024, 4096], P(('clip', 'seq'))
- new_second_down: float32 [4096, 1024], P(('clip', 'seq'))
- new_second_modulation: float32 [1024, 6144], P(('clip', 'seq'))
- new_second_bias: float32 [6144], P(('clip', 'seq'))
- new_joint: float32 [1024, 3072], P(('clip', 'seq'))
- new_output: float32 [1024, 1024], P(('clip', 'seq'))
- new_up: float32 [1024, 4096], P(('clip', 'seq'))
- new_down: float32 [4096, 1024], P(('clip', 'seq'))
- new_modulation: float32 [1024, 6144], P(('clip', 'seq'))
- new_bias: float32 [6144], P(('clip', 'seq'))
- copy_joint: bfloat16 [1024, 3072], P(('clip', 'seq'))
- copy_output: bfloat16 [1024, 1024], P(('clip', 'seq'))
- copy_up: bfloat16 [1024, 4096], P(('clip', 'seq'))
- copy_down: bfloat16 [4096, 1024], P(('clip', 'seq'))
- copy_modulation: bfloat16 [1024, 6144], P(('clip', 'seq'))
- copy_bias: bfloat16 [6144], P(('clip', 'seq'))
The draws below stay inside these ranges and needn't reach their ends.
Inputs may be any that keep to these rules, and one draw needn't show every extreme that they name: `frame_time`: within each clip the first frame's time is 0 and each later frame's time exceeds the one before by 1 to 3; in some clip every step is 3, so that its last frame's time is 45.
All inputs are finite; a program needn't handle non-finite values.
Results may differ from the reference program's by a relative error of at most 0.015.
The reference program's roundings to bfloat16 on the way count: a program that leaves them out, or rounds other values in their place, can miss the bound.
Values may be sent and summed in bfloat16 or wider, within the bound.
No kernel may reach another device: no remote copies, remote signals or barrier semaphores. Data moves between devices by JAX's collectives and lax.ppermute only.
A program may use at most 384 MiB of HBM per device.

```python
import math
import jax
import jax.numpy as jnp
from jax import lax

D = 1024
HEADS = 16
HEAD = 64
FF = 4096
FRAMES = 16
GRID_W = 16
LEVELS = 1000
STEP = 10
PATCHES = 256
LENGTH = 4096
CLIPS = 8
PARAMS = 18880512


def draw_frames_in(key, part):
    key = jax.random.fold_in(key, 11)
    first_key, second_key = jax.random.split(key)
    ramp_base = 3.0
    base_noise = jax.random.normal(first_key, (CLIPS, LENGTH, D), jnp.float32)
    feature_ramp = ramp_base ** (jnp.arange(D, dtype=jnp.float32) / (D - 1))
    row_scale = jnp.exp(jax.random.uniform(second_key, (CLIPS, LENGTH, 1), jnp.float32, math.log(0.6), math.log(1.8)))
    return (base_noise * feature_ramp * row_scale / ramp_base ** 0.5).astype(jnp.bfloat16)


def draw_frame_time(key, part):
    key = jax.random.fold_in(key, 23)
    gap_key, pick_key = jax.random.split(key)
    frame_gaps = jax.random.randint(gap_key, (CLIPS, FRAMES), 1, 4, jnp.int32)
    chosen = jax.random.randint(pick_key, (), 0, CLIPS, jnp.int32)
    frame_gaps = jnp.where(jnp.arange(CLIPS, dtype=jnp.int32)[:, None] == chosen, 3, frame_gaps)
    frame_gaps = jnp.where(jnp.arange(FRAMES, dtype=jnp.int32)[None, :] == 0, 0, frame_gaps)
    return jnp.cumsum(frame_gaps, axis=1).astype(jnp.int32)


def place_ends(array, rng, least, high):
    extent = array.shape
    spot = [jax.random.randint(jax.random.fold_in(rng, axis), (), 0, extent[axis]) for axis in range(len(extent))]
    array = array.at[tuple(spot)].set(least)
    longest = extent.index(max(extent))
    spot[longest] = (spot[longest] + 1) % extent[longest]
    return array.at[tuple(spot)].set(high)


def steps_of(stream_key, dims, cuts, smallest, largest):
    def one(position, blocks):
        steps = jax.random.uniform(jax.random.fold_in(jax.random.fold_in(stream_key, 6), position), (blocks,), jnp.float32, smallest / len(cuts), largest / len(cuts))
        return jnp.repeat(jnp.exp(steps), dims[position] // blocks).reshape((-1,) + (1,) * (len(dims) - position - 1))

    loudness = one(*cuts[0])
    for cut in cuts[1:]:
        loudness = loudness * one(*cut)
    return loudness


def bell_draw(stream_key, dims, spread, most, cuts=(), kind=jnp.bfloat16):
    loudness = steps_of(stream_key, dims, cuts, -0.22, 0.18) if cuts else 1.0
    entries = jax.random.normal(stream_key, dims, jnp.float32) * spread * loudness
    return jnp.minimum(jnp.maximum(entries, -most), most).astype(kind)


def setup_inputs(seed: int = 0) -> dict:
    streams_of = jax.random.split(jax.random.key(seed), 23)
    return {
        "frames_in": draw_frames_in(jax.random.fold_in(streams_of[22], 71), 0),
        "noise_level": place_ends(jax.random.randint(streams_of[1], (CLIPS, FRAMES), 0, LEVELS), jax.random.fold_in(streams_of[1], 1), 0, LEVELS - 1).astype(jnp.int32),
        "frame_time": draw_frame_time(jax.random.fold_in(streams_of[22], 71), 0),
        "cotangent": bell_draw(streams_of[3], (CLIPS, LENGTH, D), 1.0, 6.0, ((0, 4), (1, 8))),
        "joint_weight": bell_draw(streams_of[4], (D, 3 * D), D ** -0.5, 0.1875, ((0, 32),), jnp.float32),
        "output_weight": bell_draw(streams_of[5], (D, D), (max(1, 2 * D // LENGTH)) ** -0.5, 6.0, ((0, 32),), jnp.float32),
        "up_weight": bell_draw(streams_of[6], (D, FF), D ** -0.5, 0.1875, ((0, 32),), jnp.float32),
        "down_weight": bell_draw(streams_of[7], (FF, D), FF ** -0.5, 0.09375, ((0, 32),), jnp.float32),
        "modulation": bell_draw(streams_of[8], (D, 6 * D), D ** -0.5, 0.1875, ((0, 32),), jnp.float32),
        "modulation_bias": bell_draw(streams_of[9], (6 * D,), 0.5, 3.0, ((0, 32),), jnp.float32),
        "first_joint": bell_draw(streams_of[10], (D, 3 * D), (1.0 / PARAMS ** 0.5), 0.0014648438, ((0, 32),), jnp.float32),
        "first_output": bell_draw(streams_of[11], (D, D), (0.17 / PARAMS ** 0.5), 0.00024414062, ((0, 32),), jnp.float32),
        "first_up": bell_draw(streams_of[12], (D, FF), (0.21 / PARAMS ** 0.5), 0.00030517578, ((0, 32),), jnp.float32),
        "first_down": bell_draw(streams_of[13], (FF, D), (0.28 / PARAMS ** 0.5), 0.00036621094, ((0, 32),), jnp.float32),
        "first_modulation": bell_draw(streams_of[14], (D, 6 * D), (1.0 / PARAMS ** 0.5), 0.0014648438, ((0, 32),), jnp.float32),
        "first_bias": bell_draw(streams_of[15], (6 * D,), (4.0 / PARAMS ** 0.5), 0.005859375, ((0, 32),), jnp.float32),
        "second_joint": jnp.clip(jnp.exp(math.log(2.1185866216910654e-07) - 1.3862944 * jax.random.uniform(streams_of[16], (D, 3 * D), jnp.float32) ** steps_of(streams_of[16], (D, 3 * D), ((0, 32),), -0.2, 0.2)), 5.2964665542276634e-08, 2.1185866216910654e-07),
        "second_output": jnp.clip(jnp.exp(math.log(6.355759918363901e-09) - 1.3862944 * jax.random.uniform(streams_of[17], (D, D), jnp.float32) ** steps_of(streams_of[17], (D, D), ((0, 32),), -0.2, 0.2)), 1.5889399795909753e-09, 6.355759918363901e-09),
        "second_up": jnp.clip(jnp.exp(math.log(9.321780680693337e-09) - 1.3862944 * jax.random.uniform(streams_of[18], (D, FF), jnp.float32) ** steps_of(streams_of[18], (D, FF), ((0, 32),), -0.2, 0.2)), 2.330445170173334e-09, 9.321780680693337e-09),
        "second_down": jnp.clip(jnp.exp(math.log(1.694869311563707e-08) - 1.3862944 * jax.random.uniform(streams_of[19], (FF, D), jnp.float32) ** steps_of(streams_of[19], (FF, D), ((0, 32),), -0.2, 0.2)), 4.2371732789092675e-09, 1.694869311563707e-08),
        "second_modulation": jnp.clip(jnp.exp(math.log(2.1185866216910654e-07) - 1.3862944 * jax.random.uniform(streams_of[20], (D, 6 * D), jnp.float32) ** steps_of(streams_of[20], (D, 6 * D), ((0, 32),), -0.2, 0.2)), 5.2964665542276634e-08, 2.1185866216910654e-07),
        "second_bias": jnp.clip(jnp.exp(math.log(3.3897385947057046e-06) - 1.3862944 * jax.random.uniform(streams_of[21], (6 * D,), jnp.float32) ** steps_of(streams_of[21], (6 * D,), ((0, 32),), -0.2, 0.2)), 8.474346486764261e-07, 3.3897385947057046e-06),
    }


@jax.custom_vjp
def low(v):
    return lax.optimization_barrier(v.astype(jnp.bfloat16)).astype(jnp.float32)

@jax.custom_vjp
def low_back(v):
    return v

def low_keep(v):
    return (low(v), None)

def low_pass(kept, grad):
    return (grad,)

def back_keep(v):
    return (v, None)

def back_low(kept, grad):
    return (low(grad),)
low.defvjp(low_keep, low_pass)
low_back.defvjp(back_keep, back_low)
norm_epsilon = 1e-06
adam_epsilon = 1e-08
first_decay = 0.5
second_decay = 0.5
weight_decay = 0.1
clip_limit = 1.0
highest = lax.Precision.HIGHEST

def sinusoid(levels):
    half_width = D // 2
    frequency = jnp.exp(-math.log(10000.0) * jnp.arange(half_width, dtype=jnp.float32) / half_width)
    angles = levels.astype(jnp.float32)[..., None] * frequency
    return jnp.concatenate([jnp.cos(angles), jnp.sin(angles)], axis=-1)

def rotary_angles(frame_time, first_place, number):
    places = first_place + jnp.arange(number, dtype=jnp.int32)
    frame_ids = places // PATCHES
    patch_row = (places % PATCHES // GRID_W).astype(jnp.float32)
    column = (places % GRID_W).astype(jnp.float32)
    matches = frame_ids[:, None] == jnp.arange(FRAMES, dtype=jnp.int32)[None, :]
    moment = lax.optimization_barrier(jnp.sum(jnp.where(matches[None], frame_time[:, None, :], 0), axis=-1)).astype(jnp.float32)
    pair_count = HEAD // 2
    time_pairs = HEAD // 8
    grid_pairs = 3 * HEAD // 16
    pair_ids = jnp.arange(pair_count, dtype=jnp.int32)
    offset = jnp.where(pair_ids < time_pairs, 0, jnp.where(pair_ids < time_pairs + grid_pairs, time_pairs, time_pairs + grid_pairs))
    length = jnp.where(pair_ids < time_pairs, time_pairs, grid_pairs)
    frequency = jnp.exp(-math.log(10000.0) * (pair_ids - offset).astype(jnp.float32) / length.astype(jnp.float32))
    coordinate = jnp.where(pair_ids < time_pairs, moment[..., None], jnp.where(pair_ids < time_pairs + grid_pairs, patch_row[None, :, None], column[None, :, None]))
    angles = coordinate * frequency
    return (jnp.cos(angles), jnp.sin(angles))

def rotate(operand, cosines, sine_part):
    half_size = operand.shape[-1] // 2
    first_half = operand[..., :half_size]
    second_half = operand[..., half_size:]
    cosines = cosines[..., None, :]
    sine_part = sine_part[..., None, :]
    return jnp.concatenate([first_half * cosines - second_half * sine_part, second_half * cosines + first_half * sine_part], axis=-1)

def normalize(operand):
    centered = operand - lax.optimization_barrier(jnp.mean(operand, axis=-1, keepdims=True))
    variance = lax.optimization_barrier(jnp.mean(centered * centered, axis=-1, keepdims=True))
    return centered * lax.rsqrt(variance + norm_epsilon)

def modulate(operand, shift_by, scale_by):
    return normalize(operand) * (1.0 + scale_by) + shift_by

def attention(queries, key_rows, values):
    block_rows = min(512, LENGTH)

    def one_block(query_block):
        scores = low_back(jnp.einsum('qhe,khe->hqk', query_block, key_rows, precision=highest) * HEAD ** (-0.5))
        softened = jax.nn.softmax(scores, axis=-1)
        return jnp.einsum('hqk,khe->qhe', low(softened), values, precision=highest)
    stacked = queries.reshape(LENGTH // block_rows, block_rows, HEADS, HEAD)
    return lax.map(jax.checkpoint(one_block), stacked).reshape(LENGTH, HEADS, HEAD)

def layer(frames, weights, levels, frame_time):
    joint_full, output, upward, downward, modulation, modulation_bias = weights
    condition = jax.nn.silu(sinusoid(levels))
    modulated = jnp.dot(low(condition), low(modulation), precision=highest) + low(modulation_bias)
    pieces = modulated.reshape(FRAMES, 6, 1, D)
    tokens = frames.reshape(FRAMES, PATCHES, D)
    normed_one = modulate(tokens, pieces[:, 0], pieces[:, 1])
    joint_out = low_back(jnp.dot(low(normed_one).reshape(LENGTH, D), low(joint_full), precision=highest))
    split_out = joint_out.reshape(LENGTH, 3, HEADS, HEAD)
    cosines, sine_part = rotary_angles(frame_time[None], 0, LENGTH)
    queries = low(rotate(split_out[:, 0], cosines[0], sine_part[0]))
    key_rows = low(rotate(split_out[:, 1], cosines[0], sine_part[0]))
    values = low(split_out[:, 2])
    attended = low(low_back(attention(queries, key_rows, values)))
    projected = low_back(jnp.dot(attended.reshape(LENGTH, D), low(output), precision=highest))
    middle = tokens + pieces[:, 2] * projected.reshape(FRAMES, PATCHES, D)
    normed_two = modulate(middle, pieces[:, 3], pieces[:, 4])
    upper_out = low_back(jnp.dot(low(normed_two).reshape(LENGTH, D), low(upward), precision=highest))
    hidden = low(jax.nn.gelu(upper_out, approximate=True))
    branch = low_back(jnp.dot(hidden, low(downward), precision=highest))
    result = middle + pieces[:, 5] * branch.reshape(FRAMES, PATCHES, D)
    return result.reshape(LENGTH, D)

def adam_update(gradient, master, moment_one, moment_two, step_rate):
    moment_one = first_decay * moment_one + (1.0 - first_decay) * gradient
    moment_two = second_decay * moment_two + (1.0 - second_decay) * gradient * gradient
    corrected_one = moment_one / (1.0 - first_decay ** STEP)
    corrected_two = moment_two / (1.0 - second_decay ** STEP)
    master = master - step_rate * (corrected_one / (jnp.sqrt(corrected_two) + adam_epsilon) + weight_decay * master)
    return (moment_one, moment_two, master)

def reference(frames_in, noise_level, frame_time, cotangent, joint_weight, output_weight, up_weight, down_weight, modulation, modulation_bias, first_joint, first_output, first_up, first_down, first_modulation, first_bias, second_joint, second_output, second_up, second_down, second_modulation, second_bias):
    masters = (joint_weight, output_weight, up_weight, down_weight, modulation, modulation_bias)

    def forward(frames, weights):

        def one_clip(carried, clip_items):
            return (carried, layer(clip_items[0], weights, clip_items[1], clip_items[2]))
        carried, outputs = lax.scan(jax.checkpoint(one_clip), jnp.zeros((), jnp.float32), (frames, noise_level, frame_time))
        return outputs
    mixed, pull_back = jax.vjp(forward, frames_in.astype(jnp.float32), masters)
    input_grad, weight_grads = pull_back(cotangent.astype(jnp.float32))
    squares = sum((jnp.sum(gradient * gradient) for gradient in weight_grads))
    grad_norm = jnp.sqrt(squares)
    factor = jnp.minimum(1.0, clip_limit / (grad_norm + 1e-06))
    step_rates = (D ** (-0.5), max(1, 2 * D // LENGTH) ** (-0.5), D ** (-0.5), FF ** (-0.5), D ** (-0.5), 0.5)
    firsts = (first_joint, first_output, first_up, first_down, first_modulation, first_bias)
    seconds = (second_joint, second_output, second_up, second_down, second_modulation, second_bias)
    clipped = [gradient * factor for gradient in weight_grads]
    updates = [adam_update(clipped[slot], masters[slot], firsts[slot], seconds[slot], step_rates[slot]) for slot in range(6)]
    return (mixed.astype(jnp.bfloat16), input_grad, clipped[0], clipped[1], clipped[2], clipped[3], clipped[4], clipped[5], grad_norm, updates[0][0], updates[1][0], updates[2][0], updates[3][0], updates[4][0], updates[5][0], updates[0][1], updates[1][1], updates[2][1], updates[3][1], updates[4][1], updates[5][1], updates[0][2], updates[1][2], updates[2][2], updates[3][2], updates[4][2], updates[5][2], updates[0][2].astype(jnp.bfloat16), updates[1][2].astype(jnp.bfloat16), updates[2][2].astype(jnp.bfloat16), updates[3][2].astype(jnp.bfloat16), updates[4][2].astype(jnp.bfloat16), updates[5][2].astype(jnp.bfloat16))
```

```python
from functools import partial
import math

import jax
import jax.numpy as jnp
from jax import lax
from jax.experimental import pallas as pl
from jax.experimental.pallas import tpu as pltpu
from jax.sharding import PartitionSpec as P

D = 1024
HEADS = 16
HEAD = 64
FF = 4096
FRAMES = 16
GRID_W = 16
STEP = 10
PATCHES = 256
LENGTH = 4096

norm_epsilon = 1e-06
adam_epsilon = 1e-08
first_decay = 0.5
second_decay = 0.5
weight_decay = 0.1
clip_limit = 1.0
highest = lax.Precision.HIGHEST
AXES = ("clip", "seq")
LOW = jnp.bfloat16
WIDE = jnp.float32
SOFT = math.log2(math.e) * HEAD ** (-0.5)


def dot(left, right):
    return jnp.dot(left, right, preferred_element_type=WIDE)


def contract(left, right, left_dim, right_dim):
    return lax.dot_general(
        left, right, (((left_dim,), (right_dim,)), ((), ())), preferred_element_type=WIDE
    )


def normalize(operand):
    centered = operand - jnp.mean(operand, axis=-1, keepdims=True)
    variance = jnp.mean(centered * centered, axis=-1, keepdims=True)
    return centered * lax.rsqrt(variance + norm_epsilon)


def modulate(operand, shift_by, scale_by):
    return normalize(operand) * (1.0 + scale_by) + shift_by


def adam_update(gradient, master, moment_one, moment_two, step_rate):
    moment_one = first_decay * moment_one + (1.0 - first_decay) * gradient
    moment_two = second_decay * moment_two + (1.0 - second_decay) * gradient * gradient
    corrected_one = moment_one / (1.0 - first_decay**STEP)
    corrected_two = moment_two / (1.0 - second_decay**STEP)
    master = master - step_rate * (
        corrected_one / (jnp.sqrt(corrected_two) + adam_epsilon) + weight_decay * master
    )
    return (moment_one, moment_two, master)


def rotary_tables(times, places):
    frame_ids = places // PATCHES
    patch_row = (places % PATCHES // GRID_W).astype(WIDE)
    column = (places % GRID_W).astype(WIDE)
    matches = frame_ids[None, :] == jnp.arange(FRAMES, dtype=jnp.int32)[:, None]
    moment = jnp.sum(jnp.where(matches, times[:, None], 0), axis=0).astype(WIDE)
    time_pairs = HEAD // 8
    grid_pairs = 3 * HEAD // 16
    pair_ids = jnp.arange(HEAD // 2, dtype=jnp.int32)
    second = time_pairs + grid_pairs
    offset = jnp.where(pair_ids < time_pairs, 0, jnp.where(pair_ids < second, time_pairs, second))
    length = jnp.where(pair_ids < time_pairs, time_pairs, grid_pairs)
    frequency = jnp.exp(
        -math.log(10000.0) * (pair_ids - offset).astype(WIDE) / length.astype(WIDE)
    )
    ids = pair_ids[:, None]
    coordinate = jnp.where(
        ids < time_pairs, moment[None], jnp.where(ids < second, patch_row[None], column[None])
    )
    angles = coordinate * frequency[:, None]
    return jnp.cos(angles), jnp.sin(angles)


def project_kernel(pick, rows_ref, weight_ref, cos_ref, sin_ref, out_ref):
    turned = dot(rows_ref[...], weight_ref[...]).T
    group = pl.program_id(0)
    half = HEAD // 2

    @pl.when(group == 2)
    def _():
        out_ref[0] = turned.astype(LOW)

    @pl.when(group < 2)
    def _():
        cosines, sines = cos_ref[...], sin_ref[...]
        for head in range(turned.shape[0] // HEAD):
            start = head * HEAD
            one = turned[start : start + half]
            two = turned[start + half : start + HEAD]
            out_ref[0, start : start + half, :] = (one * cosines - two * sines).astype(LOW)
            out_ref[0, start + half : start + HEAD, :] = (two * cosines + one * sines).astype(LOW)


def project(pick, rows, weight, cosines, sines, members):
    tokens, width = rows.shape
    columns = D // members
    return pl.pallas_call(
        project_kernel,
        grid_spec=pltpu.PrefetchScalarGridSpec(
            num_scalar_prefetch=1,
            grid=(3,),
            in_specs=[
                pl.BlockSpec((tokens, width), lambda g, pick: (0, 0)),
                pl.BlockSpec((width, columns), lambda g, pick: (0, g * members + pick[0])),
                pl.BlockSpec((HEAD // 2, tokens), lambda g, pick: (0, 0)),
                pl.BlockSpec((HEAD // 2, tokens), lambda g, pick: (0, 0)),
            ],
            out_specs=pl.BlockSpec((1, columns, tokens), lambda g, pick: (g, 0, 0)),
        ),
        out_shape=jax.ShapeDtypeStruct((3, columns, tokens), LOW),
        compiler_params=pltpu.CompilerParams(vmem_limit_bytes=40 << 20),
        cost_estimate=pl.CostEstimate(
            flops=6 * tokens * width * columns,
            bytes_accessed=2 * (tokens * width + 3 * width * columns + 3 * tokens * columns),
            transcendentals=0,
        ),
        name="project",
    )(pick, rows, weight, cosines, sines)


def pick_rows(refs, step, per, size, target, index):
    start = 0 if per == 1 else pl.multiple_of(step % per * size, size)
    for member, ref in enumerate(refs):

        @pl.when(step // per == member)
        def _(ref=ref):
            target[...] = ref[index, :, pl.ds(start, size)]


def attend_kernel(*refs, members, tokens, size, block):
    parts = refs[:members]
    low_refs = refs[members : 2 * members]
    wide_ref, total_ref, key_rows, query_rows = refs[2 * members :]
    step = pl.program_id(1)
    per = tokens // size
    length = members * tokens

    @pl.when(step == 0)
    def _():
        for member in range(members):
            key_rows[member * tokens : (member + 1) * tokens, :] = parts[member][1].T

    pick_rows(parts, step, per, size, query_rows, 0)
    queries = query_rows[...]
    count = length // block
    inside = tokens // block
    gathered = jnp.zeros((HEAD, size), WIDE)
    highest_score = jnp.full((1, size), -1e30, WIDE)
    total = jnp.zeros((1, size), WIDE)
    following = dot(key_rows[0:block, :], queries)
    for number in range(count):
        scores = following
        if number + 1 < count:
            following = dot(key_rows[(number + 1) * block : (number + 2) * block, :], queries)
        raised = jnp.maximum(highest_score, jnp.max(scores, axis=0, keepdims=True))
        shrink = jnp.exp2((highest_score - raised) * SOFT)
        probs = jnp.exp2(scores * SOFT - raised * SOFT)
        total = total * shrink + jnp.sum(probs, axis=0, keepdims=True)
        start = number % inside * block
        values = parts[number // inside][2, :, start : start + block]
        gathered = gathered * shrink + dot(values, probs.astype(LOW))
        highest_score = raised
    attended = gathered / total
    wide_ref[...] = attended
    total_ref[0] = highest_score * SOFT + jnp.log2(total)
    low = attended.astype(LOW)
    start = 0 if per == 1 else pl.multiple_of(step % per * size, size)
    for member in range(members):

        @pl.when(step // per == member)
        def _(member=member):
            low_refs[member][:, pl.ds(start, size)] = low


def attend(parts):
    members = len(parts)
    _, rows, tokens = parts[0].shape
    heads = rows // HEAD
    size, block = min(1024, tokens), min(512, tokens)
    length = members * tokens
    part = pl.BlockSpec((3, HEAD, tokens), lambda h, i: (0, h, 0))
    return pl.pallas_call(
        partial(attend_kernel, members=members, tokens=tokens, size=size, block=block),
        grid=(heads, length // size),
        in_specs=[part] * members,
        out_specs=[pl.BlockSpec((HEAD, tokens), lambda h, i: (h, 0))] * members
        + [
            pl.BlockSpec((HEAD, size), lambda h, i: (h, i)),
            pl.BlockSpec((1, 1, size), lambda h, i: (h, 0, i)),
        ],
        out_shape=[jax.ShapeDtypeStruct((rows, tokens), LOW)] * members
        + [
            jax.ShapeDtypeStruct((rows, length), WIDE),
            jax.ShapeDtypeStruct((heads, 1, length), WIDE),
        ],
        scratch_shapes=[pltpu.VMEM((length, HEAD), LOW), pltpu.VMEM((HEAD, size), LOW)],
        compiler_params=pltpu.CompilerParams(vmem_limit_bytes=48 << 20),
        cost_estimate=pl.CostEstimate(
            flops=16 * heads * length * length * HEAD,
            bytes_accessed=8 * rows * length,
            transcendentals=heads * length * length,
        ),
        name="attend",
    )(*parts)


def turn_back(operand, cosines, sines):
    half = HEAD // 2
    one, two = operand[:half], operand[half:]
    return jnp.concatenate([one * cosines + two * sines, two * cosines - one * sines], axis=0)


def attend_back_kernel(*refs, members, tokens, size, block):
    parts = refs[:members]
    grads = refs[members : 2 * members]
    wide_ref, total_ref, cos_ref, sin_ref = refs[2 * members : 2 * members + 4]
    outs = refs[2 * members + 4 : 3 * members + 4]
    key_rows, query_columns, grad_columns, key_sum, value_sum = refs[3 * members + 4 :]
    step = pl.program_id(1)
    per = tokens // size
    length = members * tokens
    count = length // block
    inside = tokens // block
    back = HEAD ** (-0.5)

    @pl.when(step == 0)
    def _():
        for member in range(members):
            key_rows[member * tokens : (member + 1) * tokens, :] = parts[member][1].T
        key_sum[...] = jnp.zeros_like(key_sum)
        value_sum[...] = jnp.zeros_like(value_sum)

    pick_rows(parts, step, per, size, query_columns, 0)
    start = 0 if per == 1 else pl.multiple_of(step % per * size, size)
    for member in range(members):

        @pl.when(step // per == member)
        def _(member=member):
            grad_columns[...] = grads[member][:, pl.ds(start, size)]

    queries_across = query_columns[...]
    grads_across = grad_columns[...]
    queries = queries_across.T
    out_grads = grads_across.T
    delta = jnp.sum(grads_across.astype(WIDE) * wide_ref[...], axis=0, keepdims=True).T
    total = total_ref[0].T
    query_grad = jnp.zeros((size, HEAD), WIDE)

    def pair(number):
        member, at = number // inside, number % inside * block
        return (
            dot(queries, parts[member][1, :, at : at + block]),
            dot(out_grads, parts[member][2, :, at : at + block]),
        )

    following = pair(0)
    for number in range(count):
        scores, prob_grad = following
        if number + 1 < count:
            following = pair(number + 1)
        here = slice(number * block, (number + 1) * block)
        probs = jnp.exp2(scores * SOFT - total)
        score_grad = (probs * (prob_grad - delta)).astype(LOW)
        value_sum[:, here] += dot(grads_across, probs.astype(LOW))
        key_sum[:, here] += dot(queries_across, score_grad)
        query_grad += dot(score_grad, key_rows[here, :])

    where = pl.multiple_of(step * size, size)
    turned = turn_back(
        query_grad.T * back, cos_ref[:, pl.ds(where, size)], sin_ref[:, pl.ds(where, size)]
    ).astype(LOW)
    for member in range(members):

        @pl.when(step // per == member)
        def _(member=member):
            outs[member][0, :, pl.ds(start, size)] = turned

    @pl.when(step == length // size - 1)
    def _():
        for member in range(members):
            span = slice(member * tokens, (member + 1) * tokens)
            outs[member][1] = turn_back(
                key_sum[:, span] * back, cos_ref[:, span], sin_ref[:, span]
            ).astype(LOW)
            outs[member][2] = value_sum[:, span].astype(LOW)


def attend_back(parts, grads, wide, total, cosines, sines):
    members = len(parts)
    _, rows, tokens = parts[0].shape
    heads = rows // HEAD
    size, block = min(1024, tokens), min(512, tokens)
    length = members * tokens
    part = pl.BlockSpec((3, HEAD, tokens), lambda h, i: (0, h, 0))
    table = pl.BlockSpec((HEAD // 2, length), lambda h, i: (0, 0))
    return pl.pallas_call(
        partial(attend_back_kernel, members=members, tokens=tokens, size=size, block=block),
        grid=(heads, length // size),
        in_specs=[part] * members
        + [pl.BlockSpec((HEAD, tokens), lambda h, i: (h, 0))] * members
        + [
            pl.BlockSpec((HEAD, size), lambda h, i: (h, i)),
            pl.BlockSpec((1, 1, size), lambda h, i: (h, 0, i)),
            table,
            table,
        ],
        out_specs=[part] * members,
        out_shape=[jax.ShapeDtypeStruct((3, rows, tokens), LOW)] * members,
        scratch_shapes=[
            pltpu.VMEM((length, HEAD), LOW),
            pltpu.VMEM((HEAD, size), LOW),
            pltpu.VMEM((HEAD, size), LOW),
            pltpu.VMEM((HEAD, length), WIDE),
            pltpu.VMEM((HEAD, length), WIDE),
        ],
        compiler_params=pltpu.CompilerParams(vmem_limit_bytes=56 << 20),
        cost_estimate=pl.CostEstimate(
            flops=40 * heads * length * length * HEAD,
            bytes_accessed=16 * rows * length,
            transcendentals=heads * length * length,
        ),
        name="attend_back",
    )(*parts, *grads, wide, total, cosines, sines)


def per_device(
    clip_size,
    seq_size,
    frames_in,
    noise_level,
    frame_time,
    cotangent,
    joint_weight,
    output_weight,
    up_weight,
    down_weight,
    modulation,
    modulation_bias,
    first_joint,
    first_output,
    first_up,
    first_down,
    first_modulation,
    first_bias,
    second_joint,
    second_output,
    second_up,
    second_down,
    second_modulation,
    second_bias,
):
    total_devices = clip_size * seq_size
    masters = (joint_weight, output_weight, up_weight, down_weight, modulation, modulation_bias)
    firsts = (first_joint, first_output, first_up, first_down, first_modulation, first_bias)
    seconds = (second_joint, second_output, second_up, second_down, second_modulation, second_bias)
    clip_id, seq_id = lax.axis_index("clip"), lax.axis_index("seq")
    rank = clip_id * seq_size + seq_id
    half = seq_size // 2
    side = seq_id // half
    place = seq_id % half
    members = half

    def swap_with(value, mask):
        return lax.ppermute(value, AXES, [(i, i ^ mask) for i in range(total_devices)])

    def pick(value, index):
        return lax.dynamic_index_in_dim(value, index, 0, keepdims=False)

    core_mask = seq_size
    clip_masks = [seq_size << bit for bit in range(clip_size.bit_length() - 1)]
    seq_masks = [1 << bit for bit in range(seq_size.bit_length() - 1)]
    order = clip_masks + seq_masks

    joint_full, output_full, upward, downward = (
        lax.all_gather(weight.astype(LOW), AXES, axis=0, tiled=True) for weight in masters[:4]
    )

    local_rows = frames_in.shape[1]
    frame_count = max(1, local_rows // PATCHES)
    per_frame = local_rows // frame_count
    tokens_here = 2 * local_rows

    def to_one_clip(value):
        return jnp.stack([pick(value, side), swap_with(pick(value, 1 - side), half)])

    def to_two_clips(own, others):
        arrived = swap_with(others, half)
        return jnp.where(side == 0, jnp.stack([own, arrived]), jnp.stack([arrived, own]))

    tokens_low = to_one_clip(frames_in)
    upstream_low = to_one_clip(cotangent)
    shape = (2, frame_count, per_frame, D)
    tokens = tokens_low.astype(WIDE).reshape(shape)

    levels = noise_level.astype(WIDE)
    levels_of = [levels]
    for mask in clip_masks:
        levels_of = levels_of + [swap_with(jnp.stack(levels_of), mask)[i] for i in range(len(levels_of))]
    all_levels = jnp.concatenate(levels_of, axis=0).reshape(-1)
    masks = [0]
    for mask in reversed(order):
        masks = masks + [other ^ mask for other in masks]
    masks = jnp.array(masks, jnp.int32)
    seq_of = seq_id ^ (masks % seq_size)
    chunk = jnp.stack([seq_of, seq_of ^ half], axis=1)
    frame_of = (
        chunk[:, :, None] * local_rows // PATCHES + jnp.arange(frame_count, dtype=jnp.int32)
    )
    clip_of = masks // seq_size * 2 + seq_of // half
    level_ids = (clip_of[:, None, None] * FRAMES + frame_of).reshape(-1)
    level_of = jnp.sum(
        jnp.where(
            level_ids[:, None] == jnp.arange(all_levels.shape[0], dtype=jnp.int32), all_levels, 0.0
        ),
        axis=1,
    )
    own_width = modulation.shape[0]
    columns = rank * own_width + jnp.arange(own_width, dtype=jnp.int32)
    half_width = D // 2
    frequency = jnp.exp(-math.log(10000.0) * (columns % half_width).astype(WIDE) / half_width)
    angles = level_of[:, None] * frequency
    wave = jnp.where(columns < half_width, jnp.cos(angles), jnp.sin(angles))
    condition = jax.nn.silu(wave).astype(LOW)

    bias_width = modulation_bias.shape[0]
    bias_row = lax.dynamic_update_slice_in_dim(
        jnp.zeros((6 * D,), WIDE), modulation_bias.astype(LOW).astype(WIDE), rank * bias_width, 0
    )
    modulation_low = modulation.astype(LOW)

    def modulated_part(first, last):
        terms = dot(condition, modulation_low[:, first:last]) + bias_row[first:last]
        for mask in order:
            middle = terms.shape[0] // 2
            terms = terms[:middle] + swap_with(terms[middle:], mask)
        return terms.reshape(2, frame_count, 1, last - first)

    early = modulated_part(0, 2 * D)
    shift_one, scale_one = early[..., :D], early[..., D:]
    late = modulated_part(2 * D, 6 * D)
    gate_one, shift_two, scale_two, gate_two = (
        late[..., i * D : (i + 1) * D] for i in range(4)
    )

    member_seq = seq_id ^ jnp.arange(members, dtype=jnp.int32)
    starts = jnp.stack([member_seq, member_seq ^ half], axis=1) * local_rows
    places = (starts[:, :, None] + jnp.arange(local_rows, dtype=jnp.int32)).reshape(-1)
    cosines, sines = rotary_tables(pick(frame_time, side), places)

    normed_one_low = modulate(tokens, shift_one, scale_one).astype(LOW).reshape(tokens_here, D)
    own_tables = cosines[:, :tokens_here], sines[:, :tokens_here]

    def group_of(member):
        return (place ^ member).astype(jnp.int32).reshape(1)

    def project_group(member):
        if D // members % 128 == 0:
            return project(group_of(member), normed_one_low, joint_full, *own_tables, members)
        wide = [
            project(jnp.full((1,), i, jnp.int32), normed_one_low, joint_full, *own_tables, 4)
            for i in range(4)
        ]
        every = jnp.concatenate(wide, axis=1).reshape(3, members, D // members, tokens_here)
        return lax.dynamic_index_in_dim(every, place ^ member, 1, keepdims=False)

    parts = [None] * members
    for member in list(range(1, members)) + [0]:
        part = project_group(member)
        parts[member] = swap_with(part, member) if member else part
    *attended_parts, attended_wide, totals = attend(parts)

    def by_head(values):
        lead = values[0].shape[:-2]
        result = jnp.zeros(lead + (members,) + values[0].shape[-2:], values[0].dtype)
        for member, value in enumerate(values):
            result = lax.dynamic_update_slice_in_dim(
                result, jnp.expand_dims(value, -3), place ^ member, len(lead)
            )
        return result.reshape(-1, values[0].shape[-1])

    attended_across = by_head(
        [swap_with(value, member) if member else value for member, value in enumerate(attended_parts)]
    )
    projected = contract(attended_across, output_full, 0, 0).reshape(shape)
    middle = tokens + gate_one * projected
    normed_two_low = modulate(middle, shift_two, scale_two).astype(LOW).reshape(tokens_here, D)
    upper_out = dot(normed_two_low, upward)
    hidden_low = jax.nn.gelu(upper_out, approximate=True).astype(LOW)
    branch = dot(hidden_low, downward).reshape(shape)
    result = (middle + gate_two * branch).astype(LOW).reshape(2, local_rows, D)
    mixed = to_two_clips(result[0], result[1])

    def scatter_rows(gradient, masks):
        rows, width = gradient.shape
        bits = total_devices.bit_length() - 1
        value = gradient.reshape((2,) * bits + (rows // total_devices, width))
        left = list(range(bits - 1, -1, -1))
        for mask in masks:
            bit = mask.bit_length() - 1
            axis = left.index(bit)
            left.pop(axis)
            mine = rank // mask % 2
            sent = lax.dynamic_index_in_dim(value, 1 - mine, axis, keepdims=False).astype(LOW)
            kept = lax.dynamic_index_in_dim(value, mine, axis, keepdims=False)
            value = kept + swap_with(sent, mask).astype(WIDE)
        return value

    first_order = clip_masks + seq_masks
    second_order = [core_mask] + seq_masks[:1] + clip_masks[1:] + seq_masks[1:]

    def scatter(gradient):
        width = gradient.shape[1] // 2
        return jnp.concatenate(
            [
                scatter_rows(gradient[:, :width], first_order),
                scatter_rows(gradient[:, width:], second_order),
            ],
            axis=1,
        )

    upstream = upstream_low.astype(WIDE).reshape(shape)
    gate_two_grad = jnp.sum(upstream * branch, axis=2)
    branch_grad = (gate_two * upstream).astype(LOW).reshape(tokens_here, D)
    down_sum = scatter(contract(hidden_low, branch_grad, 0, 0))
    hidden_grad = contract(branch_grad, downward, 1, 1)
    gelu_pull = jax.vjp(partial(jax.nn.gelu, approximate=True), upper_out)[1]
    upper_grad = gelu_pull(hidden_grad)[0].astype(LOW)
    up_sum = scatter(contract(normed_two_low, upper_grad, 0, 0))
    normed_two_grad = contract(upper_grad, upward, 1, 1).reshape(shape)
    middle_pull = jax.vjp(modulate, middle, shift_two, scale_two)[1]
    middle_grad, shift_two_grad, scale_two_grad = middle_pull(normed_two_grad)
    middle_grad = middle_grad + upstream
    gate_one_grad = jnp.sum(middle_grad * projected, axis=2)
    projected_grad = (gate_one * middle_grad).astype(LOW).reshape(tokens_here, D)
    outer_across = contract(output_full, projected_grad, 1, 1).astype(LOW)
    outer_across = outer_across.reshape(members, D // members, tokens_here)
    outer_parts = []
    for member in range(members):
        outer = pick(outer_across, place ^ member)
        outer_parts.append(swap_with(outer, member) if member else outer)
    output_sum = scatter(dot(attended_across, projected_grad))

    def gather_frames(value):
        for mask in reversed(order):
            value = jnp.concatenate([value, swap_with(value, mask)], axis=0)
        return value

    def piece_rows(*pieces):
        return jnp.concatenate(
            [piece.reshape(2 * frame_count, D) for piece in pieces], axis=1
        )

    late_pieces = gather_frames(
        piece_rows(gate_one_grad, shift_two_grad, scale_two_grad, gate_two_grad)
    )
    joint_parts = attend_back(parts, outer_parts, attended_wide, totals, cosines, sines)
    joint_across = by_head(
        [swap_with(value, member) if member else value for member, value in enumerate(joint_parts)]
    )
    joint_sum = scatter(contract(normed_one_low, joint_across, 0, 1))
    normed_one_grad = contract(joint_across, joint_full, 0, 1).reshape(shape)
    tokens_pull = jax.vjp(modulate, tokens, shift_one, scale_one)[1]
    token_grad, shift_one_grad, scale_one_grad = tokens_pull(normed_one_grad)
    input_rows = (token_grad + middle_grad).reshape(2, local_rows, D)
    input_grad = to_two_clips(input_rows[0], input_rows[1].astype(LOW)).astype(WIDE)
    early_pieces = gather_frames(piece_rows(shift_one_grad, scale_one_grad))

    pieces = jnp.concatenate([early_pieces, late_pieces], axis=1)
    mod_sum = lax.dot_general(
        condition.astype(WIDE), pieces, (((0,), (0,)), ((), ())), precision=highest
    )
    bias_sum = lax.dynamic_slice_in_dim(
        jnp.sum(pieces, axis=0), rank * bias_width, bias_width, 0
    )

    summed = (joint_sum, output_sum, up_sum, down_sum, mod_sum, bias_sum)
    squares = sum(jnp.sum(shard * shard) for shard in summed).reshape(1, 1)
    for group in (
        [i * seq_size for i in range(1, clip_size)],
        list(range(1, seq_size)),
    ):
        squares = squares + sum(swap_with(squares, mask) for mask in group)
    grad_norm = jnp.sqrt(squares[0, 0])
    factor = jnp.minimum(1.0, clip_limit / (grad_norm + 1e-06))
    step_rates = (
        D ** (-0.5),
        max(1, 2 * D // LENGTH) ** (-0.5),
        D ** (-0.5),
        FF ** (-0.5),
        D ** (-0.5),
        0.5,
    )
    clipped = [shard * factor for shard in summed]
    updates = [
        adam_update(clipped[slot], masters[slot], firsts[slot], seconds[slot], step_rates[slot])
        for slot in range(6)
    ]
    return (
        mixed,
        input_grad,
        *clipped,
        grad_norm,
        *(update[0] for update in updates),
        *(update[1] for update in updates),
        *(update[2] for update in updates),
        *(update[2].astype(LOW) for update in updates),
    )


def solution(mesh):
    tokens = P("clip", "seq", None)
    rows = P(AXES, None)
    weights = (rows, rows, rows, rows, rows, P(AXES))
    in_specs = (tokens, P("clip", None), P("clip", None), tokens) + weights * 3
    out_specs = (tokens, tokens) + weights + (P(),) + weights * 4
    return jax.shard_map(
        partial(per_device, mesh.shape["clip"], mesh.shape["seq"]),
        mesh=mesh,
        in_specs=in_specs,
        out_specs=out_specs,
        check_vma=False,
    )
```

```python
from functools import partial
import math

import jax
import jax.numpy as jnp
from jax import lax
from jax.experimental import pallas as pl
from jax.experimental.pallas import tpu as pltpu
from jax.sharding import PartitionSpec as P

D = 1024
HEADS = 16
HEAD = 64
FF = 4096
FRAMES = 16
GRID_W = 16
STEP = 10
PATCHES = 256
LENGTH = 4096

norm_epsilon = 1e-06
adam_epsilon = 1e-08
first_decay = 0.5
second_decay = 0.5
weight_decay = 0.1
clip_limit = 1.0
highest = lax.Precision.HIGHEST
AXES = ("clip", "seq")
LOW = jnp.bfloat16
WIDE = jnp.float32
SOFT = math.log2(math.e) * HEAD ** (-0.5)


def dot(left, right):
    return jnp.dot(left, right, preferred_element_type=WIDE)


def contract(left, right, left_dim, right_dim):
    return lax.dot_general(
        left, right, (((left_dim,), (right_dim,)), ((), ())), preferred_element_type=WIDE
    )


def normalize(operand):
    centered = operand - jnp.mean(operand, axis=-1, keepdims=True)
    variance = jnp.mean(centered * centered, axis=-1, keepdims=True)
    return centered * lax.rsqrt(variance + norm_epsilon)


def modulate(operand, shift_by, scale_by):
    return normalize(operand) * (1.0 + scale_by) + shift_by


def adam_update(gradient, master, moment_one, moment_two, step_rate):
    moment_one = first_decay * moment_one + (1.0 - first_decay) * gradient
    moment_two = second_decay * moment_two + (1.0 - second_decay) * gradient * gradient
    corrected_one = moment_one / (1.0 - first_decay**STEP)
    corrected_two = moment_two / (1.0 - second_decay**STEP)
    master = master - step_rate * (
        corrected_one / (jnp.sqrt(corrected_two) + adam_epsilon) + weight_decay * master
    )
    return (moment_one, moment_two, master)


def rotary_tables(times, places):
    frame_ids = places // PATCHES
    patch_row = (places % PATCHES // GRID_W).astype(WIDE)
    column = (places % GRID_W).astype(WIDE)
    matches = frame_ids[None, :] == jnp.arange(FRAMES, dtype=jnp.int32)[:, None]
    moment = jnp.sum(jnp.where(matches, times[:, None], 0), axis=0).astype(WIDE)
    time_pairs = HEAD // 8
    grid_pairs = 3 * HEAD // 16
    pair_ids = jnp.arange(HEAD // 2, dtype=jnp.int32)
    second = time_pairs + grid_pairs
    offset = jnp.where(pair_ids < time_pairs, 0, jnp.where(pair_ids < second, time_pairs, second))
    length = jnp.where(pair_ids < time_pairs, time_pairs, grid_pairs)
    frequency = jnp.exp(
        -math.log(10000.0) * (pair_ids - offset).astype(WIDE) / length.astype(WIDE)
    )
    ids = pair_ids[:, None]
    coordinate = jnp.where(
        ids < time_pairs, moment[None], jnp.where(ids < second, patch_row[None], column[None])
    )
    angles = coordinate * frequency[:, None]
    return jnp.cos(angles), jnp.sin(angles)


anywhere = pl.BlockSpec(memory_space=pl.ANY)


def whole(shape):
    return pl.BlockSpec(shape, lambda *ids: (0,) * len(shape))


def call(
    kernel,
    name,
    ids,
    grid,
    ins,
    in_specs,
    outs,
    out_specs,
    scratch=(),
    after=(),
    room=56,
    aliases=None,
    time=2,
):
    count, extra = 1 + len(ins), len(after)

    def body(*refs):
        kernel(*refs[:count], *refs[count + extra :])

    body.__name__ = name
    return pl.pallas_call(
        body,
        grid_spec=pltpu.PrefetchScalarGridSpec(
            num_scalar_prefetch=1,
            grid=grid,
            in_specs=list(in_specs) + [anywhere] * extra,
            out_specs=out_specs,
            scratch_shapes=list(scratch),
        ),
        out_shape=outs,
        input_output_aliases=aliases or {},
        compiler_params=pltpu.CompilerParams(vmem_limit_bytes=room << 20),
        cost_estimate=pl.CostEstimate(
            flops=int(time * 1.15e9), bytes_accessed=int(time * 3e6), transcendentals=0
        ),
        name=name,
    )(ids, *ins, *after)


def low_array(*shape):
    return jax.ShapeDtypeStruct(shape, LOW)


def wide_array(*shape):
    return jax.ShapeDtypeStruct(shape, WIDE)


def bit_of(rank, mask):
    return rank // mask % 2


def chunk_spec(rows, frames):
    return pl.BlockSpec((1, rows // frames, D), lambda r, f, ids: (r, f, 0))


def pair_specs(rows, frames):
    size = rows // frames
    return [
        pl.BlockSpec((1, size, D), lambda r, f, ids: (ids[1], f, 0)),
        pl.BlockSpec((size, D), lambda r, f, ids: (f, 0)),
    ]


def row_spec(rows, frames):
    return pl.BlockSpec((rows // frames, D), lambda r, f, ids: (r * frames + f, 0))


def read_pair(ids_ref, own_ref, other_ref):
    own = pl.program_id(0) == ids_ref[1]
    return jnp.where(own, own_ref[0].astype(WIDE), other_ref[...].astype(WIDE))


def piece(ref, number, frames):
    row = pl.program_id(0) * frames + pl.program_id(1)
    return ref[pl.ds(row, 1), number * D : (number + 1) * D]


def put_piece(ref, number, frames, value):
    row = pl.program_id(0) * frames + pl.program_id(1)
    ref[pl.ds(row, 1), number * D : (number + 1) * D] = value


def norm_parts(operand):
    centered = operand - jnp.mean(operand, axis=-1, keepdims=True)
    variance = jnp.mean(centered * centered, axis=-1, keepdims=True)
    inverse = lax.rsqrt(variance + norm_epsilon)
    return centered * inverse, inverse


def norm_back(gradient, normed, inverse, scale):
    shift_grad = jnp.sum(gradient, axis=0, keepdims=True)
    scale_grad = jnp.sum(gradient * normed, axis=0, keepdims=True)
    inner = gradient * (1.0 + scale)
    mean = jnp.mean(inner, axis=-1, keepdims=True)
    along = jnp.mean(inner * normed, axis=-1, keepdims=True)
    return (inner - mean - normed * along) * inverse, shift_grad, scale_grad


def norm_one(ids, tokens, early, frames, after=()):
    rows = tokens.shape[1]

    def kernel(ids_ref, tokens_ref, early_ref, out_ref):
        normed, _ = norm_parts(tokens_ref[0].astype(WIDE))
        shift, scale = piece(early_ref, 0, frames), piece(early_ref, 1, frames)
        out_ref[...] = (normed * (1.0 + scale) + shift).astype(LOW)

    return call(
        kernel,
        "norm_one",
        ids,
        (2, frames),
        [tokens, early],
        [chunk_spec(rows, frames), whole(early.shape)],
        low_array(2 * rows, D),
        row_spec(rows, frames),
        after=after,
        time=5,
    )


def project(ids, rows, weight, cosines, sines, members, first, after=()):
    tokens, width = rows.shape
    columns = members * HEAD
    half = HEAD // 2

    def kernel(ids_ref, rows_ref, weight_ref, cos_ref, sin_ref, out_ref):
        across = dot(rows_ref[...], weight_ref[...]).T
        kind = pl.program_id(0)

        @pl.when(kind == 2)
        def _():
            for member in range(members):
                out_ref[member, 0] = across[member * HEAD : (member + 1) * HEAD].astype(LOW)

        @pl.when(kind < 2)
        def _():
            cosines, sines = cos_ref[...], sin_ref[...]
            for member in range(members):
                one = across[member * HEAD : member * HEAD + half]
                two = across[member * HEAD + half : (member + 1) * HEAD]
                out_ref[member, 0, :half] = (one * cosines - two * sines).astype(LOW)
                out_ref[member, 0, half:] = (two * cosines + one * sines).astype(LOW)

    table = pl.BlockSpec((half, tokens), lambda t, ids: (0, ids[0]))
    return call(
        kernel,
        "project",
        ids,
        (3,),
        [rows, weight, cosines, sines],
        [
            whole((tokens, width)),
            pl.BlockSpec((width, columns), lambda t, ids: (0, first * 3 + t)),
            table,
            table,
        ],
        low_array(members, 3, HEAD, tokens),
        pl.BlockSpec((members, 1, HEAD, tokens), lambda t, ids: (0, t, 0, 0)),
        after=after,
        time=6,
    )


def attend(ids, parts, into, head, heads, after=()):
    members, _, _, tokens = parts.shape
    size, block = min(1024, tokens), min(512, tokens)
    length = members * tokens
    per, count, inside = tokens // size, length // block, tokens // block
    before = [] if into is None else [into]

    def kernel(ids_ref, part_ref, *refs):
        low_ref, wide_ref, total_ref, key_rows = refs[len(before) :]
        step = pl.program_id(0)

        @pl.when(step == 0)
        def _():
            for member in range(members):
                key_rows[member * tokens : (member + 1) * tokens, :] = part_ref[member, 1].T

        member = step // per
        start = 0 if per == 1 else pl.multiple_of(step % per * size, size)
        queries = part_ref[member, 0, :, pl.ds(start, size)]
        gathered = jnp.zeros((HEAD, size), WIDE)
        top = jnp.full((1, size), -1e30, WIDE)
        total = jnp.zeros((1, size), WIDE)
        following = dot(key_rows[0:block, :], queries)
        for number in range(count):
            scores = following
            if number + 1 < count:
                following = dot(key_rows[(number + 1) * block : (number + 2) * block, :], queries)
            raised = jnp.maximum(top, jnp.max(scores, axis=0, keepdims=True))
            shrink = jnp.exp2((top - raised) * SOFT)
            probs = jnp.exp2(scores * SOFT - raised * SOFT)
            total = total * shrink + jnp.sum(probs, axis=0, keepdims=True)
            at = number % inside * block
            values = part_ref[number // inside, 2, :, at : at + block]
            gathered = gathered * shrink + dot(values, probs.astype(LOW))
            top = raised
        attended = gathered / total
        wide_ref[...] = attended
        total_ref[...] = top * SOFT + jnp.log2(total)
        low_ref[member, :, pl.ds(start, size)] = attended.astype(LOW)

    return call(
        kernel,
        "attend",
        ids,
        (length // size,),
        [parts, *before],
        [whole(parts.shape)] + [anywhere] * len(before),
        [
            low_array(members, heads * HEAD, tokens),
            wide_array(HEAD, length),
            wide_array(1, length),
        ],
        [
            pl.BlockSpec((members, HEAD, tokens), lambda i, ids: (0, head, 0)),
            pl.BlockSpec((HEAD, size), lambda i, ids: (0, i)),
            pl.BlockSpec((1, size), lambda i, ids: (0, i)),
        ],
        [pltpu.VMEM((length, HEAD), LOW)],
        after,
        aliases={2: 0} if before else {},
        time=26,
    )


def middle_part(ids, parts, members, weight, tokens, upstream, late, frames, after=()):
    rows = tokens.shape[1]
    size = rows // frames
    group = D // members

    def kernel(ids_ref, *refs):
        part_refs = refs[: len(parts)]
        weight_ref, tokens_ref, g_own, g_other, late_ref = refs[len(parts) : len(parts) + 5]
        low_ref, projected_ref, middle_ref, normed_ref, grad_ref, across = refs[len(parts) + 5 :]
        for member in range(members):
            at = member * group
            for ref in part_refs:
                across[at : at + ref.shape[1], :] = ref[member]
                at += ref.shape[1]
        low = across[...].T
        low_ref[...] = low
        projected = dot(low, weight_ref[...].reshape(D, D))
        projected_ref[...] = projected
        middle = tokens_ref[0].astype(WIDE) + piece(late_ref, 0, frames) * projected
        middle_ref[...] = middle
        normed, _ = norm_parts(middle)
        shift, scale = piece(late_ref, 1, frames), piece(late_ref, 2, frames)
        normed_ref[...] = (normed * (1.0 + scale) + shift).astype(LOW)
        upstream = read_pair(ids_ref, g_own, g_other)
        grad_ref[...] = (piece(late_ref, 3, frames) * upstream).astype(LOW)

    part_specs = [
        pl.BlockSpec(part.shape[:2] + (size,), lambda r, f, ids: (0, 0, r * frames + f))
        for part in parts
    ]
    return call(
        kernel,
        "middle_part",
        ids,
        (2, frames),
        [*parts, weight[0], tokens, *upstream, late],
        part_specs
        + [weight[1], chunk_spec(rows, frames)]
        + pair_specs(rows, frames)
        + [whole(late.shape)],
        [
            low_array(2 * rows, D),
            wide_array(2 * rows, D),
            wide_array(2 * rows, D),
            low_array(2 * rows, D),
            low_array(2 * rows, D),
        ],
        [row_spec(rows, frames)] * 5,
        [pltpu.VMEM((D, size), LOW)],
        after,
        time=12,
    )


def quarter_at(step, ids, core_mask, pairs):
    core = bit_of(ids[2], core_mask)
    return step % pairs * 2 + jnp.where(step < pairs, 1 - core, core)


def feed(ids, rows, grads, up, down, hidden, devices, core_mask, pairs, after=()):
    tokens, width = rows.shape
    chunk = 512
    own_up, own_down = width // devices, hidden // devices
    aside = width // chunk
    quarter = width // (2 * pairs)
    owners = devices // 2
    spans = hidden // (2 * pairs) // chunk
    steps = hidden // chunk
    kind = LOW if own_up % 16 == 0 else WIDE

    def chunk_at(step, ids):
        return quarter_at(step // spans, ids, core_mask, pairs) * spans + step % spans

    def kernel(
        ids_ref,
        rows_ref,
        grad_ref,
        up_ref,
        down_ref,
        branch_ref,
        back_ref,
        down_sent,
        down_kept,
        up_sent,
        up_kept,
        across,
    ):
        step = pl.program_id(0)

        @pl.when(step == 0)
        def _():
            across[...] = rows_ref[...].T
            branch_ref[...] = jnp.zeros_like(branch_ref)
            back_ref[...] = jnp.zeros_like(back_ref)

        grads = grad_ref[...]
        up, down = up_ref[...].reshape(width, chunk), down_ref[...].reshape(chunk, width)
        upper = dot(rows_ref[...], up)
        hidden_grad = dot(grads, down.T)
        root = math.sqrt(2 / math.pi)
        square = upper * upper
        curve = jnp.tanh(upper * (root + root * 0.044715 * square))
        share = 0.5 + 0.5 * curve
        low = (upper * share).astype(LOW)
        slope = share + 0.5 * upper * (1.0 - curve * curve) * (root + 3 * root * 0.044715 * square)
        upper_grad = (hidden_grad * slope).astype(LOW)
        branch_ref[...] += dot(low, down)
        back_ref[...] += dot(upper_grad, up.T)
        down_grad = dot(low.T, grads)

        @pl.when(step < steps // 2)
        def _():
            down_sent[...] = down_grad.astype(LOW).reshape(down_sent.shape)

        @pl.when(step >= steps // 2)
        def _():
            down_kept[...] = down_grad.astype(kind).reshape(down_kept.shape)

        core = bit_of(ids_ref[2], core_mask)
        taken = owners // pairs
        for out, bit in ((up_sent, 1 - core), (up_kept, core)):
            for number in range(pairs):
                start = pl.multiple_of((2 * number + bit) * quarter, quarter)
                value = dot(across[pl.ds(start, quarter), :], upper_grad).astype(out.dtype)
                out[number * taken : (number + 1) * taken] = value.reshape(
                    (taken,) + out.shape[1:]
                )

    def sent_at(step, ids):
        return (jnp.minimum(step, steps // 2 - 1), 0, 0)

    def kept_at(step, ids):
        return (jnp.maximum(step - steps // 2, 0), 0, 0)

    def up_at(step, ids):
        at = chunk_at(step, ids)
        return (0, at // aside, 0, at % aside)

    down_block = (chunk // own_down, own_down, width)
    up_block = (owners, 1, own_up, chunk)
    up_shape = (owners, hidden // width, own_up, width)
    return call(
        kernel,
        "feed",
        ids,
        (steps,),
        [rows, grads, up[0], down[0]],
        [
            whole((tokens, width)),
            whole((tokens, width)),
            pl.BlockSpec(up[1], lambda step, ids: up[2](chunk_at(step, ids))),
            pl.BlockSpec(down[1], lambda step, ids: down[2](chunk_at(step, ids))),
        ],
        [
            wide_array(tokens, width),
            wide_array(tokens, width),
            low_array(owners, own_down, width),
            jax.ShapeDtypeStruct((owners, own_down, width), kind),
            low_array(*up_shape) if kind == LOW else wide_array(*up_shape),
            jax.ShapeDtypeStruct(up_shape, kind),
        ],
        [
            whole((tokens, width)),
            whole((tokens, width)),
            pl.BlockSpec(down_block, sent_at),
            pl.BlockSpec(down_block, kept_at),
            pl.BlockSpec(up_block, up_at),
            pl.BlockSpec(up_block, up_at),
        ],
        [pltpu.VMEM((width, tokens), LOW)],
        after,
        room=62,
        time=66,
    )


def middle_back(ids, middle, branch, back, projected, upstream, late, frames, after=()):
    rows = upstream[1].shape[0]

    def kernel(
        ids_ref,
        middle_ref,
        branch_ref,
        back_ref,
        projected_ref,
        g_own,
        g_other,
        late_ref,
        result_ref,
        middle_grad_ref,
        projected_grad_ref,
        pieces_ref,
    ):
        middle, branch = middle_ref[...], branch_ref[...]
        upstream = read_pair(ids_ref, g_own, g_other)
        result_ref[0] = (middle + piece(late_ref, 3, frames) * branch).astype(LOW)
        normed, inverse = norm_parts(middle)
        grad, shift_grad, scale_grad = norm_back(
            back_ref[...], normed, inverse, piece(late_ref, 2, frames)
        )
        grad = grad + upstream
        middle_grad_ref[...] = grad
        projected_grad_ref[...] = (piece(late_ref, 0, frames) * grad).astype(LOW)
        gate_grad = jnp.sum(grad * projected_ref[...], axis=0, keepdims=True)
        put_piece(pieces_ref, 0, frames, gate_grad)
        put_piece(pieces_ref, 1, frames, shift_grad)
        put_piece(pieces_ref, 2, frames, scale_grad)
        put_piece(pieces_ref, 3, frames, jnp.sum(upstream * branch, axis=0, keepdims=True))

    block = row_spec(rows, frames)
    return call(
        kernel,
        "middle_back",
        ids,
        (2, frames),
        [middle, branch, back, projected, *upstream, late],
        [block] * 4 + pair_specs(rows, frames) + [whole(late.shape)],
        [
            low_array(2, rows, D),
            wide_array(2 * rows, D),
            low_array(2 * rows, D),
            wide_array(2 * frames, 4 * D),
        ],
        [chunk_spec(rows, frames)] + [block] * 2 + [whole((2 * frames, 4 * D))],
        after=after,
        time=12,
    )


def put_half(step, pairs, value, sent_ref, kept_ref):
    @pl.when(step < pairs)
    def _():
        sent_ref[0] = value.astype(LOW)

    @pl.when(step >= pairs)
    def _():
        kept_ref[0] = value


def half_specs(pairs, rows, width):
    return [
        pl.BlockSpec((1, rows, width), lambda i, ids: (jnp.minimum(i, pairs - 1), 0, 0)),
        pl.BlockSpec((1, rows, width), lambda i, ids: (jnp.maximum(i - pairs, 0), 0, 0)),
    ]


def hand_out(ids, weight, gradient, attended, members, head_count, core_mask, pairs, after=()):
    tokens, width = gradient.shape
    quarter = width // (2 * pairs)
    groups = members // (2 * pairs)
    group = width // members
    front = group - HEAD

    def kernel(ids_ref, weight_ref, grad_ref, attended_ref, *refs):
        *out_refs, sent_ref, kept_ref = refs
        step = pl.program_id(0)
        grads = grad_ref[...]
        if weight_ref.shape[0] == 1:
            taken = weight_ref[0, pl.ds(pl.multiple_of(step * quarter, quarter), quarter), :]
        else:
            blocks = quarter // weight_ref.shape[1]
            taken = weight_ref[pl.ds(step * blocks, blocks)].reshape(quarter, width)
        block = contract(taken, grads, 1, 1).astype(LOW)
        for number in range(groups):
            at = number * group
            out_refs[0][number] = block[at + front : at + group]
            if front:
                out_refs[1][number] = block[at : at + front]
        put_half(step, pairs, dot(attended_ref[...].T, grads), sent_ref, kept_ref)

    shapes = [(members, HEAD, tokens)] + [(members, front, tokens)] * (front > 0)
    halves = (pairs, quarter, width)
    return call(
        kernel,
        "hand_out",
        ids,
        (2 * pairs,),
        [weight[0], gradient, attended],
        [
            weight[1],
            whole(gradient.shape),
            pl.BlockSpec(
                (tokens, quarter), lambda i, ids: (0, quarter_at(i, ids, core_mask, pairs))
            ),
        ],
        [low_array(*shape) for shape in shapes] + [low_array(*halves), wide_array(*halves)],
        [
            pl.BlockSpec((groups,) + shape[1:], lambda i, ids: (i, 0, 0))
            for shape in shapes
        ]
        + half_specs(pairs, quarter, width),
        after=after,
        time=10,
    )


def turn_back(operand, cosines, sines):
    half = HEAD // 2
    one, two = operand[:half], operand[half:]
    return jnp.concatenate([one * cosines + two * sines, two * cosines - one * sines], axis=0)


def attend_back(ids, parts, grads, head, wide, total, cosines, sines, after=()):
    members, _, _, tokens = parts.shape
    size, block = min(1024, tokens), min(512, tokens)
    length = members * tokens
    per, count, inside = tokens // size, length // block, tokens // block
    back = HEAD ** (-0.5)

    def kernel(
        ids_ref,
        part_ref,
        grad_ref,
        wide_ref,
        total_ref,
        cos_ref,
        sin_ref,
        out_ref,
        key_rows,
        key_sum,
        value_sum,
    ):
        step = pl.program_id(0)

        @pl.when(step == 0)
        def _():
            for member in range(members):
                key_rows[member * tokens : (member + 1) * tokens, :] = part_ref[member, 1].T
            key_sum[...] = jnp.zeros_like(key_sum)
            value_sum[...] = jnp.zeros_like(value_sum)

        member = step // per
        start = 0 if per == 1 else pl.multiple_of(step % per * size, size)
        queries_across = part_ref[member, 0, :, pl.ds(start, size)]
        grads_across = grad_ref[member, :, pl.ds(start, size)]
        queries = queries_across.T
        out_grads = grads_across.T
        delta = jnp.sum(grads_across.astype(WIDE) * wide_ref[...], axis=0, keepdims=True).T
        totals = total_ref[...].T
        query_grad = jnp.zeros((size, HEAD), WIDE)

        def pair(number):
            source, at = number // inside, number % inside * block
            return (
                dot(queries, part_ref[source, 1, :, at : at + block]),
                dot(out_grads, part_ref[source, 2, :, at : at + block]),
            )

        following = pair(0)
        for number in range(count):
            scores, prob_grad = following
            if number + 1 < count:
                following = pair(number + 1)
            here = slice(number * block, (number + 1) * block)
            probs = jnp.exp2(scores * SOFT - totals)
            score_grad = (probs * (prob_grad - delta)).astype(LOW)
            value_sum[:, here] += dot(grads_across, probs.astype(LOW))
            key_sum[:, here] += dot(queries_across, score_grad)
            query_grad += dot(score_grad, key_rows[here, :])

        where = pl.multiple_of(step * size, size)
        out_ref[member, 0, :, pl.ds(start, size)] = turn_back(
            query_grad.T * back, cos_ref[:, pl.ds(where, size)], sin_ref[:, pl.ds(where, size)]
        ).astype(LOW)

        @pl.when(step == length // size - 1)
        def _():
            for source in range(members):
                span = slice(source * tokens, (source + 1) * tokens)
                out_ref[source, 1] = turn_back(
                    key_sum[:, span] * back, cos_ref[:, span], sin_ref[:, span]
                ).astype(LOW)
                out_ref[source, 2] = value_sum[:, span].astype(LOW)

    return call(
        kernel,
        "attend_back",
        ids,
        (length // size,),
        [parts, grads, wide, total, cosines, sines],
        [
            whole(parts.shape),
            pl.BlockSpec((members, HEAD, tokens), lambda i, ids: (0, head, 0)),
            pl.BlockSpec((HEAD, size), lambda i, ids: (0, i)),
            pl.BlockSpec((1, size), lambda i, ids: (0, i)),
            whole(cosines.shape),
            whole(sines.shape),
        ],
        low_array(members, 3, HEAD, tokens),
        whole((members, 3, HEAD, tokens)),
        [
            pltpu.VMEM((length, HEAD), LOW),
            pltpu.VMEM((HEAD, length), WIDE),
            pltpu.VMEM((HEAD, length), WIDE),
        ],
        after,
        time=44,
    )


def joint_back(ids, parts, normed, weight, column, total, core_mask, pairs, after=()):
    members, _, _, tokens = parts.shape
    group = members * HEAD
    width = 3 * group
    quarter = D // (2 * pairs)
    halves = (pairs, quarter, width)
    before = [] if total is None else [total]

    def kernel(ids_ref, part_ref, normed_ref, weight_ref, *refs):
        *total_refs, sent_ref, kept_ref, total_ref, across, lined = refs
        step = pl.program_id(0)

        @pl.when(step == 0)
        def _():
            for member in range(members):
                for kind in range(3):
                    at = kind * group + member * HEAD
                    across[at : at + HEAD, :] = part_ref[member, kind]
            lined[...] = across[...].T

        rows = lined[...]
        put_half(step, pairs, dot(normed_ref[...].T, rows), sent_ref, kept_ref)
        added = contract(rows, weight_ref[...], 1, 1)
        total_ref[...] = total_refs[0][...] + added if total_refs else added

    def at(i, ids):
        return quarter_at(i, ids, core_mask, pairs)

    strip = pl.BlockSpec((tokens, quarter), lambda i, ids: (0, at(i, ids)))
    return call(
        kernel,
        "joint_back",
        ids,
        (2 * pairs,),
        [parts, normed, weight, *before],
        [
            whole(parts.shape),
            strip,
            pl.BlockSpec((quarter, width), lambda i, ids: (at(i, ids), column)),
        ]
        + [strip] * len(before),
        [low_array(*halves), wide_array(*halves), wide_array(tokens, D)],
        half_specs(pairs, quarter, width) + [strip],
        [pltpu.VMEM((width, tokens), LOW), pltpu.VMEM((tokens, width), LOW)],
        after,
        time=10,
    )


def tokens_back(ids, gradient, tokens, middle_grad, early, frames, after=()):
    rows = tokens.shape[1]
    size = rows // frames

    def kernel(
        ids_ref, grad_ref, tokens_ref, middle_ref, early_ref, own_ref, other_ref, pieces_ref
    ):
        normed, inverse = norm_parts(tokens_ref[0].astype(WIDE))
        grad, shift_grad, scale_grad = norm_back(
            grad_ref[...], normed, inverse, piece(early_ref, 1, frames)
        )
        grad = grad + middle_ref[...]
        put_piece(pieces_ref, 0, frames, shift_grad)
        put_piece(pieces_ref, 1, frames, scale_grad)

        @pl.when(pl.program_id(0) == ids_ref[1])
        def _():
            own_ref[...] = grad

        @pl.when(pl.program_id(0) != ids_ref[1])
        def _():
            other_ref[...] = grad.astype(LOW)

    def chunk_at(number):
        def index(r, f, ids):
            mine = ids[1] if number == 0 else 1 - ids[1]
            return (jnp.where(r == mine, f, jnp.where(r < mine, 0, frames - 1)), 0)

        return index

    block = row_spec(rows, frames)
    return call(
        kernel,
        "tokens_back",
        ids,
        (2, frames),
        [gradient, tokens, middle_grad, early],
        [block, chunk_spec(rows, frames), block, whole(early.shape)],
        [wide_array(rows, D), low_array(rows, D), wide_array(2 * frames, 2 * D)],
        [
            pl.BlockSpec((size, D), chunk_at(0)),
            pl.BlockSpec((size, D), chunk_at(1)),
            whole((2 * frames, 2 * D)),
        ],
        after=after,
        time=9,
    )


def two_clips(ids, own, others, kind, frames, after=()):
    rows = others.shape[0]
    size = rows // frames
    if own.ndim == 3:
        own_spec = pl.BlockSpec((1, size, D), lambda r, f, ids: (ids[1], f, 0))
    else:
        own_spec = pl.BlockSpec((size, D), lambda r, f, ids: (f, 0))

    def kernel(ids_ref, own_ref, other_ref, out_ref):
        mine = pl.program_id(0) == ids_ref[1]

        @pl.when(mine)
        def _():
            out_ref[0] = own_ref[...].reshape(size, D).astype(kind)

        @pl.when(jnp.logical_not(mine))
        def _():
            out_ref[0] = other_ref[...].astype(kind)

    return call(
        kernel,
        "two_clips",
        ids,
        (2, frames),
        [own, others],
        [own_spec, pl.BlockSpec((size, D), lambda r, f, ids: (f, 0))],
        jax.ShapeDtypeStruct((2, rows, D), kind),
        chunk_spec(rows, frames),
        after=after,
        time=3,
    )


def modulation_back(ids, condition, pieces, after=()):
    count, width = pieces.shape
    own = condition.shape[1]
    size = 1024

    def kernel(ids_ref, condition_ref, pieces_ref, out_ref, sum_ref):
        pieces = pieces_ref[...]
        out_ref[...] = lax.dot_general(
            condition_ref[...].astype(WIDE).T,
            pieces,
            (((1,), (0,)), ((), ())),
            precision=highest,
            preferred_element_type=WIDE,
        )
        sum_ref[...] = jnp.sum(pieces, axis=0, keepdims=True)

    return call(
        kernel,
        "modulation_back",
        ids,
        (width // size,),
        [condition, pieces],
        [whole(condition.shape), pl.BlockSpec((count, size), lambda i, ids: (0, i))],
        [wide_array(own, width), wide_array(1, width)],
        [
            pl.BlockSpec((own, size), lambda i, ids: (0, i)),
            pl.BlockSpec((1, size), lambda i, ids: (0, i)),
        ],
        after=after,
        time=4,
    )


def join_and_add(ids, joins, adds, after=()):
    ins, outs = [], []
    for own, arrived, _ in joins:
        ins += [own, arrived]
        pre, post, width = own.shape
        outs.append(jax.ShapeDtypeStruct((pre, 2, post, width), own.dtype))
    for kept, arrived, final in adds:
        ins += [kept, arrived]
        rows, width = kept.shape
        outs += [wide_array(rows, width)] if final else [wide_array(rows // 2, width)] * 2

    def kernel(ids_ref, *refs):
        in_refs, out_refs = list(refs[: len(ins)]), list(refs[len(ins) :])
        for _, _, mask in joins:
            own, arrived, out = in_refs.pop(0), in_refs.pop(0), out_refs.pop(0)
            bit = bit_of(ids_ref[2], mask)
            for row in range(own.shape[0]):
                out[row, pl.ds(bit, 1)] = own[row][None]
                out[row, pl.ds(1 - bit, 1)] = arrived[row][None]
        for _, _, final in adds:
            kept, arrived = in_refs.pop(0), in_refs.pop(0)
            rows = kept.shape[0]
            if final:
                out_refs.pop(0)[...] = kept[...] + arrived[...]
            else:
                for start in (0, rows // 2):
                    span = slice(start, start + rows // 2)
                    out_refs.pop(0)[...] = kept[span] + arrived[span]

    return call(
        kernel,
        "join_and_add",
        ids,
        (1,),
        ins,
        [whole(value.shape) for value in ins],
        outs,
        [whole(out.shape) for out in outs],
        after=after,
        time=3,
    )


def stack_rows(ids, first, second, after=()):
    count, width = first.shape

    def kernel(ids_ref, first_ref, second_ref, out_ref):
        out_ref[:count] = first_ref[...]
        out_ref[count:] = second_ref[...]

    return call(
        kernel,
        "stack_rows",
        ids,
        (1,),
        [first, second],
        [whole(first.shape)] * 2,
        wide_array(2 * count, width),
        whole((2 * count, width)),
        after=after,
    )


def pack(ids, down, up, output, after=()):
    count = down.shape[0] + up.shape[0] * (up.shape[1] // D) + output.shape[0]

    def kernel(ids_ref, down_ref, up_ref, output_ref, out_ref):
        at = 0
        pieces = [down_ref[...]]
        pieces += [up_ref[:, i * D : (i + 1) * D] for i in range(up.shape[1] // D)]
        for value in pieces + [output_ref[...]]:
            out_ref[at : at + value.shape[0]] = value.astype(LOW)
            at += value.shape[0]

    return call(
        kernel,
        "pack",
        ids,
        (1,),
        [down, up, output],
        [whole(down.shape), whole(up.shape), whole(output.shape)],
        low_array(count, D),
        whole((count, D)),
        after=after,
        time=3,
    )


def other_clip(ids, tokens, frames, after=()):
    rows = tokens.shape[1]
    size = rows // frames

    def kernel(ids_ref, in_ref, out_ref):
        out_ref[...] = in_ref[0]

    return call(
        kernel,
        "other_clip",
        ids,
        (frames,),
        [tokens],
        [pl.BlockSpec((1, size, D), lambda f, ids: (1 - ids[1], f, 0))],
        low_array(rows, D),
        pl.BlockSpec((size, D), lambda f, ids: (f, 0)),
        after=after,
    )


def copy_of(ids, value, after=()):
    def kernel(ids_ref, in_ref, out_ref):
        out_ref[...] = in_ref[...]

    return call(
        kernel,
        "copy_of",
        ids,
        (1,),
        [value],
        [whole(value.shape)],
        jax.ShapeDtypeStruct(value.shape, value.dtype),
        whole(value.shape),
        after=after,
    )


def halve(ids, jobs, after=()):
    ins, in_specs, outs, out_specs = [], [], [], []
    count = jobs[0][1].shape[0]
    together = min([post or 1 for _, _, post, _ in jobs] + [4])
    steps = max(1, count // 2) // together
    for kept, arrived, post, mask in jobs:
        block = (together,) + arrived.shape[1:]

        def source(i, ids, side, post=post // together, mask=mask):
            if not post:
                return (i, 0, 0)
            bit = bit_of(ids[2], mask)
            return (i // post * 2 * post + (bit if side else 1 - bit) * post + i % post, 0, 0)

        for side in (0, 1) if post else (1,):
            ins += [kept, arrived]
            spec = pl.BlockSpec(
                block, lambda i, ids, side=side, source=source: source(i, ids, side)
            )
            in_specs += [spec, spec]
            kind = LOW if side == 0 else WIDE
            outs.append(jax.ShapeDtypeStruct((max(1, count // 2),) + arrived.shape[1:], kind))
            out_specs.append(pl.BlockSpec(block, lambda i, ids: (i, 0, 0)))

    def kernel(ids_ref, *refs):
        for number, out in enumerate(refs[len(ins) :]):
            value = refs[2 * number][...].astype(WIDE) + refs[2 * number + 1][...].astype(WIDE)
            out[...] = value.astype(out.dtype)

    return call(kernel, "halve", ids, (steps,), ins, in_specs, outs, out_specs, after=after, time=5)


def halve_plain(rank, jobs):
    outs = []
    for kept, arrived, post, mask in jobs:
        value = kept.astype(WIDE) + arrived.astype(WIDE)
        if not post:
            outs.append(value)
            continue
        split = value.reshape((-1, 2, post) + value.shape[1:])
        for side in (1 - bit_of(rank, mask), bit_of(rank, mask)):
            taken = lax.dynamic_index_in_dim(split, side, 1, keepdims=False)
            outs.append(taken.reshape((-1,) + value.shape[1:]))
        outs[-2] = outs[-2].astype(LOW)
    return outs


def per_device(
    clip_size,
    seq_size,
    frames_in,
    noise_level,
    frame_time,
    cotangent,
    joint_weight,
    output_weight,
    up_weight,
    down_weight,
    modulation,
    modulation_bias,
    first_joint,
    first_output,
    first_up,
    first_down,
    first_modulation,
    first_bias,
    second_joint,
    second_output,
    second_up,
    second_down,
    second_modulation,
    second_bias,
):
    devices = clip_size * seq_size
    masters = (joint_weight, output_weight, up_weight, down_weight, modulation, modulation_bias)
    firsts = (first_joint, first_output, first_up, first_down, first_modulation, first_bias)
    seconds = (second_joint, second_output, second_up, second_down, second_modulation, second_bias)
    clip_id, seq_id = lax.axis_index("clip"), lax.axis_index("seq")
    rank = clip_id * seq_size + seq_id
    half = seq_size // 2
    side = seq_id // half
    members = half
    ids = jnp.stack([seq_id % half, side, rank]).astype(jnp.int32)
    head_count = HEADS // members
    group_ids = [[i * half + j for j in range(half)] for i in range(2)]
    last = []

    def swap_with(value, mask):
        return lax.ppermute(value, AXES, [(i, i ^ mask) for i in range(devices)])

    def pick(value, index):
        return lax.dynamic_index_in_dim(value, index, 0, keepdims=False)

    def run(kernel, *args, **options):
        result = kernel(ids, *args, after=tuple(last), **options)
        last[:] = jax.tree.leaves(result)[:1]
        return result

    clip_masks = [seq_size << bit for bit in range(clip_size.bit_length() - 1)]
    seq_masks = [1 << bit for bit in range(seq_size.bit_length() - 1)]
    order = clip_masks + seq_masks
    core_mask = clip_masks[0]
    pairs = clip_size // 2

    local_rows = frames_in.shape[1]
    frames = max(1, local_rows // PATCHES)
    tokens_here = 2 * local_rows
    pair_ids = [[j, j + half] for j in range(half)]
    tokens = lax.all_to_all(frames_in, "seq", 0, 0, axis_index_groups=pair_ids)

    levels = noise_level.astype(WIDE)[None]
    for mask in clip_masks:
        levels = jnp.concatenate([levels, swap_with(levels, mask)], axis=0)
    all_levels = levels.reshape(-1)
    masks = [0]
    for mask in reversed(order):
        masks = masks + [other ^ mask for other in masks]
    own_width = modulation.shape[0]
    columns = rank * own_width + jnp.arange(own_width, dtype=jnp.int32)
    half_width = D // 2
    frequency = jnp.exp(-math.log(10000.0) * (columns % half_width).astype(WIDE) / half_width)

    def condition_of(targets):
        seq_of = targets % seq_size
        chunk = jnp.stack([seq_of % half, seq_of % half + half], axis=1)
        frame_of = chunk[:, :, None] * local_rows // PATCHES + jnp.arange(frames, dtype=jnp.int32)
        clip_of = (targets // seq_size ^ clip_id) * 2 + seq_of // half
        level_ids = (clip_of[:, None, None] * FRAMES + frame_of).reshape(-1)
        every = jnp.arange(all_levels.shape[0], dtype=jnp.int32)
        level_of = jnp.sum(jnp.where(level_ids[:, None] == every, all_levels, 0.0), axis=1)
        angles = level_of[:, None] * frequency
        wave = jnp.where(columns < half_width, jnp.cos(angles), jnp.sin(angles))
        return jax.nn.silu(wave).astype(LOW)

    condition = condition_of(rank ^ jnp.array(masks, jnp.int32))

    bias_width = modulation_bias.shape[0]
    bias_row = lax.dynamic_update_slice_in_dim(
        jnp.zeros((6 * D,), WIDE), modulation_bias.astype(LOW).astype(WIDE), rank * bias_width, 0
    )
    modulation_low = modulation.astype(LOW)

    class Terms:
        def __init__(self, condition, first, stop):
            terms = dot(condition, modulation_low[:, first:stop]) + bias_row[first:stop]
            middle = terms.shape[0] // 2
            self.kept, self.sent = terms[:middle], terms[middle:]
            self.masks = order[:]
            self.send()

        def send(self):
            self.arrived = swap_with(self.sent, self.masks.pop(0))

        def job(self):
            return (self.kept, self.arrived, not self.masks)

        def take(self, outs):
            self.kept = outs.pop(0)
            if self.masks:
                self.sent = outs.pop(0)
                self.send()

    rows = joint_weight.shape[0]
    joint_low = joint_weight.astype(LOW).reshape(rows, 3, members, head_count, HEAD)
    joint_low = jnp.transpose(joint_low, (0, 3, 1, 2, 4)).reshape(1, rows, 3 * D)
    far = seq_masks[:0:-1]
    routes = [
        far + [seq_masks[0]] + clip_masks[::-1],
        far + clip_masks[:0:-1] + [seq_masks[0], clip_masks[0]],
    ]
    joined = [joint_low]
    early_terms = None
    for stage in range(len(order) + 1):
        joins = []
        if stage < len(order):
            if stage == len(far):
                middle_column = joint_low.shape[2] // 2
                joined = [joined[0][..., :middle_column], joined[0][..., middle_column:]]
            for value, route in zip(joined, routes):
                mask, done = route[stage], route[:stage]
                pre = 2 ** sum(1 for other in done if other > mask)
                width = value.shape[-1]
                own = value.reshape(pre, -1, width)
                arrived = swap_with(value, mask).reshape(pre, -1, width)
                joins.append((own, arrived, mask))
        if stage == 1:
            early_terms = Terms(condition, 0, 2 * D)
        adds = [early_terms.job()] if stage else []
        if stage == 3:
            last.append(tokens)
        outs = list(run(join_and_add, joins, adds))
        if stage < len(order):
            joined = [outs.pop(0) for _ in joins]
            joined = [value.reshape(1, -1, value.shape[-1]) for value in joined]
        if stage:
            early_terms.take(outs)
    early = early_terms.kept
    joint_sides = [value[0] for value in joined]
    if head_count % 2:
        joint_sides = [jnp.concatenate(joint_sides, axis=1)]
    heads_aside = head_count // len(joint_sides)

    up_blocks = FF // D
    own_up = up_weight.shape[0]
    own_down = down_weight.shape[0]
    tiled = own_up % 16 == 0
    packed = run(pack, down_weight, up_weight, output_weight)
    packed = lax.all_gather(packed, AXES, axis=0, tiled=False)
    chunk_rows = 512
    up_first = own_down // own_up
    if tiled:
        chunks_aside = D // chunk_rows
        up_source = (
            packed,
            (devices, own_up, chunk_rows),
            lambda at: (0, up_first + at // chunks_aside, at % chunks_aside),
        )
        output_source = (
            packed,
            pl.BlockSpec((devices, own_up, D), lambda *at: (0, up_first + up_blocks, 0)),
        )
    else:
        upward = packed[:, own_down : own_down + own_up * up_blocks]
        upward = jnp.transpose(
            upward.reshape(devices, up_blocks, own_up, D), (0, 2, 1, 3)
        ).reshape(1, D, FF)
        up_source = (upward, (1, D, chunk_rows), lambda at: (0, 0, at))
        output_full = packed[:, own_down + own_up * up_blocks :].reshape(1, D, D)
        output_source = (output_full, whole((1, D, D)))
    down_source = (packed, (chunk_rows // own_down, own_down, D), lambda at: (at, 0, 0))

    member_seq = side * half + jnp.arange(members, dtype=jnp.int32)
    starts = jnp.stack([member_seq % half, member_seq % half + half], axis=1) * local_rows
    places = (starts[:, :, None] + jnp.arange(local_rows, dtype=jnp.int32)).reshape(-1)
    cosines, sines = rotary_tables(pick(frame_time, side), places)

    normed_one_low = run(norm_one, tokens, early, frames)

    def exchange(value):
        return lax.all_to_all(value, "seq", 0, 0, axis_index_groups=group_ids)

    late_terms = Terms(run(copy_of, condition), 2 * D, 6 * D)

    def late_step():
        if late_terms.masks or late_terms.arrived is not None:
            final = not late_terms.masks
            outs = list(run(join_and_add, [], [late_terms.job()]))
            late_terms.take(outs)
            if final:
                late_terms.arrived = None

    def project_head(head):
        weight, offset = joint_sides[head // heads_aside], head % heads_aside
        return exchange(
            run(project, normed_one_low, weight, cosines, sines, members, offset)
        )

    parts = {0: project_head(0)}
    late_step()
    upstream = (cotangent, swap_with(run(other_clip, cotangent, frames), half))
    wide, totals = {}, {}
    front = None
    front_heads = head_count - 1
    for head in range(head_count):
        if head + 1 < head_count:
            parts[head + 1] = project_head(head + 1)
            late_step()
        else:
            last.append(upstream[1])
        if head < front_heads:
            front, wide[head], totals[head] = run(attend, parts[head], front, head, front_heads)
            if head + 1 == front_heads:
                front = exchange(front)
        else:
            back, wide[head], totals[head] = run(attend, parts[head], None, 0, 1)
        late_step()
    while late_terms.arrived is not None:
        late_step()
    late = late_terms.kept
    back = exchange(back)

    attended_low, projected, middle, normed_two_low, branch_grad = run(
        middle_part,
        [back] if front is None else [front, back],
        members,
        output_source,
        tokens,
        upstream,
        late,
        frames,
    )
    branch, normed_two_grad, down_sent, down_kept, up_sent, up_kept = run(
        feed,
        normed_two_low,
        branch_grad,
        up_source,
        down_source,
        FF,
        devices,
        core_mask,
        pairs,
    )

    class Chain:
        def __init__(self, sent, kept, masks):
            self.kept, self.masks = kept, list(masks)
            self.remaining = sorted(self.masks)
            self.arrived = swap_with(sent.astype(LOW), core_mask)

        def job(self):
            if not self.masks:
                return (self.kept, self.arrived, 0, 1)
            post = 2 ** self.remaining.index(self.masks[0])
            return (self.kept, self.arrived, post, self.masks[0])

        def take(self, outs):
            if self.masks:
                mask = self.masks.pop(0)
                self.remaining.remove(mask)
                self.arrived, self.kept = swap_with(outs.pop(0), mask), outs.pop(0)
            else:
                self.arrived, self.kept = None, outs.pop(0)

    def step(*chains):
        chains = [chain for chain in chains if chain.arrived is not None]
        if not chains:
            return
        jobs = [chain.job() for chain in chains]
        outs = list(run(halve, jobs)) if tiled else halve_plain(rank, jobs)
        for chain in chains:
            chain.take(outs)

    def owners(value):
        return value.reshape(devices // 2, -1, value.shape[2])

    one_way = clip_masks[1:] + seq_masks
    other_way = seq_masks[:1] + clip_masks[1:] + seq_masks[1:]
    up_shape = (devices // 2, up_blocks * own_up, D)
    down_chain = Chain(down_sent, down_kept, one_way)
    up_chain = Chain(up_sent.reshape(up_shape), up_kept.reshape(up_shape), other_way)

    result, middle_grad, projected_grad, late_rows = run(
        middle_back, middle, branch, normed_two_grad, projected, upstream, late, frames
    )
    *outer, output_sent, output_kept = run(
        hand_out,
        output_source,
        projected_grad,
        attended_low,
        members,
        head_count,
        core_mask,
        pairs,
    )
    outer_back = exchange(outer[0])
    output_chain = Chain(owners(output_sent), owners(output_kept), one_way)
    step(down_chain, up_chain)
    last.append(outer_back)
    late_pieces = lax.all_gather(late_rows, AXES, axis=0, tiled=True)

    class Frames:
        def __init__(self, rows):
            self.rows, self.masks = rows, order[::-1]
            self.send()

        def send(self):
            self.arrived = swap_with(self.rows, self.masks.pop(0)) if self.masks else None

        def step(self):
            if self.arrived is not None:
                self.rows = run(stack_rows, self.rows, self.arrived)
                self.send()

    def head_back(head):
        grads, at = (outer_front, head) if head < front_heads else (outer_back, 0)
        return run(
            attend_back, parts[head], grads, at, wide[head], totals[head], cosines, sines
        )

    def head_joint(head, total):
        weight, offset = joint_sides[head // heads_aside], head % heads_aside
        sent, kept, total = run(
            joint_back,
            joint_parts[head],
            normed_one_low,
            weight,
            offset,
            total,
            core_mask,
            pairs,
        )
        return owners(sent), owners(kept), total

    joint_parts, head_chains = {}, {}
    total = None
    outer_front = exchange(outer[1]) if front_heads else None
    heads = list(reversed(range(head_count)))
    ready = []
    for number, head in enumerate(heads):
        raw = head_back(head)
        joint_parts[head] = exchange(raw)
        if number == 0:
            other_rows = pick(result, 1 - side)
            if head_count > 1:
                other_rows = run(copy_of, other_rows)
            others = swap_with(other_rows, half)
        if number == min(2, head_count - 1):
            mixed = run(two_clips, result, others, LOW, frames)
        step(down_chain, up_chain)
        step(output_chain)
        if number == 2:
            for other in heads[:2]:
                sent, kept, total = head_joint(other, total)
                head_chains[other] = Chain(sent, kept, other_way if other % 2 else one_way)
            mod_late, sum_late = run(
                modulation_back, condition_of(jnp.arange(devices, dtype=jnp.int32)), late_pieces
            )
            step(*head_chains.values())
    early_chains = list(head_chains.values())
    late_chains = []
    waiting = [head for head in heads if head not in head_chains]
    for head in waiting:
        sent, kept, total = head_joint(head, total)
        head_chains[head] = Chain(sent, kept, other_way if head % 2 else one_way)
        late_chains.append(head_chains[head])
        step(*early_chains)
    own_rows, other_rows, early_rows = run(
        tokens_back, total, tokens, middle_grad, early, frames
    )
    early_frames = Frames(early_rows)
    others = swap_with(other_rows, half)
    chains = late_chains + early_chains + [up_chain, output_chain, down_chain]
    while any(chain.arrived is not None for chain in chains) or early_frames.arrived is not None:
        step(*late_chains)
        early_frames.step()
        step(*early_chains)
        step(down_chain, up_chain)
        step(output_chain)
    if head_count < 3:
        mod_late, sum_late = run(
            modulation_back, condition_of(jnp.arange(devices, dtype=jnp.int32)), late_pieces
        )
    mod_early, sum_early = run(modulation_back, condition, early_frames.rows)
    input_grad = run(two_clips, own_rows, others, WIDE, frames)

    output_sum = output_chain.kept[0]
    down_sum = down_chain.kept[0]
    up_sum = up_chain.kept[0].reshape(up_blocks, own_up, D)
    up_sum = jnp.transpose(up_sum, (1, 0, 2)).reshape(own_up, FF)
    joint_sum = jnp.stack([head_chains[head].kept[0] for head in range(head_count)], axis=1)
    joint_sum = joint_sum.reshape(rows, head_count, 3, members, HEAD)
    joint_sum = jnp.transpose(joint_sum, (0, 2, 3, 1, 4)).reshape(rows, 3 * D)
    mod_sum = jnp.concatenate([mod_early, mod_late], axis=1)
    bias_sum = lax.dynamic_slice_in_dim(
        jnp.concatenate([sum_early[0], sum_late[0]]), rank * bias_width, bias_width, 0
    )

    summed = (joint_sum, output_sum, up_sum, down_sum, mod_sum, bias_sum)
    squares = sum(jnp.sum(shard * shard) for shard in summed).reshape(1, 1)
    for mask in order:
        squares = squares + swap_with(squares, mask)
    grad_norm = jnp.sqrt(squares[0, 0])
    factor = jnp.minimum(1.0, clip_limit / (grad_norm + 1e-06))
    step_rates = (
        D ** (-0.5),
        max(1, 2 * D // LENGTH) ** (-0.5),
        D ** (-0.5),
        FF ** (-0.5),
        D ** (-0.5),
        0.5,
    )
    clipped = [shard * factor for shard in summed]
    updates = [
        adam_update(clipped[slot], masters[slot], firsts[slot], seconds[slot], step_rates[slot])
        for slot in range(6)
    ]
    return (
        mixed,
        input_grad,
        *clipped,
        grad_norm,
        *(update[0] for update in updates),
        *(update[1] for update in updates),
        *(update[2] for update in updates),
        *(update[2].astype(LOW) for update in updates),
    )


def solution(mesh):
    tokens = P("clip", "seq", None)
    rows = P(AXES, None)
    weights = (rows, rows, rows, rows, rows, P(AXES))
    in_specs = (tokens, P("clip", None), P("clip", None), tokens) + weights * 3
    out_specs = (tokens, tokens) + weights + (P(),) + weights * 4
    return jax.shard_map(
        partial(per_device, mesh.shape["clip"], mesh.shape["seq"]),
        mesh=mesh,
        in_specs=in_specs,
        out_specs=out_specs,
        check_vma=False,
    )
```

```python
from functools import partial
import math

import jax
import jax.numpy as jnp
from jax import lax
from jax.experimental import pallas as pl
from jax.experimental.pallas import tpu as pltpu
from jax.sharding import PartitionSpec as P

D = 1024
HEADS = 16
HEAD = 64
FF = 4096
FRAMES = 16
GRID_W = 16
STEP = 10
PATCHES = 256
LENGTH = 4096

norm_epsilon = 1e-06
adam_epsilon = 1e-08
first_decay = 0.5
second_decay = 0.5
weight_decay = 0.1
clip_limit = 1.0
highest = lax.Precision.HIGHEST
AXES = ("clip", "seq")
LOW = jnp.bfloat16
WIDE = jnp.float32
SOFT = math.log2(math.e) * HEAD ** (-0.5)


def dot(left, right):
    return jnp.dot(left, right, preferred_element_type=WIDE)


def contract(left, right, left_dim, right_dim):
    return lax.dot_general(
        left, right, (((left_dim,), (right_dim,)), ((), ())), preferred_element_type=WIDE
    )


def normalize(operand):
    centered = operand - jnp.mean(operand, axis=-1, keepdims=True)
    variance = jnp.mean(centered * centered, axis=-1, keepdims=True)
    return centered * lax.rsqrt(variance + norm_epsilon)


def modulate(operand, shift_by, scale_by):
    return normalize(operand) * (1.0 + scale_by) + shift_by


def adam_update(gradient, master, moment_one, moment_two, step_rate):
    moment_one = first_decay * moment_one + (1.0 - first_decay) * gradient
    moment_two = second_decay * moment_two + (1.0 - second_decay) * gradient * gradient
    corrected_one = moment_one / (1.0 - first_decay**STEP)
    corrected_two = moment_two / (1.0 - second_decay**STEP)
    master = master - step_rate * (
        corrected_one / (jnp.sqrt(corrected_two) + adam_epsilon) + weight_decay * master
    )
    return (moment_one, moment_two, master)


def rotary_tables(times, places):
    frame_ids = places // PATCHES
    patch_row = (places % PATCHES // GRID_W).astype(WIDE)
    column = (places % GRID_W).astype(WIDE)
    matches = frame_ids[None, :] == jnp.arange(FRAMES, dtype=jnp.int32)[:, None]
    moment = jnp.sum(jnp.where(matches, times[:, None], 0), axis=0).astype(WIDE)
    time_pairs = HEAD // 8
    grid_pairs = 3 * HEAD // 16
    pair_ids = jnp.arange(HEAD // 2, dtype=jnp.int32)
    second = time_pairs + grid_pairs
    offset = jnp.where(pair_ids < time_pairs, 0, jnp.where(pair_ids < second, time_pairs, second))
    length = jnp.where(pair_ids < time_pairs, time_pairs, grid_pairs)
    frequency = jnp.exp(
        -math.log(10000.0) * (pair_ids - offset).astype(WIDE) / length.astype(WIDE)
    )
    ids = pair_ids[:, None]
    coordinate = jnp.where(
        ids < time_pairs, moment[None], jnp.where(ids < second, patch_row[None], column[None])
    )
    angles = coordinate * frequency[:, None]
    return jnp.cos(angles), jnp.sin(angles)


anywhere = pl.BlockSpec(memory_space=pl.ANY)


def whole(shape):
    return pl.BlockSpec(shape, lambda *ids: (0,) * len(shape))


def call(
    kernel,
    name,
    ids,
    grid,
    ins,
    in_specs,
    outs,
    out_specs,
    scratch=(),
    after=(),
    room=56,
    aliases=None,
    time=2,
):
    count, extra = 1 + len(ins), len(after)

    def body(*refs):
        kernel(*refs[:count], *refs[count + extra :])

    body.__name__ = name
    return pl.pallas_call(
        body,
        grid_spec=pltpu.PrefetchScalarGridSpec(
            num_scalar_prefetch=1,
            grid=grid,
            in_specs=list(in_specs) + [anywhere] * extra,
            out_specs=out_specs,
            scratch_shapes=list(scratch),
        ),
        out_shape=outs,
        input_output_aliases=aliases or {},
        compiler_params=pltpu.CompilerParams(vmem_limit_bytes=room << 20),
        cost_estimate=pl.CostEstimate(
            flops=int(time * 1.15e9), bytes_accessed=int(time * 3e6), transcendentals=0
        ),
        name=name,
    )(ids, *ins, *after)


def low_array(*shape):
    return jax.ShapeDtypeStruct(shape, LOW)


def wide_array(*shape):
    return jax.ShapeDtypeStruct(shape, WIDE)


def bit_of(rank, mask):
    return rank // mask % 2


def chunk_spec(rows, frames):
    return pl.BlockSpec((1, rows // frames, D), lambda r, f, ids: (r, f, 0))


def pair_specs(rows, frames):
    size = rows // frames
    return [
        pl.BlockSpec((1, size, D), lambda r, f, ids: (ids[1], f, 0)),
        pl.BlockSpec((size, D), lambda r, f, ids: (f, 0)),
    ]


def row_spec(rows, frames):
    return pl.BlockSpec((rows // frames, D), lambda r, f, ids: (r * frames + f, 0))


def column_spec(rows, frames):
    return pl.BlockSpec((D, rows // frames), lambda r, f, ids: (0, r * frames + f))


def read_pair(ids_ref, own_ref, other_ref):
    own = pl.program_id(0) == ids_ref[1]
    return jnp.where(own, own_ref[0].astype(WIDE), other_ref[...].astype(WIDE))


def piece(ref, number, frames):
    row = pl.program_id(0) * frames + pl.program_id(1)
    return ref[pl.ds(row, 1), number * D : (number + 1) * D]


def put_piece(ref, number, frames, value):
    row = pl.program_id(0) * frames + pl.program_id(1)
    ref[pl.ds(row, 1), number * D : (number + 1) * D] = value


def norm_parts(operand):
    centered = operand - jnp.mean(operand, axis=-1, keepdims=True)
    variance = jnp.mean(centered * centered, axis=-1, keepdims=True)
    inverse = lax.rsqrt(variance + norm_epsilon)
    return centered * inverse, inverse


def norm_back(gradient, normed, inverse, scale):
    shift_grad = jnp.sum(gradient, axis=0, keepdims=True)
    scale_grad = jnp.sum(gradient * normed, axis=0, keepdims=True)
    inner = gradient * (1.0 + scale)
    mean = jnp.mean(inner, axis=-1, keepdims=True)
    along = jnp.mean(inner * normed, axis=-1, keepdims=True)
    return (inner - mean - normed * along) * inverse, shift_grad, scale_grad


def norm_one(ids, tokens, early, frames, after=()):
    rows = tokens.shape[1]

    def kernel(ids_ref, tokens_ref, early_ref, out_ref):
        normed, _ = norm_parts(tokens_ref[0].astype(WIDE))
        shift, scale = piece(early_ref, 0, frames), piece(early_ref, 1, frames)
        out_ref[...] = (normed * (1.0 + scale) + shift).astype(LOW).T

    return call(
        kernel,
        "norm_one",
        ids,
        (2, frames),
        [tokens, early],
        [chunk_spec(rows, frames), whole(early.shape)],
        low_array(D, 2 * rows),
        column_spec(rows, frames),
        after=after,
        time=5,
    )


def project(ids, rows, weight, cosines, sines, members, first, after=()):
    width, tokens = rows.shape
    columns = members * HEAD
    half = HEAD // 2

    def kernel(ids_ref, rows_ref, weight_ref, cos_ref, sin_ref, out_ref):
        across = dot(weight_ref[...].T, rows_ref[...])
        kind = pl.program_id(0)

        @pl.when(kind == 2)
        def _():
            for member in range(members):
                out_ref[member, 0] = across[member * HEAD : (member + 1) * HEAD].astype(LOW)

        @pl.when(kind < 2)
        def _():
            cosines, sines = cos_ref[...], sin_ref[...]
            for member in range(members):
                one = across[member * HEAD : member * HEAD + half]
                two = across[member * HEAD + half : (member + 1) * HEAD]
                out_ref[member, 0, :half] = (one * cosines - two * sines).astype(LOW)
                out_ref[member, 0, half:] = (two * cosines + one * sines).astype(LOW)

    table = pl.BlockSpec((half, tokens), lambda t, ids: (0, ids[0]))
    return call(
        kernel,
        "project",
        ids,
        (3,),
        [rows, weight, cosines, sines],
        [
            whole((width, tokens)),
            pl.BlockSpec((width, columns), lambda t, ids: (0, first * 3 + t)),
            table,
            table,
        ],
        low_array(members, 3, HEAD, tokens),
        pl.BlockSpec((members, 1, HEAD, tokens), lambda t, ids: (0, t, 0, 0)),
        after=after,
        time=6,
    )


def two_lows(value):
    high = value.astype(LOW)
    return high, (value - high.astype(WIDE)).astype(LOW)


def attend(ids, parts, into, head, heads, relative, after=()):
    members, _, _, tokens = parts.shape
    size, block = min(1024, tokens), min(512, tokens)
    length = members * tokens
    per, count, inside = tokens // size, length // block, tokens // block
    before = [] if into is None else [into]

    def kernel(ids_ref, part_ref, *refs):
        low_ref, wide_ref, total_ref, key_rows, key_top = refs[len(before) :]
        step = pl.program_id(0)

        @pl.when(step == 0)
        def _():
            top = jnp.zeros((1, 1), WIDE)
            for member in range(members):
                keys = part_ref[member, 1].astype(WIDE) * SOFT
                top = jnp.maximum(top, jnp.max(jnp.sum(keys * keys, axis=0, keepdims=True)))
                high, low = two_lows(keys)
                key_rows[member * tokens : (member + 1) * tokens, :] = jnp.concatenate(
                    [high, low], axis=0
                ).T
            key_top[...] = top

        member = step // per
        start = 0 if per == 1 else pl.multiple_of(step % per * size, size)
        queries = part_ref[member, 0, :, pl.ds(start, size)]
        doubled = jnp.concatenate([queries, queries], axis=0)
        wide_queries = queries.astype(WIDE)
        query_top = jnp.max(jnp.sum(wide_queries * wide_queries, axis=0, keepdims=True))
        bounded = query_top * jnp.max(key_top[...]) <= 60.0**2

        def scores_of(number):
            return dot(key_rows[number * block : (number + 1) * block, :], doubled)

        def values_of(number):
            at = number % inside * block
            return part_ref[number // inside, 2, :, at : at + block]

        def finish(gathered, total, top):
            attended = gathered / total
            wide_ref[...] = attended
            total_ref[...] = top + jnp.log2(total)
            target = member ^ ids_ref[0] if relative else member
            low_ref[target, :, pl.ds(start, size)] = attended.astype(LOW)

        @pl.when(bounded)
        def _():
            gathered = jnp.zeros((HEAD, size), WIDE)
            total = jnp.zeros((1, size), WIDE)
            following = scores_of(0)
            for number in range(count):
                scores = following
                if number + 1 < count:
                    following = scores_of(number + 1)
                probs = jnp.exp2(scores)
                total = total + jnp.sum(probs, axis=0, keepdims=True)
                gathered = gathered + dot(values_of(number), probs.astype(LOW))
            finish(gathered, total, 0.0)

        @pl.when(jnp.logical_not(bounded))
        def _():
            gathered = jnp.zeros((HEAD, size), WIDE)
            top = jnp.full((1, size), -1e30, WIDE)
            total = jnp.zeros((1, size), WIDE)
            following = scores_of(0)
            for number in range(count):
                scores = following
                if number + 1 < count:
                    following = scores_of(number + 1)
                raised = jnp.maximum(top, jnp.max(scores, axis=0, keepdims=True))
                shrink = jnp.exp2(top - raised)
                probs = jnp.exp2(scores - raised)
                total = total * shrink + jnp.sum(probs, axis=0, keepdims=True)
                gathered = gathered * shrink + dot(values_of(number), probs.astype(LOW))
                top = raised
            finish(gathered, total, top)

    return call(
        kernel,
        "attend",
        ids,
        (length // size,),
        [parts, *before],
        [whole(parts.shape)] + [anywhere] * len(before),
        [
            low_array(members, heads * HEAD, tokens),
            wide_array(HEAD, length),
            wide_array(1, length),
        ],
        [
            pl.BlockSpec((members, HEAD, tokens), lambda i, ids: (0, head, 0)),
            pl.BlockSpec((HEAD, size), lambda i, ids: (0, i)),
            pl.BlockSpec((1, size), lambda i, ids: (0, i)),
        ],
        [pltpu.VMEM((length, 2 * HEAD), LOW), pltpu.VMEM((1, 1), WIDE)],
        after,
        aliases={2: 0} if before else {},
        time=18,
    )


def middle_part(ids, front, backs, members, weight, tokens, upstream, late, frames, after=()):
    rows = tokens.shape[1]
    size = rows // frames
    group = D // members
    parts = [front] * (front is not None) + list(backs)

    def kernel(ids_ref, *refs):
        part_refs = list(refs[: len(parts)])
        weight_ref, tokens_ref, g_own, g_other, late_ref = refs[len(parts) : len(parts) + 5]
        low_ref, projected_ref, middle_ref, normed_ref, grad_ref, across = refs[len(parts) + 5 :]
        if front is not None:
            front_ref = part_refs.pop(0)
            for member in range(members):
                across[member * group : member * group + group - HEAD, :] = front_ref[member]
        for member, ref in enumerate(part_refs):
            at = pl.multiple_of((ids_ref[0] ^ member) * group + group - HEAD, HEAD)
            across[pl.ds(at, HEAD), :] = ref[...]
        low = across[...]
        low_ref[...] = low
        projected = dot(low.T, weight_ref[...].reshape(D, D))
        projected_ref[...] = projected
        middle = tokens_ref[0].astype(WIDE) + piece(late_ref, 0, frames) * projected
        middle_ref[...] = middle
        normed, _ = norm_parts(middle)
        shift, scale = piece(late_ref, 1, frames), piece(late_ref, 2, frames)
        normed_ref[...] = (normed * (1.0 + scale) + shift).astype(LOW)
        upstream = read_pair(ids_ref, g_own, g_other)
        grad_ref[...] = (piece(late_ref, 3, frames) * upstream).astype(LOW)

    part_specs = [
        pl.BlockSpec(
            part.shape[:-1] + (size,),
            lambda r, f, ids, lead=part.ndim - 1: (0,) * lead + (r * frames + f,),
        )
        for part in parts
    ]
    return call(
        kernel,
        "middle_part",
        ids,
        (2, frames),
        [*parts, weight[0], tokens, *upstream, late],
        part_specs
        + [weight[1], chunk_spec(rows, frames)]
        + pair_specs(rows, frames)
        + [whole(late.shape)],
        [
            low_array(D, 2 * rows),
            wide_array(2 * rows, D),
            wide_array(2 * rows, D),
            low_array(2 * rows, D),
            low_array(2 * rows, D),
        ],
        [column_spec(rows, frames)] + [row_spec(rows, frames)] * 4,
        [pltpu.VMEM((D, size), LOW)],
        after,
        time=12,
    )


def quarter_at(step, ids, core_mask, pairs):
    core = bit_of(ids[2], core_mask)
    return step % pairs * 2 + jnp.where(step < pairs, 1 - core, core)


def feed(ids, rows, grads, up, down, hidden, devices, kind, after=()):
    tokens, width = rows.shape
    chunk = 512
    own_up, own_down = width // devices, hidden // devices
    aside, down_blocks = width // chunk, chunk // own_down
    steps = hidden // chunk
    own_rows = own_down + own_up * (hidden // width) + own_up

    def kernel(
        ids_ref,
        rows_ref,
        grad_ref,
        up_ref,
        down_ref,
        branch_ref,
        back_ref,
        out_ref,
        across,
        down_rows,
        up_rows,
        sems,
    ):
        step = pl.program_id(0)
        slot = step % 2

        def copies(step, slot):
            first = own_down + step // aside * own_up
            return (
                pltpu.make_async_copy(
                    down_rows.at[slot],
                    out_ref.at[pl.ds(step * down_blocks, down_blocks), pl.ds(0, own_down)],
                    sems.at[0, slot],
                ),
                pltpu.make_async_copy(
                    up_rows.at[slot],
                    out_ref.at[
                        :,
                        pl.ds(pl.multiple_of(first, own_up), own_up),
                        pl.ds(pl.multiple_of(step % aside * chunk, chunk), chunk),
                    ],
                    sems.at[1, slot],
                ),
            )

        @pl.when(step == 0)
        def _():
            across[...] = rows_ref[...].T
            branch_ref[...] = jnp.zeros_like(branch_ref)
            back_ref[...] = jnp.zeros_like(back_ref)

        @pl.when(step >= 2)
        def _():
            for copy in copies(step - 2, slot):
                copy.wait()

        grads = grad_ref[...]
        up, down = up_ref[...].reshape(width, chunk), down_ref[...].reshape(chunk, width)
        upper = dot(rows_ref[...], up)
        hidden_grad = dot(grads, down.T)
        root = math.sqrt(2 / math.pi)
        square = upper * upper
        curve = jnp.tanh(upper * (root + root * 0.044715 * square))
        share = 0.5 + 0.5 * curve
        low = (upper * share).astype(LOW)
        slope = share + 0.5 * upper * (1.0 - curve * curve) * (root + 3 * root * 0.044715 * square)
        upper_grad = (hidden_grad * slope).astype(LOW)
        branch_ref[...] += dot(low, down)
        back_ref[...] += dot(upper_grad, up.T)
        down_grad = dot(low.T, grads).astype(kind)
        up_grad = dot(across[...], upper_grad).astype(kind)
        down_rows[slot] = down_grad.reshape(down_rows.shape[1:])
        up_rows[slot] = up_grad.reshape(up_rows.shape[1:])
        for copy in copies(step, slot):
            copy.start()

        @pl.when(step == steps - 1)
        def _():
            for copy in copies(step - 1, 1 - slot) + copies(step, slot):
                copy.wait()

    return call(
        kernel,
        "feed",
        ids,
        (steps,),
        [rows, grads, up[0], down[0]],
        [
            whole((tokens, width)),
            whole((tokens, width)),
            pl.BlockSpec(up[1], lambda step, ids: up[2](step)),
            pl.BlockSpec(down[1], lambda step, ids: down[2](step)),
        ],
        [
            wide_array(tokens, width),
            wide_array(tokens, width),
            jax.ShapeDtypeStruct((devices, own_rows, width), kind),
        ],
        [whole((tokens, width)), whole((tokens, width)), anywhere],
        [
            pltpu.VMEM((width, tokens), LOW),
            pltpu.VMEM((2, down_blocks, own_down, width), kind),
            pltpu.VMEM((2, devices, own_up, chunk), kind),
            pltpu.SemaphoreType.DMA((2, 2)),
        ],
        after,
        room=62,
        time=64,
    )


def middle_back(ids, middle, branch, back, projected, upstream, late, frames, after=()):
    rows = upstream[1].shape[0]

    def kernel(
        ids_ref,
        middle_ref,
        branch_ref,
        back_ref,
        projected_ref,
        g_own,
        g_other,
        late_ref,
        result_ref,
        middle_grad_ref,
        projected_grad_ref,
        pieces_ref,
    ):
        middle, branch = middle_ref[...], branch_ref[...]
        upstream = read_pair(ids_ref, g_own, g_other)
        result_ref[0] = (middle + piece(late_ref, 3, frames) * branch).astype(LOW)
        normed, inverse = norm_parts(middle)
        grad, shift_grad, scale_grad = norm_back(
            back_ref[...], normed, inverse, piece(late_ref, 2, frames)
        )
        grad = grad + upstream
        middle_grad_ref[...] = grad
        projected_grad_ref[...] = (piece(late_ref, 0, frames) * grad).astype(LOW)
        gate_grad = jnp.sum(grad * projected_ref[...], axis=0, keepdims=True)
        put_piece(pieces_ref, 0, frames, gate_grad)
        put_piece(pieces_ref, 1, frames, shift_grad)
        put_piece(pieces_ref, 2, frames, scale_grad)
        put_piece(pieces_ref, 3, frames, jnp.sum(upstream * branch, axis=0, keepdims=True))

    block = row_spec(rows, frames)
    return call(
        kernel,
        "middle_back",
        ids,
        (2, frames),
        [middle, branch, back, projected, *upstream, late],
        [block] * 4 + pair_specs(rows, frames) + [whole(late.shape)],
        [
            low_array(2, rows, D),
            wide_array(2 * rows, D),
            low_array(2 * rows, D),
            wide_array(2 * frames, 4 * D),
        ],
        [chunk_spec(rows, frames)] + [block] * 2 + [whole((2 * frames, 4 * D))],
        after=after,
        time=12,
    )


def put_half(step, pairs, value, sent_ref, kept_ref):
    @pl.when(step < pairs)
    def _():
        sent_ref[0] = value.astype(LOW)

    @pl.when(step >= pairs)
    def _():
        kept_ref[0] = value


def half_specs(pairs, rows, width, slot):
    return [
        pl.BlockSpec((1, rows, width), lambda i, ids: (jnp.minimum(i, pairs - 1), 0, slot)),
        pl.BlockSpec((1, rows, width), lambda i, ids: (jnp.maximum(i - pairs, 0), 0, slot)),
    ]


def hand_out(ids, weight, gradient, attended, into, members, steps, after=()):
    tokens, width = gradient.shape
    quarter = width // steps
    groups = members // steps
    group = width // members
    front = group - HEAD
    devices, own_rows, _ = into.shape
    own = width // devices

    def kernel(ids_ref, weight_ref, grad_ref, attended_ref, into_ref, *refs):
        gradient_ref, *out_refs = refs
        step = pl.program_id(0)
        grads = grad_ref[...]
        if weight_ref.shape[0] == 1:
            taken = weight_ref[0, pl.ds(pl.multiple_of(step * quarter, quarter), quarter), :]
        else:
            blocks = quarter // weight_ref.shape[1]
            taken = weight_ref[pl.ds(step * blocks, blocks)].reshape(quarter, width)
        block = contract(taken, grads, 1, 1).astype(LOW)
        for number in range(groups):
            at = number * group
            out_refs[0][number] = block[at + front : at + group]
            if front:
                out_refs[1][number] = block[at : at + front]
        value = dot(attended_ref[...], grads).astype(into.dtype)
        gradient_ref[...] = value.reshape(gradient_ref.shape)

    shapes = [(members, HEAD, tokens)] + [(members, front, tokens)] * (front > 0)
    return call(
        kernel,
        "hand_out",
        ids,
        (steps,),
        [weight[0], gradient, attended, into],
        [
            weight[1],
            whole(gradient.shape),
            pl.BlockSpec((quarter, tokens), lambda i, ids: (i, 0)),
            anywhere,
        ],
        [jax.ShapeDtypeStruct(into.shape, into.dtype)]
        + [low_array(*shape) for shape in shapes],
        [pl.BlockSpec((quarter // own, own, width), lambda i, ids: (i, own_rows // own - 1, 0))]
        + [pl.BlockSpec((groups,) + shape[1:], lambda i, ids: (i, 0, 0)) for shape in shapes],
        after=after,
        aliases={4: 0},
        time=9,
    )


def turn_back(operand, cosines, sines):
    half = HEAD // 2
    one, two = operand[:half], operand[half:]
    return jnp.concatenate([one * cosines + two * sines, two * cosines - one * sines], axis=0)


def attend_back(ids, parts, grads, head, wide, total, cosines, sines, after=()):
    members, _, _, tokens = parts.shape
    size, block = min(1024, tokens), min(512, tokens)
    length = members * tokens
    per, count = tokens // size, length // block
    back = HEAD ** (-0.5)

    def kernel(
        ids_ref,
        part_ref,
        grad_ref,
        wide_ref,
        total_ref,
        cos_ref,
        sin_ref,
        out_ref,
        key_rows,
        key_more,
        value_more,
        key_sum,
        value_sum,
    ):
        step = pl.program_id(0)

        @pl.when(step == 0)
        def _():
            for member in range(members):
                span = slice(member * tokens, (member + 1) * tokens)
                key_rows[span, :] = part_ref[member, 1].T
                key_more[:HEAD, span] = part_ref[member, 1]
                value_more[:HEAD, span] = part_ref[member, 2]
            key_more[HEAD:, :] = jnp.full((16, length), -1.0, LOW)
            value_more[HEAD:, :] = jnp.full((16, length), -1.0, LOW)
            key_sum[...] = jnp.zeros_like(key_sum)
            value_sum[...] = jnp.zeros_like(value_sum)

        member = step // per
        start = 0 if per == 1 else pl.multiple_of(step % per * size, size)
        queries_across = part_ref[member, 0, :, pl.ds(start, size)]
        grads_across = grad_ref[member, :, pl.ds(start, size)]
        delta = jnp.sum(grads_across.astype(WIDE) * wide_ref[...], axis=0, keepdims=True)

        def less(rows, amount):
            high = amount.astype(LOW)
            middle, low = two_lows(amount - high.astype(WIDE))
            spare = jnp.zeros((13, size), LOW)
            return jnp.concatenate([rows, high, middle, low, spare], axis=0).T

        queries = less(queries_across, total_ref[...] * (1 / SOFT))
        out_grads = less(grads_across, delta)
        query_grad = jnp.zeros((size, HEAD), WIDE)

        def pair(number):
            here = slice(number * block, (number + 1) * block)
            return dot(queries, key_more[:, here]), dot(out_grads, value_more[:, here])

        following = pair(0)
        for number in range(count):
            scores, prob_grad = following
            if number + 1 < count:
                following = pair(number + 1)
            here = slice(number * block, (number + 1) * block)
            probs = jnp.exp2(scores * SOFT)
            score_grad = (probs * prob_grad).astype(LOW)
            value_sum[:, here] += dot(grads_across, probs.astype(LOW))
            key_sum[:, here] += dot(queries_across, score_grad)
            query_grad += dot(score_grad, key_rows[here, :])

        where = pl.multiple_of(step * size, size)
        out_ref[member, 0, :, pl.ds(start, size)] = turn_back(
            query_grad.T * back, cos_ref[:, pl.ds(where, size)], sin_ref[:, pl.ds(where, size)]
        ).astype(LOW)

        @pl.when(step == length // size - 1)
        def _():
            for source in range(members):
                span = slice(source * tokens, (source + 1) * tokens)
                out_ref[source, 1] = turn_back(
                    key_sum[:, span] * back, cos_ref[:, span], sin_ref[:, span]
                ).astype(LOW)
                out_ref[source, 2] = value_sum[:, span].astype(LOW)

    return call(
        kernel,
        "attend_back",
        ids,
        (length // size,),
        [parts, grads, wide, total, cosines, sines],
        [
            whole(parts.shape),
            pl.BlockSpec((members, HEAD, tokens), lambda i, ids: (0, head, 0)),
            pl.BlockSpec((HEAD, size), lambda i, ids: (0, i)),
            pl.BlockSpec((1, size), lambda i, ids: (0, i)),
            whole(cosines.shape),
            whole(sines.shape),
        ],
        low_array(members, 3, HEAD, tokens),
        whole((members, 3, HEAD, tokens)),
        [
            pltpu.VMEM((length, HEAD), LOW),
            pltpu.VMEM((HEAD + 16, length), LOW),
            pltpu.VMEM((HEAD + 16, length), LOW),
            pltpu.VMEM((HEAD, length), WIDE),
            pltpu.VMEM((HEAD, length), WIDE),
        ],
        after,
        time=26,
    )


def joint_back(
    ids, parts, normed, weight, column, total, core_mask, pairs, into, slot, slots, after=()
):
    members, _, _, tokens = parts.shape
    group = members * HEAD
    width = 3 * group
    quarter = D // (2 * pairs)
    halves = (pairs, quarter, slots * width)
    before = [] if total is None else [total]
    held = [] if into is None else list(into)

    def kernel(ids_ref, part_ref, normed_ref, weight_ref, *refs):
        refs = list(refs)
        total_refs = [refs.pop(0) for _ in before]
        sent_ref, kept_ref, total_ref, across, lined = refs[len(held) :]
        step = pl.program_id(0)

        @pl.when(step == 0)
        def _():
            for member in range(members):
                for kind in range(3):
                    at = kind * group + member * HEAD
                    across[at : at + HEAD, :] = part_ref[member, kind]
            lined[...] = across[...].T

        rows = lined[...]
        put_half(step, pairs, dot(normed_ref[...], rows), sent_ref, kept_ref)
        added = contract(rows, weight_ref[...], 1, 1)
        total_ref[...] = total_refs[0][...] + added if total_refs else added

    def at(i, ids):
        return quarter_at(i, ids, core_mask, pairs)

    strip = pl.BlockSpec((tokens, quarter), lambda i, ids: (0, at(i, ids)))
    first = 4 + len(before)
    return call(
        kernel,
        "joint_back",
        ids,
        (2 * pairs,),
        [parts, normed, weight, *before, *held],
        [
            whole(parts.shape),
            pl.BlockSpec((quarter, tokens), lambda i, ids: (at(i, ids), 0)),
            pl.BlockSpec((quarter, width), lambda i, ids: (at(i, ids), column)),
        ]
        + [strip] * len(before)
        + [anywhere] * len(held),
        [low_array(*halves), wide_array(*halves), wide_array(tokens, D)],
        half_specs(pairs, quarter, width, slot) + [strip],
        [pltpu.VMEM((width, tokens), LOW), pltpu.VMEM((tokens, width), LOW)],
        after,
        aliases={first: 0, first + 1: 1} if held else {},
        time=9,
    )


def tokens_back(ids, gradient, tokens, middle_grad, early, frames, after=()):
    rows = tokens.shape[1]
    size = rows // frames

    def kernel(
        ids_ref, grad_ref, tokens_ref, middle_ref, early_ref, own_ref, other_ref, pieces_ref
    ):
        normed, inverse = norm_parts(tokens_ref[0].astype(WIDE))
        grad, shift_grad, scale_grad = norm_back(
            grad_ref[...], normed, inverse, piece(early_ref, 1, frames)
        )
        grad = grad + middle_ref[...]
        put_piece(pieces_ref, 0, frames, shift_grad)
        put_piece(pieces_ref, 1, frames, scale_grad)

        @pl.when(pl.program_id(0) == ids_ref[1])
        def _():
            own_ref[...] = grad

        @pl.when(pl.program_id(0) != ids_ref[1])
        def _():
            other_ref[...] = grad.astype(LOW)

    def chunk_at(number):
        def index(r, f, ids):
            mine = ids[1] if number == 0 else 1 - ids[1]
            return (jnp.where(r == mine, f, jnp.where(r < mine, 0, frames - 1)), 0)

        return index

    block = row_spec(rows, frames)
    return call(
        kernel,
        "tokens_back",
        ids,
        (2, frames),
        [gradient, tokens, middle_grad, early],
        [block, chunk_spec(rows, frames), block, whole(early.shape)],
        [wide_array(rows, D), low_array(rows, D), wide_array(2 * frames, 2 * D)],
        [
            pl.BlockSpec((size, D), chunk_at(0)),
            pl.BlockSpec((size, D), chunk_at(1)),
            whole((2 * frames, 2 * D)),
        ],
        after=after,
        time=9,
    )


def two_clips(ids, own, others, kind, frames, after=()):
    rows = others.shape[0]
    size = rows // frames
    if own.ndim == 3:
        own_spec = pl.BlockSpec((1, size, D), lambda r, f, ids: (ids[1], f, 0))
    else:
        own_spec = pl.BlockSpec((size, D), lambda r, f, ids: (f, 0))

    def kernel(ids_ref, own_ref, other_ref, out_ref):
        mine = pl.program_id(0) == ids_ref[1]

        @pl.when(mine)
        def _():
            out_ref[0] = own_ref[...].reshape(size, D).astype(kind)

        @pl.when(jnp.logical_not(mine))
        def _():
            out_ref[0] = other_ref[...].astype(kind)

    return call(
        kernel,
        "two_clips",
        ids,
        (2, frames),
        [own, others],
        [own_spec, pl.BlockSpec((size, D), lambda r, f, ids: (f, 0))],
        jax.ShapeDtypeStruct((2, rows, D), kind),
        chunk_spec(rows, frames),
        after=after,
        time=4,
    )


def modulation_back(ids, condition, pieces, after=()):
    count, width = pieces.shape
    own = condition.shape[1]
    size = 1024

    def kernel(ids_ref, condition_ref, pieces_ref, out_ref, sum_ref):
        pieces = pieces_ref[...]
        out_ref[...] = lax.dot_general(
            condition_ref[...].astype(WIDE).T,
            pieces,
            (((1,), (0,)), ((), ())),
            precision=highest,
            preferred_element_type=WIDE,
        )
        sum_ref[...] = jnp.sum(pieces, axis=0, keepdims=True)

    return call(
        kernel,
        "modulation_back",
        ids,
        (width // size,),
        [condition, pieces],
        [whole(condition.shape), pl.BlockSpec((count, size), lambda i, ids: (0, i))],
        [wide_array(own, width), wide_array(1, width)],
        [
            pl.BlockSpec((own, size), lambda i, ids: (0, i)),
            pl.BlockSpec((1, size), lambda i, ids: (0, i)),
        ],
        after=after,
        time=4,
    )


def join_and_add(ids, joins, adds, after=()):
    ins, outs = [], []
    for own, arrived, _ in joins:
        ins += [own, arrived]
        pre, post, width = own.shape
        outs.append(jax.ShapeDtypeStruct((pre, 2, post, width), own.dtype))
    for kept, arrived, final in adds:
        ins += [kept, arrived]
        rows, width = kept.shape
        outs += [wide_array(rows, width)] if final else [wide_array(rows // 2, width)] * 2

    def kernel(ids_ref, *refs):
        in_refs, out_refs = list(refs[: len(ins)]), list(refs[len(ins) :])
        for _, _, mask in joins:
            own, arrived, out = in_refs.pop(0), in_refs.pop(0), out_refs.pop(0)
            bit = bit_of(ids_ref[2], mask)
            for row in range(own.shape[0]):
                out[row, pl.ds(bit, 1)] = own[row][None]
                out[row, pl.ds(1 - bit, 1)] = arrived[row][None]
        for _, _, final in adds:
            kept, arrived = in_refs.pop(0), in_refs.pop(0)
            rows = kept.shape[0]
            if final:
                out_refs.pop(0)[...] = kept[...] + arrived[...]
            else:
                for start in (0, rows // 2):
                    span = slice(start, start + rows // 2)
                    out_refs.pop(0)[...] = kept[span] + arrived[span]

    return call(
        kernel,
        "join_and_add",
        ids,
        (1,),
        ins,
        [whole(value.shape) for value in ins],
        outs,
        [whole(out.shape) for out in outs],
        after=after,
        time=3,
    )


def stack_rows(ids, values, after=()):
    count, width = values[0].shape

    def kernel(ids_ref, *refs):
        for number, ref in enumerate(refs[:-1]):
            refs[-1][number * count : (number + 1) * count] = ref[...]

    return call(
        kernel,
        "stack_rows",
        ids,
        (1,),
        values,
        [whole(values[0].shape)] * len(values),
        wide_array(len(values) * count, width),
        whole((len(values) * count, width)),
        after=after,
        time=1,
    )


def pack(ids, down, up, output, after=()):
    count = down.shape[0] + up.shape[0] * (up.shape[1] // D) + output.shape[0]

    def kernel(ids_ref, down_ref, up_ref, output_ref, out_ref):
        at = 0
        pieces = [down_ref[...]]
        pieces += [up_ref[:, i * D : (i + 1) * D] for i in range(up.shape[1] // D)]
        for value in pieces + [output_ref[...]]:
            out_ref[at : at + value.shape[0]] = value.astype(LOW)
            at += value.shape[0]

    return call(
        kernel,
        "pack",
        ids,
        (1,),
        [down, up, output],
        [whole(down.shape), whole(up.shape), whole(output.shape)],
        low_array(count, D),
        whole((count, D)),
        after=after,
        time=3,
    )


def other_clip(ids, tokens, frames, after=()):
    rows = tokens.shape[1]
    size = rows // frames

    def kernel(ids_ref, in_ref, out_ref):
        out_ref[...] = in_ref[0]

    return call(
        kernel,
        "other_clip",
        ids,
        (frames,),
        [tokens],
        [pl.BlockSpec((1, size, D), lambda f, ids: (1 - ids[1], f, 0))],
        low_array(rows, D),
        pl.BlockSpec((size, D), lambda f, ids: (f, 0)),
        after=after,
    )


def settle(ids, rows, own_down, blocks, after=()):
    own = (rows.shape[0] - own_down) // (blocks + 1)

    def kernel(ids_ref, rows_ref, down_out, up_out, output_out):
        down_out[...] = rows_ref[:own_down].astype(WIDE)
        for number in range(blocks):
            at = own_down + number * own
            up_out[:, number * D : (number + 1) * D] = rows_ref[at : at + own].astype(WIDE)
        output_out[...] = rows_ref[own_down + blocks * own :].astype(WIDE)

    shapes = [(own_down, D), (own, blocks * D), (own, D)]
    return call(
        kernel,
        "settle",
        ids,
        (1,),
        [rows],
        [whole(rows.shape)],
        [wide_array(*shape) for shape in shapes],
        [whole(shape) for shape in shapes],
        after=after,
    )


def copy_of(ids, value, after=()):
    def kernel(ids_ref, in_ref, out_ref):
        out_ref[...] = in_ref[...]

    return call(
        kernel,
        "copy_of",
        ids,
        (1,),
        [value],
        [whole(value.shape)],
        jax.ShapeDtypeStruct(value.shape, value.dtype),
        whole(value.shape),
        after=after,
    )


def split_four(ids, kept, arrived, blocks_of, masks, after=()):
    rows = kept.shape[1:]
    ins = [kept, *arrived]
    if not masks:

        def add(ids_ref, *refs):
            *in_refs, out_ref = refs
            out_ref[...] = sum(ref[...].astype(WIDE) for ref in in_refs)

        return call(
            add,
            "split_four",
            ids,
            (1,),
            ins,
            [whole(kept.shape)] * len(ins),
            wide_array(*kept.shape),
            whole(kept.shape),
            after=after,
        )
    pre, mid, post = blocks_of
    high, low = masks

    def kernel(ids_ref, *refs):
        in_refs, out_refs = refs[: len(ins)], refs[len(ins) :]
        bits = bit_of(ids_ref[2], high), bit_of(ids_ref[2], low)
        for out, (across, aside) in zip(out_refs, ((0, 0), (1, 0), (0, 1), (1, 1))):
            first = 1 - bits[0] if across else bits[0]
            second = 1 - bits[1] if aside else bits[1]
            for one in range(pre):
                for two in range(post):
                    value = sum(ref[one, first, 0, second, two].astype(WIDE) for ref in in_refs)
                    out[one, 0, two] = value.astype(out.dtype)

    shape = (pre, 2, mid, 2, post) + rows
    lead = (pre, 2, 1, 2, post) + rows
    out_shape = (pre, mid, post) + rows
    zeros = (0,) * len(rows)
    return call(
        kernel,
        "split_four",
        ids,
        (mid,),
        [value.reshape(shape) for value in ins],
        [pl.BlockSpec(lead, lambda i, ids: (0, 0, i, 0, 0) + zeros)] * len(ins),
        [wide_array(*out_shape)] + [low_array(*out_shape)] * 3,
        [pl.BlockSpec((pre, 1, post) + rows, lambda i, ids: (0, i, 0) + zeros)] * 4,
        after=after,
        time=3,
    )


def halve_plain(rank, jobs):
    outs = []
    for kept, arrived, post, mask in jobs:
        value = kept.astype(WIDE) + arrived.astype(WIDE)
        if not post:
            outs.append(value)
            continue
        split = value.reshape((-1, 2, post) + value.shape[1:])
        for side in (1 - bit_of(rank, mask), bit_of(rank, mask)):
            taken = lax.dynamic_index_in_dim(split, side, 1, keepdims=False)
            outs.append(taken.reshape((-1,) + value.shape[1:]))
        outs[-2] = outs[-2].astype(LOW)
    return outs


def per_device(
    clip_size,
    seq_size,
    frames_in,
    noise_level,
    frame_time,
    cotangent,
    joint_weight,
    output_weight,
    up_weight,
    down_weight,
    modulation,
    modulation_bias,
    first_joint,
    first_output,
    first_up,
    first_down,
    first_modulation,
    first_bias,
    second_joint,
    second_output,
    second_up,
    second_down,
    second_modulation,
    second_bias,
):
    devices = clip_size * seq_size
    masters = (joint_weight, output_weight, up_weight, down_weight, modulation, modulation_bias)
    firsts = (first_joint, first_output, first_up, first_down, first_modulation, first_bias)
    seconds = (second_joint, second_output, second_up, second_down, second_modulation, second_bias)
    clip_id, seq_id = lax.axis_index("clip"), lax.axis_index("seq")
    rank = clip_id * seq_size + seq_id
    half = seq_size // 2
    side = seq_id // half
    members = half
    ids = jnp.stack([seq_id % half, side, rank]).astype(jnp.int32)
    head_count = HEADS // members
    group_ids = [[i * half + j for j in range(half)] for i in range(2)]
    last = []

    def swap_with(value, mask):
        return lax.ppermute(value, AXES, [(i, i ^ mask) for i in range(devices)])

    def pick(value, index):
        return lax.dynamic_index_in_dim(value, index, 0, keepdims=False)

    def run(kernel, *args, **options):
        result = kernel(ids, *args, after=tuple(last), **options)
        last[:] = jax.tree.leaves(result)[-1:]
        return result

    clip_masks = [seq_size << bit for bit in range(clip_size.bit_length() - 1)]
    seq_masks = [1 << bit for bit in range(seq_size.bit_length() - 1)]
    order = clip_masks + seq_masks
    core_mask = clip_masks[0]
    pairs = clip_size // 2

    local_rows = frames_in.shape[1]
    frames = max(1, local_rows // PATCHES)
    tokens_here = 2 * local_rows
    pair_ids = [[j, j + half] for j in range(half)]
    tokens = lax.all_to_all(frames_in, "seq", 0, 0, axis_index_groups=pair_ids)

    levels = noise_level.astype(WIDE)[None]
    for mask in clip_masks:
        levels = jnp.concatenate([levels, swap_with(levels, mask)], axis=0)
    all_levels = levels.reshape(-1)
    masks = [0]
    for mask in reversed(order):
        masks = masks + [other ^ mask for other in masks]
    own_width = modulation.shape[0]
    columns = rank * own_width + jnp.arange(own_width, dtype=jnp.int32)
    half_width = D // 2
    frequency = jnp.exp(-math.log(10000.0) * (columns % half_width).astype(WIDE) / half_width)

    def condition_of(targets):
        seq_of = targets % seq_size
        chunk = jnp.stack([seq_of % half, seq_of % half + half], axis=1)
        frame_of = chunk[:, :, None] * local_rows // PATCHES + jnp.arange(frames, dtype=jnp.int32)
        clip_of = (targets // seq_size ^ clip_id) * 2 + seq_of // half
        level_ids = (clip_of[:, None, None] * FRAMES + frame_of).reshape(-1)
        every = jnp.arange(all_levels.shape[0], dtype=jnp.int32)
        level_of = jnp.sum(jnp.where(level_ids[:, None] == every, all_levels, 0.0), axis=1)
        angles = level_of[:, None] * frequency
        wave = jnp.where(columns < half_width, jnp.cos(angles), jnp.sin(angles))
        return jax.nn.silu(wave).astype(LOW)

    condition = condition_of(rank ^ jnp.array(masks, jnp.int32))

    bias_width = modulation_bias.shape[0]
    bias_row = lax.dynamic_update_slice_in_dim(
        jnp.zeros((6 * D,), WIDE), modulation_bias.astype(LOW).astype(WIDE), rank * bias_width, 0
    )
    modulation_low = modulation.astype(LOW)

    class Terms:
        def __init__(self, condition, first, stop):
            terms = dot(condition, modulation_low[:, first:stop]) + bias_row[first:stop]
            middle = terms.shape[0] // 2
            self.kept, self.sent = terms[:middle], terms[middle:]
            self.masks = order[:]
            self.send()

        def send(self):
            self.arrived = swap_with(self.sent, self.masks.pop(0))

        def job(self):
            return (self.kept, self.arrived, not self.masks)

        def take(self, outs):
            self.kept = outs.pop(0)
            if self.masks:
                self.sent = outs.pop(0)
                self.send()

    rows = joint_weight.shape[0]
    joint_low = joint_weight.astype(LOW).reshape(rows, 3, members, head_count, HEAD)
    joint_low = jnp.transpose(joint_low, (0, 3, 1, 2, 4)).reshape(1, rows, 3 * D)
    far = seq_masks[:0:-1]
    routes = [
        far + [seq_masks[0]] + clip_masks[::-1],
        far + clip_masks[:0:-1] + [seq_masks[0], clip_masks[0]],
    ]
    joined = [joint_low]
    early_terms = None
    packed = run(pack, down_weight, up_weight, output_weight)
    packed = lax.all_gather(packed, AXES, axis=0, tiled=False)
    for stage in range(len(order) + 1):
        joins = []
        if stage < len(order):
            if stage == len(far):
                middle_column = joint_low.shape[2] // 2
                joined = [joined[0][..., :middle_column], joined[0][..., middle_column:]]
            for value, route in zip(joined, routes):
                mask, done = route[stage], route[:stage]
                pre = 2 ** sum(1 for other in done if other > mask)
                width = value.shape[-1]
                own = value.reshape(pre, -1, width)
                arrived = swap_with(value, mask).reshape(pre, -1, width)
                joins.append((own, arrived, mask))
        if stage == 1:
            early_terms = Terms(condition, 0, 2 * D)
        adds = [early_terms.job()] if stage else []
        if stage == 3:
            last.append(tokens)
        outs = list(run(join_and_add, joins, adds))
        if stage < len(order):
            joined = [outs.pop(0) for _ in joins]
            joined = [value.reshape(1, -1, value.shape[-1]) for value in joined]
        if stage:
            early_terms.take(outs)
    early = early_terms.kept
    joint_sides = [value[0] for value in joined]
    if head_count % 2:
        joint_sides = [jnp.concatenate(joint_sides, axis=1)]
    heads_aside = head_count // len(joint_sides)

    up_blocks = FF // D
    own_up = up_weight.shape[0]
    own_down = down_weight.shape[0]
    tiled = own_up % 16 == 0
    chunk_rows = 512
    up_first = own_down // own_up
    if tiled:
        chunks_aside = D // chunk_rows
        up_source = (
            packed,
            (devices, own_up, chunk_rows),
            lambda at: (0, up_first + at // chunks_aside, at % chunks_aside),
        )
        output_source = (
            packed,
            pl.BlockSpec((devices, own_up, D), lambda *at: (0, up_first + up_blocks, 0)),
        )
    else:
        upward = packed[:, own_down : own_down + own_up * up_blocks]
        upward = jnp.transpose(
            upward.reshape(devices, up_blocks, own_up, D), (0, 2, 1, 3)
        ).reshape(1, D, FF)
        up_source = (upward, (1, D, chunk_rows), lambda at: (0, 0, at))
        output_full = packed[:, own_down + own_up * up_blocks :].reshape(1, D, D)
        output_source = (output_full, whole((1, D, D)))
    down_source = (packed, (chunk_rows // own_down, own_down, D), lambda at: (at, 0, 0))

    member_seq = side * half + jnp.arange(members, dtype=jnp.int32)
    starts = jnp.stack([member_seq % half, member_seq % half + half], axis=1) * local_rows
    places = (starts[:, :, None] + jnp.arange(local_rows, dtype=jnp.int32)).reshape(-1)
    cosines, sines = rotary_tables(pick(frame_time, side), places)

    normed_across = run(norm_one, tokens, early, frames)

    def exchange(value):
        return lax.all_to_all(value, "seq", 0, 0, axis_index_groups=group_ids)

    late_terms = Terms(run(copy_of, condition), 2 * D, 6 * D)

    def late_step():
        if late_terms.arrived is not None:
            final = not late_terms.masks
            outs = list(run(join_and_add, [], [late_terms.job()]))
            late_terms.take(outs)
            if final:
                late_terms.arrived = None

    def project_head(head):
        weight, offset = joint_sides[head // heads_aside], head % heads_aside
        return exchange(
            run(project, normed_across, weight, cosines, sines, members, offset)
        )

    parts = {0: project_head(0)}
    late_step()
    wide, totals = {}, {}
    front = None
    front_heads = head_count - 1
    for head in range(head_count):
        if head + 1 < head_count:
            parts[head + 1] = project_head(head + 1)
        else:
            last.append(upstream[1] if head else tokens)
        late_step()
        if head == 0:
            late_step()
        if head < front_heads:
            front, wide[head], totals[head] = run(
                attend, parts[head], front, head, front_heads, False
            )
            if head + 1 == front_heads:
                front = exchange(front)
        else:
            back, wide[head], totals[head] = run(attend, parts[head], None, 0, 1, True)
        if head == 0:
            upstream = (cotangent, swap_with(run(other_clip, cotangent, frames), half))
    while late_terms.arrived is not None:
        late_step()
    late = late_terms.kept
    backs = [swap_with(back[i], i) if i else back[i] for i in range(members)]

    attended_across, projected, middle, normed_two_low, branch_grad = run(
        middle_part, front, backs, members, output_source, tokens, upstream, late, frames
    )
    branch, normed_two_grad, weight_grads = run(
        feed,
        normed_two_low,
        branch_grad,
        up_source,
        down_source,
        FF,
        devices,
        LOW if tiled else WIDE,
    )

    class Chain:
        def __init__(self, sent, kept):
            self.kept = kept
            self.masks = [clip_masks[1], *seq_masks]
            self.arrived = [swap_with(sent.astype(LOW), core_mask)]

        def step(self):
            if self.arrived is None:
                return
            if not tiled:
                mask = self.masks.pop(0) if self.masks else None
                post = 2 ** sum(1 for other in self.masks if other < mask) if mask else 0
                outs = halve_plain(rank, [(self.kept, self.arrived[0], post, mask)])
                self.arrived = [swap_with(outs[0], mask)] if mask else None
                self.kept = outs[-1]
                return
            rows = self.kept.shape[1:]
            if not self.masks:
                self.kept = run(split_four, self.kept, self.arrived, None, None)
                self.arrived = None
                return
            pair = sorted((self.masks.pop(0), self.masks.pop(0)), reverse=True)
            pre = 2 ** sum(1 for other in self.masks if other > pair[0])
            post = 2 ** sum(1 for other in self.masks if other < pair[1])
            mid = 2 ** len(self.masks) // pre // post
            kept, *sent = run(split_four, self.kept, self.arrived, (pre, mid, post), pair)
            self.kept = kept.reshape((-1,) + rows)
            ways = (*pair, pair[0] ^ pair[1])
            self.arrived = [
                swap_with(value.reshape((-1,) + rows), mask) for value, mask in zip(sent, ways)
            ]

    def owners(value):
        return value.reshape(devices // 2, -1, value.shape[2])

    result, middle_grad, projected_grad, late_rows = run(
        middle_back, middle, branch, normed_two_grad, projected, upstream, late, frames
    )
    weight_grads, *outer = run(
        hand_out, output_source, projected_grad, attended_across, weight_grads, members, 2 * pairs
    )
    weight_sums = lax.psum_scatter(
        weight_grads.astype(LOW), AXES, scatter_dimension=0, tiled=True
    )[0]
    outer_back = exchange(outer[0])
    last.append(outer_back)

    class Frames:
        def __init__(self, rows, groups):
            self.rows, self.groups = rows, list(groups)
            self.send()

        def send(self):
            self.arrived = None
            if self.groups:
                group = self.groups.pop(0)
                masks = group if len(group) == 1 else (*group, group[0] ^ group[1])
                self.arrived = [swap_with(self.rows, mask) for mask in masks]

        def step(self):
            if self.arrived is not None:
                self.rows = run(stack_rows, [self.rows, *self.arrived])
                self.send()

    def ranks_of(groups):
        masks = [0]
        for mask in [mask for group in groups for mask in group]:
            masks = masks + [other ^ mask for other in masks]
        return rank ^ jnp.array(masks, jnp.int32)

    late_frames = Frames(late_rows, [(mask,) for mask in reversed(order)])
    late_frames.step()

    def head_back(head):
        grads, at = (outer_front, head) if head < front_heads else (outer_back, 0)
        return run(
            attend_back, parts[head], grads, at, wide[head], totals[head], cosines, sines
        )

    heads = list(reversed(range(head_count)))
    early_heads = heads[:2] if head_count > 3 else []
    last_heads = heads[len(early_heads) :]

    def head_joint(head, group, total, into):
        weight, offset = joint_sides[head // heads_aside], head % heads_aside
        sent, kept, total = run(
            joint_back,
            joint_parts[head],
            normed_across,
            weight,
            offset,
            total,
            core_mask,
            pairs,
            into,
            group.index(head),
            len(group),
        )
        return total, (sent, kept)

    joint_parts = {}
    total = early_chain = None
    outer_front = exchange(outer[1]) if front_heads else None
    for number, head in enumerate(heads):
        joint_parts[head] = exchange(head_back(head))
        if number < 3:
            late_frames.step()
        if number == 0:
            other_rows = pick(result, 1 - side)
            if head_count > 1:
                other_rows = run(copy_of, other_rows)
            mixed_others = swap_with(other_rows, half)
        if number == 2 and early_heads:
            into = None
            for other in early_heads:
                total, into = head_joint(other, early_heads, total, into)
            early_chain = Chain(owners(into[0]), owners(into[1]))
        if number == 3:
            early_chain.step()
            mixed = run(two_clips, result, mixed_others, LOW, frames)
            late_frames.step()
        if number == 2 and early_heads:
            early_chain.step()
    into = None
    for head in last_heads:
        total, into = head_joint(head, last_heads, total, into)
        if head == last_heads[0] and early_heads:
            while early_chain.arrived is not None:
                early_chain.step()
    last_chain = Chain(owners(into[0]), owners(into[1]))
    own_rows, other_rows, early_rows = run(
        tokens_back, total, tokens, middle_grad, early, frames
    )
    groups = [tuple(far[i : i + 2]) for i in range(0, len(far), 2)]
    groups += [(core_mask,), (seq_masks[0], clip_masks[1])]
    early_frames = Frames(early_rows, groups)
    middle_row = local_rows // 2
    others = [swap_with(other_rows[:middle_row], half)]
    last_chain.step()
    early_frames.step()
    if head_count < 4:
        mixed = run(two_clips, result, mixed_others, LOW, frames)
    while late_frames.arrived is not None:
        late_frames.step()
    mod_late, sum_late = run(modulation_back, condition, late_frames.rows)
    down_sum, up_sum, output_sum = run(settle, weight_sums, own_down, up_blocks)
    early_frames.step()
    last_chain.step()
    others.append(swap_with(run(copy_of, other_rows[middle_row:]), half))
    while early_frames.arrived is not None:
        early_frames.step()
    mod_early, sum_early = run(
        modulation_back, condition_of(ranks_of(groups)), early_frames.rows
    )
    while last_chain.arrived is not None:
        last_chain.step()

    joint_heads = {}
    for chain, group in ((early_chain, early_heads), (last_chain, last_heads)):
        for slot, head in enumerate(group):
            width = 3 * D // head_count
            joint_heads[head] = chain.kept[0][:, slot * width : (slot + 1) * width]
    joint_sum = jnp.stack([joint_heads[head] for head in range(head_count)], axis=1)
    joint_sum = joint_sum.reshape(rows, head_count, 3, members, HEAD)
    joint_sum = jnp.transpose(joint_sum, (0, 2, 3, 1, 4)).reshape(rows, 3 * D)
    mod_sum = jnp.concatenate([mod_early, mod_late], axis=1)
    bias_sum = lax.dynamic_slice_in_dim(
        jnp.concatenate([sum_early[0], sum_late[0]]), rank * bias_width, bias_width, 0
    )

    summed = (joint_sum, output_sum, up_sum, down_sum, mod_sum, bias_sum)
    squares = sum(jnp.sum(shard * shard) for shard in summed).reshape(1, 1)
    for first, second in zip(order[::2], order[1::2]):
        squares = (squares + swap_with(squares, first)) + (
            swap_with(squares, second) + swap_with(squares, first ^ second)
        )
    if len(order) % 2:
        squares = squares + swap_with(squares, order[-1])
    last.append(squares)
    input_grad = run(two_clips, own_rows, jnp.concatenate(others), WIDE, frames)
    grad_norm = jnp.sqrt(squares[0, 0])
    factor = jnp.minimum(1.0, clip_limit / (grad_norm + 1e-06))
    step_rates = (
        D ** (-0.5),
        max(1, 2 * D // LENGTH) ** (-0.5),
        D ** (-0.5),
        FF ** (-0.5),
        D ** (-0.5),
        0.5,
    )
    clipped = [shard * factor for shard in summed]
    updates = [
        adam_update(clipped[slot], masters[slot], firsts[slot], seconds[slot], step_rates[slot])
        for slot in range(6)
    ]
    return (
        mixed,
        input_grad,
        *clipped,
        grad_norm,
        *(update[0] for update in updates),
        *(update[1] for update in updates),
        *(update[2] for update in updates),
        *(update[2].astype(LOW) for update in updates),
    )


def solution(mesh):
    tokens = P("clip", "seq", None)
    rows = P(AXES, None)
    weights = (rows, rows, rows, rows, rows, P(AXES))
    in_specs = (tokens, P("clip", None), P("clip", None), tokens) + weights * 3
    out_specs = (tokens, tokens) + weights + (P(),) + weights * 4
    return jax.shard_map(
        partial(per_device, mesh.shape["clip"], mesh.shape["seq"]),
        mesh=mesh,
        in_specs=in_specs,
        out_specs=out_specs,
        check_vma=False,
    )
```

```python
from functools import partial
import math

import jax
import jax.numpy as jnp
from jax import lax
from jax.experimental import pallas as pl
from jax.experimental.pallas import tpu as pltpu
from jax.sharding import PartitionSpec as P

D = 1024
HEADS = 16
HEAD = 64
FF = 4096
FRAMES = 16
GRID_W = 16
STEP = 10
PATCHES = 256
LENGTH = 4096

norm_epsilon = 1e-06
adam_epsilon = 1e-08
first_decay = 0.5
second_decay = 0.5
weight_decay = 0.1
clip_limit = 1.0
highest = lax.Precision.HIGHEST
AXES = ("clip", "seq")
LOW = jnp.bfloat16
WIDE = jnp.float32
SOFT = math.log2(math.e) * HEAD ** (-0.5)


def dot(left, right):
    return jnp.dot(left, right, preferred_element_type=WIDE)


def contract(left, right, left_dim, right_dim):
    return lax.dot_general(
        left, right, (((left_dim,), (right_dim,)), ((), ())), preferred_element_type=WIDE
    )


def normalize(operand):
    centered = operand - jnp.mean(operand, axis=-1, keepdims=True)
    variance = jnp.mean(centered * centered, axis=-1, keepdims=True)
    return centered * lax.rsqrt(variance + norm_epsilon)


def modulate(operand, shift_by, scale_by):
    return normalize(operand) * (1.0 + scale_by) + shift_by


def adam_update(gradient, master, moment_one, moment_two, step_rate):
    moment_one = first_decay * moment_one + (1.0 - first_decay) * gradient
    moment_two = second_decay * moment_two + (1.0 - second_decay) * gradient * gradient
    corrected_one = moment_one / (1.0 - first_decay**STEP)
    corrected_two = moment_two / (1.0 - second_decay**STEP)
    master = master - step_rate * (
        corrected_one / (jnp.sqrt(corrected_two) + adam_epsilon) + weight_decay * master
    )
    return (moment_one, moment_two, master)


def rotary_tables(times, places):
    frame_ids = places // PATCHES
    patch_row = (places % PATCHES // GRID_W).astype(WIDE)
    column = (places % GRID_W).astype(WIDE)
    matches = frame_ids[None, :] == jnp.arange(FRAMES, dtype=jnp.int32)[:, None]
    moment = jnp.sum(jnp.where(matches, times[:, None], 0), axis=0).astype(WIDE)
    time_pairs = HEAD // 8
    grid_pairs = 3 * HEAD // 16
    pair_ids = jnp.arange(HEAD // 2, dtype=jnp.int32)
    second = time_pairs + grid_pairs
    offset = jnp.where(pair_ids < time_pairs, 0, jnp.where(pair_ids < second, time_pairs, second))
    length = jnp.where(pair_ids < time_pairs, time_pairs, grid_pairs)
    frequency = jnp.exp(
        -math.log(10000.0) * (pair_ids - offset).astype(WIDE) / length.astype(WIDE)
    )
    ids = pair_ids[:, None]
    coordinate = jnp.where(
        ids < time_pairs, moment[None], jnp.where(ids < second, patch_row[None], column[None])
    )
    angles = coordinate * frequency[:, None]
    return jnp.cos(angles), jnp.sin(angles)


anywhere = pl.BlockSpec(memory_space=pl.ANY)


def whole(shape):
    return pl.BlockSpec(shape, lambda *ids: (0,) * len(shape))


def call(
    kernel,
    name,
    ids,
    grid,
    ins,
    in_specs,
    outs,
    out_specs,
    scratch=(),
    after=(),
    room=56,
    aliases=None,
    time=2,
):
    count, extra = 1 + len(ins), len(after)

    def body(*refs):
        kernel(*refs[:count], *refs[count + extra :])

    body.__name__ = name
    return pl.pallas_call(
        body,
        grid_spec=pltpu.PrefetchScalarGridSpec(
            num_scalar_prefetch=1,
            grid=grid,
            in_specs=list(in_specs) + [anywhere] * extra,
            out_specs=out_specs,
            scratch_shapes=list(scratch),
        ),
        out_shape=outs,
        input_output_aliases=aliases or {},
        compiler_params=pltpu.CompilerParams(vmem_limit_bytes=room << 20),
        cost_estimate=pl.CostEstimate(
            flops=int(time * 1.15e9), bytes_accessed=int(time * 3e6), transcendentals=0
        ),
        name=name,
    )(ids, *ins, *after)


def low_array(*shape):
    return jax.ShapeDtypeStruct(shape, LOW)


def wide_array(*shape):
    return jax.ShapeDtypeStruct(shape, WIDE)


def bit_of(rank, mask):
    return rank // mask % 2


def chunk_spec(rows, frames):
    return pl.BlockSpec((1, rows // frames, D), lambda r, f, ids: (r, f, 0))


def pair_specs(rows, frames):
    size = rows // frames
    return [
        pl.BlockSpec((1, size, D), lambda r, f, ids: (ids[1], f, 0)),
        pl.BlockSpec((size, D), lambda r, f, ids: (f, 0)),
    ]


def row_spec(rows, frames):
    return pl.BlockSpec((rows // frames, D), lambda r, f, ids: (r * frames + f, 0))


def column_spec(rows, frames):
    return pl.BlockSpec((D, rows // frames), lambda r, f, ids: (0, r * frames + f))


def read_pair(ids_ref, own_ref, other_ref):
    own = pl.program_id(0) == ids_ref[1]
    return jnp.where(own, own_ref[0].astype(WIDE), other_ref[...].astype(WIDE))


def piece(ref, number, frames):
    row = pl.program_id(0) * frames + pl.program_id(1)
    return ref[pl.ds(row, 1), number * D : (number + 1) * D]


def put_piece(ref, number, frames, value):
    row = pl.program_id(0) * frames + pl.program_id(1)
    ref[pl.ds(row, 1), number * D : (number + 1) * D] = value


def norm_parts(operand):
    centered = operand - jnp.mean(operand, axis=-1, keepdims=True)
    variance = jnp.mean(centered * centered, axis=-1, keepdims=True)
    inverse = lax.rsqrt(variance + norm_epsilon)
    return centered * inverse, inverse


def norm_back(gradient, normed, inverse, scale):
    shift_grad = jnp.sum(gradient, axis=0, keepdims=True)
    scale_grad = jnp.sum(gradient * normed, axis=0, keepdims=True)
    inner = gradient * (1.0 + scale)
    mean = jnp.mean(inner, axis=-1, keepdims=True)
    along = jnp.mean(inner * normed, axis=-1, keepdims=True)
    return (inner - mean - normed * along) * inverse, shift_grad, scale_grad


def norm_one(ids, tokens, early, frames, after=()):
    rows = tokens.shape[1]

    def kernel(ids_ref, tokens_ref, early_ref, out_ref):
        normed, _ = norm_parts(tokens_ref[0].astype(WIDE))
        shift, scale = piece(early_ref, 0, frames), piece(early_ref, 1, frames)
        out_ref[...] = (normed * (1.0 + scale) + shift).astype(LOW).T

    return call(
        kernel,
        "norm_one",
        ids,
        (2, frames),
        [tokens, early],
        [chunk_spec(rows, frames), whole(early.shape)],
        low_array(D, 2 * rows),
        column_spec(rows, frames),
        after=after,
        time=5,
    )


def project(ids, rows, weight, cosines, sines, members, first, after=()):
    width, tokens = rows.shape
    columns = members * HEAD
    half = HEAD // 2

    def kernel(ids_ref, rows_ref, weight_ref, cos_ref, sin_ref, out_ref):
        across = dot(weight_ref[...].T, rows_ref[...])
        kind = pl.program_id(0)

        @pl.when(kind == 2)
        def _():
            for member in range(members):
                out_ref[member, 0] = across[member * HEAD : (member + 1) * HEAD].astype(LOW)

        @pl.when(kind < 2)
        def _():
            cosines, sines = cos_ref[...], sin_ref[...]
            for member in range(members):
                one = across[member * HEAD : member * HEAD + half]
                two = across[member * HEAD + half : (member + 1) * HEAD]
                out_ref[member, 0, :half] = (one * cosines - two * sines).astype(LOW)
                out_ref[member, 0, half:] = (two * cosines + one * sines).astype(LOW)

    table = pl.BlockSpec((half, tokens), lambda t, ids: (0, ids[0]))
    return call(
        kernel,
        "project",
        ids,
        (3,),
        [rows, weight, cosines, sines],
        [
            whole((width, tokens)),
            pl.BlockSpec((width, columns), lambda t, ids: (0, first * 3 + t)),
            table,
            table,
        ],
        low_array(members, 3, HEAD, tokens),
        pl.BlockSpec((members, 1, HEAD, tokens), lambda t, ids: (0, t, 0, 0)),
        after=after,
        time=6,
    )


def two_lows(value):
    high = value.astype(LOW)
    return high, (value - high.astype(WIDE)).astype(LOW)


def attend(ids, parts, into, head, heads, relative, after=()):
    members, _, _, tokens = parts.shape
    size, block = min(1024, tokens), min(512, tokens)
    length = members * tokens
    per, count, inside = tokens // size, length // block, tokens // block
    before = [] if into is None else [into]

    def kernel(ids_ref, part_ref, *refs):
        low_ref, wide_ref, total_ref, key_rows, key_top = refs[len(before) :]
        step = pl.program_id(0)

        @pl.when(step == 0)
        def _():
            top = jnp.zeros((1, 1), WIDE)
            for member in range(members):
                keys = part_ref[member, 1].astype(WIDE) * SOFT
                top = jnp.maximum(top, jnp.max(jnp.sum(keys * keys, axis=0, keepdims=True)))
                high, low = two_lows(keys)
                key_rows[member * tokens : (member + 1) * tokens, :] = jnp.concatenate(
                    [high, low], axis=0
                ).T
            key_top[...] = top

        member = step // per
        start = 0 if per == 1 else pl.multiple_of(step % per * size, size)
        queries = part_ref[member, 0, :, pl.ds(start, size)]
        doubled = jnp.concatenate([queries, queries], axis=0)
        wide_queries = queries.astype(WIDE)
        query_top = jnp.max(jnp.sum(wide_queries * wide_queries, axis=0, keepdims=True))
        bounded = query_top * jnp.max(key_top[...]) <= 60.0**2

        def scores_of(number):
            return dot(key_rows[number * block : (number + 1) * block, :], doubled)

        def values_of(number):
            at = number % inside * block
            return part_ref[number // inside, 2, :, at : at + block]

        def finish(gathered, total, top):
            attended = gathered / total
            wide_ref[...] = attended
            total_ref[...] = top + jnp.log2(total)
            target = member ^ ids_ref[0] if relative else member
            low_ref[target, :, pl.ds(start, size)] = attended.astype(LOW)

        @pl.when(bounded)
        def _():
            gathered = jnp.zeros((HEAD, size), WIDE)
            total = jnp.zeros((1, size), WIDE)
            following = scores_of(0)
            for number in range(count):
                scores = following
                if number + 1 < count:
                    following = scores_of(number + 1)
                probs = jnp.exp2(scores)
                total = total + jnp.sum(probs, axis=0, keepdims=True)
                gathered = gathered + dot(values_of(number), probs.astype(LOW))
            finish(gathered, total, 0.0)

        @pl.when(jnp.logical_not(bounded))
        def _():
            gathered = jnp.zeros((HEAD, size), WIDE)
            top = jnp.full((1, size), -1e30, WIDE)
            total = jnp.zeros((1, size), WIDE)
            following = scores_of(0)
            for number in range(count):
                scores = following
                if number + 1 < count:
                    following = scores_of(number + 1)
                raised = jnp.maximum(top, jnp.max(scores, axis=0, keepdims=True))
                shrink = jnp.exp2(top - raised)
                probs = jnp.exp2(scores - raised)
                total = total * shrink + jnp.sum(probs, axis=0, keepdims=True)
                gathered = gathered * shrink + dot(values_of(number), probs.astype(LOW))
                top = raised
            finish(gathered, total, top)

    return call(
        kernel,
        "attend",
        ids,
        (length // size,),
        [parts, *before],
        [whole(parts.shape)] + [anywhere] * len(before),
        [
            low_array(members, heads * HEAD, tokens),
            wide_array(HEAD, length),
            wide_array(1, length),
        ],
        [
            pl.BlockSpec((members, HEAD, tokens), lambda i, ids: (0, head, 0)),
            pl.BlockSpec((HEAD, size), lambda i, ids: (0, i)),
            pl.BlockSpec((1, size), lambda i, ids: (0, i)),
        ],
        [pltpu.VMEM((length, 2 * HEAD), LOW), pltpu.VMEM((1, 1), WIDE)],
        after,
        aliases={2: 0} if before else {},
        time=18,
    )


def middle_part(ids, front, backs, members, weight, tokens, upstream, late, frames, after=()):
    rows = tokens.shape[1]
    size = rows // frames
    group = D // members
    parts = [front] * (front is not None) + list(backs)

    def kernel(ids_ref, *refs):
        part_refs = list(refs[: len(parts)])
        weight_ref, tokens_ref, g_own, g_other, late_ref = refs[len(parts) : len(parts) + 5]
        low_ref, projected_ref, middle_ref, normed_ref, grad_ref, across = refs[len(parts) + 5 :]
        if front is not None:
            front_ref = part_refs.pop(0)
            for member in range(members):
                across[member * group : member * group + group - HEAD, :] = front_ref[member]
        for member, ref in enumerate(part_refs):
            at = pl.multiple_of((ids_ref[0] ^ member) * group + group - HEAD, HEAD)
            across[pl.ds(at, HEAD), :] = ref[...]
        low = across[...]
        low_ref[...] = low
        projected = dot(low.T, weight_ref[...].reshape(D, D))
        projected_ref[...] = projected
        middle = tokens_ref[0].astype(WIDE) + piece(late_ref, 0, frames) * projected
        middle_ref[...] = middle
        normed, _ = norm_parts(middle)
        shift, scale = piece(late_ref, 1, frames), piece(late_ref, 2, frames)
        normed_ref[...] = (normed * (1.0 + scale) + shift).astype(LOW)
        upstream = read_pair(ids_ref, g_own, g_other)
        grad_ref[...] = (piece(late_ref, 3, frames) * upstream).astype(LOW)

    part_specs = [
        pl.BlockSpec(
            part.shape[:-1] + (size,),
            lambda r, f, ids, lead=part.ndim - 1: (0,) * lead + (r * frames + f,),
        )
        for part in parts
    ]
    return call(
        kernel,
        "middle_part",
        ids,
        (2, frames),
        [*parts, weight[0], tokens, *upstream, late],
        part_specs
        + [weight[1], chunk_spec(rows, frames)]
        + pair_specs(rows, frames)
        + [whole(late.shape)],
        [
            low_array(D, 2 * rows),
            wide_array(2 * rows, D),
            wide_array(2 * rows, D),
            low_array(2 * rows, D),
            low_array(2 * rows, D),
        ],
        [column_spec(rows, frames)] + [row_spec(rows, frames)] * 4,
        [pltpu.VMEM((D, size), LOW)],
        after,
        time=12,
    )


def quarter_at(step, ids, core_mask, pairs):
    core = bit_of(ids[2], core_mask)
    return step % pairs * 2 + jnp.where(step < pairs, 1 - core, core)


def feed(ids, rows, grads, up, down, hidden, devices, kind, after=()):
    tokens, width = rows.shape
    chunk = 512
    own_up, own_down = width // devices, hidden // devices
    aside, down_blocks = width // chunk, chunk // own_down
    steps = hidden // chunk
    own_rows = own_down + own_up * (hidden // width) + own_up

    def kernel(
        ids_ref,
        rows_ref,
        grad_ref,
        up_ref,
        down_ref,
        branch_ref,
        back_ref,
        out_ref,
        across,
        down_rows,
        up_rows,
        sems,
    ):
        step = pl.program_id(0)
        slot = step % 2

        def copies(step, slot):
            first = own_down + step // aside * own_up
            return (
                pltpu.make_async_copy(
                    down_rows.at[slot],
                    out_ref.at[pl.ds(step * down_blocks, down_blocks), pl.ds(0, own_down)],
                    sems.at[0, slot],
                ),
                pltpu.make_async_copy(
                    up_rows.at[slot],
                    out_ref.at[
                        :,
                        pl.ds(pl.multiple_of(first, own_up), own_up),
                        pl.ds(pl.multiple_of(step % aside * chunk, chunk), chunk),
                    ],
                    sems.at[1, slot],
                ),
            )

        @pl.when(step == 0)
        def _():
            across[...] = rows_ref[...].T
            branch_ref[...] = jnp.zeros_like(branch_ref)
            back_ref[...] = jnp.zeros_like(back_ref)

        @pl.when(step >= 2)
        def _():
            for copy in copies(step - 2, slot):
                copy.wait()

        grads = grad_ref[...]
        up, down = up_ref[...].reshape(width, chunk), down_ref[...].reshape(chunk, width)
        upper = dot(rows_ref[...], up)
        hidden_grad = dot(grads, down.T)
        root = math.sqrt(2 / math.pi)
        square = upper * upper
        curve = jnp.tanh(upper * (root + root * 0.044715 * square))
        share = 0.5 + 0.5 * curve
        low = (upper * share).astype(LOW)
        slope = share + 0.5 * upper * (1.0 - curve * curve) * (root + 3 * root * 0.044715 * square)
        upper_grad = (hidden_grad * slope).astype(LOW)
        branch_ref[...] += dot(low, down)
        back_ref[...] += dot(upper_grad, up.T)
        down_grad = dot(low.T, grads).astype(kind)
        up_grad = dot(across[...], upper_grad).astype(kind)
        down_rows[slot] = down_grad.reshape(down_rows.shape[1:])
        up_rows[slot] = up_grad.reshape(up_rows.shape[1:])
        for copy in copies(step, slot):
            copy.start()

        @pl.when(step == steps - 1)
        def _():
            for copy in copies(step - 1, 1 - slot) + copies(step, slot):
                copy.wait()

    return call(
        kernel,
        "feed",
        ids,
        (steps,),
        [rows, grads, up[0], down[0]],
        [
            whole((tokens, width)),
            whole((tokens, width)),
            pl.BlockSpec(up[1], lambda step, ids: up[2](step)),
            pl.BlockSpec(down[1], lambda step, ids: down[2](step)),
        ],
        [
            wide_array(tokens, width),
            wide_array(tokens, width),
            jax.ShapeDtypeStruct((devices, own_rows, width), kind),
        ],
        [whole((tokens, width)), whole((tokens, width)), anywhere],
        [
            pltpu.VMEM((width, tokens), LOW),
            pltpu.VMEM((2, down_blocks, own_down, width), kind),
            pltpu.VMEM((2, devices, own_up, chunk), kind),
            pltpu.SemaphoreType.DMA((2, 2)),
        ],
        after,
        room=62,
        time=64,
    )


def middle_back(ids, middle, branch, back, projected, upstream, late, frames, after=()):
    rows = upstream[1].shape[0]

    def kernel(
        ids_ref,
        middle_ref,
        branch_ref,
        back_ref,
        projected_ref,
        g_own,
        g_other,
        late_ref,
        result_ref,
        middle_grad_ref,
        projected_grad_ref,
        pieces_ref,
    ):
        middle, branch = middle_ref[...], branch_ref[...]
        upstream = read_pair(ids_ref, g_own, g_other)
        result_ref[0] = (middle + piece(late_ref, 3, frames) * branch).astype(LOW)
        normed, inverse = norm_parts(middle)
        grad, shift_grad, scale_grad = norm_back(
            back_ref[...], normed, inverse, piece(late_ref, 2, frames)
        )
        grad = grad + upstream
        middle_grad_ref[...] = grad
        projected_grad_ref[...] = (piece(late_ref, 0, frames) * grad).astype(LOW)
        gate_grad = jnp.sum(grad * projected_ref[...], axis=0, keepdims=True)
        put_piece(pieces_ref, 0, frames, gate_grad)
        put_piece(pieces_ref, 1, frames, shift_grad)
        put_piece(pieces_ref, 2, frames, scale_grad)
        put_piece(pieces_ref, 3, frames, jnp.sum(upstream * branch, axis=0, keepdims=True))

    block = row_spec(rows, frames)
    return call(
        kernel,
        "middle_back",
        ids,
        (2, frames),
        [middle, branch, back, projected, *upstream, late],
        [block] * 4 + pair_specs(rows, frames) + [whole(late.shape)],
        [
            low_array(2, rows, D),
            wide_array(2 * rows, D),
            low_array(2 * rows, D),
            wide_array(2 * frames, 4 * D),
        ],
        [chunk_spec(rows, frames)] + [block] * 2 + [whole((2 * frames, 4 * D))],
        after=after,
        time=12,
    )


def put_half(step, pairs, value, sent_ref, kept_ref):
    @pl.when(step < pairs)
    def _():
        sent_ref[0] = value.astype(LOW)

    @pl.when(step >= pairs)
    def _():
        kept_ref[0] = value


def half_specs(pairs, rows, width, slot):
    return [
        pl.BlockSpec((1, rows, width), lambda i, ids: (jnp.minimum(i, pairs - 1), 0, slot)),
        pl.BlockSpec((1, rows, width), lambda i, ids: (jnp.maximum(i - pairs, 0), 0, slot)),
    ]


def hand_out(ids, weight, gradient, attended, into, members, steps, after=()):
    tokens, width = gradient.shape
    quarter = width // steps
    groups = members // steps
    group = width // members
    front = group - HEAD
    devices, own_rows, _ = into.shape
    own = width // devices

    def kernel(ids_ref, weight_ref, grad_ref, attended_ref, into_ref, *refs):
        gradient_ref, *out_refs = refs
        step = pl.program_id(0)
        grads = grad_ref[...]
        if weight_ref.shape[0] == 1:
            taken = weight_ref[0, pl.ds(pl.multiple_of(step * quarter, quarter), quarter), :]
        else:
            blocks = quarter // weight_ref.shape[1]
            taken = weight_ref[pl.ds(step * blocks, blocks)].reshape(quarter, width)
        block = contract(taken, grads, 1, 1).astype(LOW)
        for number in range(groups):
            at = number * group
            out_refs[0][number] = block[at + front : at + group]
            if front:
                out_refs[1][number] = block[at : at + front]
        value = dot(attended_ref[...], grads).astype(into.dtype)
        gradient_ref[...] = value.reshape(gradient_ref.shape)

    shapes = [(members, HEAD, tokens)] + [(members, front, tokens)] * (front > 0)
    return call(
        kernel,
        "hand_out",
        ids,
        (steps,),
        [weight[0], gradient, attended, into],
        [
            weight[1],
            whole(gradient.shape),
            pl.BlockSpec((quarter, tokens), lambda i, ids: (i, 0)),
            anywhere,
        ],
        [jax.ShapeDtypeStruct(into.shape, into.dtype)]
        + [low_array(*shape) for shape in shapes],
        [pl.BlockSpec((quarter // own, own, width), lambda i, ids: (i, own_rows // own - 1, 0))]
        + [pl.BlockSpec((groups,) + shape[1:], lambda i, ids: (i, 0, 0)) for shape in shapes],
        after=after,
        aliases={4: 0},
        time=9,
    )


def turn_back(operand, cosines, sines):
    half = HEAD // 2
    one, two = operand[:half], operand[half:]
    return jnp.concatenate([one * cosines + two * sines, two * cosines - one * sines], axis=0)


def attend_back(ids, parts, grads, head, wide, total, cosines, sines, after=()):
    members, _, _, tokens = parts.shape
    size, block = min(1024, tokens), min(512, tokens)
    length = members * tokens
    per, count = tokens // size, length // block
    back = HEAD ** (-0.5)

    def kernel(
        ids_ref,
        part_ref,
        grad_ref,
        wide_ref,
        total_ref,
        cos_ref,
        sin_ref,
        out_ref,
        key_rows,
        key_more,
        value_more,
        key_sum,
        value_sum,
    ):
        step = pl.program_id(0)

        @pl.when(step == 0)
        def _():
            for member in range(members):
                span = slice(member * tokens, (member + 1) * tokens)
                key_rows[span, :] = part_ref[member, 1].T
                key_more[:HEAD, span] = part_ref[member, 1]
                value_more[:HEAD, span] = part_ref[member, 2]
            key_more[HEAD:, :] = jnp.full((16, length), -1.0, LOW)
            value_more[HEAD:, :] = jnp.full((16, length), -1.0, LOW)
            key_sum[...] = jnp.zeros_like(key_sum)
            value_sum[...] = jnp.zeros_like(value_sum)

        member = step // per
        start = 0 if per == 1 else pl.multiple_of(step % per * size, size)
        queries_across = part_ref[member, 0, :, pl.ds(start, size)]
        grads_across = grad_ref[member, :, pl.ds(start, size)]
        delta = jnp.sum(grads_across.astype(WIDE) * wide_ref[...], axis=0, keepdims=True)

        def less(rows, amount):
            high = amount.astype(LOW)
            middle, low = two_lows(amount - high.astype(WIDE))
            spare = jnp.zeros((13, size), LOW)
            return jnp.concatenate([rows, high, middle, low, spare], axis=0).T

        queries = less(queries_across, total_ref[...] * (1 / SOFT))
        out_grads = less(grads_across, delta)
        query_grad = jnp.zeros((size, HEAD), WIDE)

        def pair(number):
            here = slice(number * block, (number + 1) * block)
            return dot(queries, key_more[:, here]), dot(out_grads, value_more[:, here])

        following = pair(0)
        for number in range(count):
            scores, prob_grad = following
            if number + 1 < count:
                following = pair(number + 1)
            here = slice(number * block, (number + 1) * block)
            probs = jnp.exp2(scores * SOFT)
            score_grad = (probs * prob_grad).astype(LOW)
            value_sum[:, here] += dot(grads_across, probs.astype(LOW))
            key_sum[:, here] += dot(queries_across, score_grad)
            query_grad += dot(score_grad, key_rows[here, :])

        where = pl.multiple_of(step * size, size)
        out_ref[member, 0, :, pl.ds(start, size)] = turn_back(
            query_grad.T * back, cos_ref[:, pl.ds(where, size)], sin_ref[:, pl.ds(where, size)]
        ).astype(LOW)

        @pl.when(step == length // size - 1)
        def _():
            for source in range(members):
                span = slice(source * tokens, (source + 1) * tokens)
                out_ref[source, 1] = turn_back(
                    key_sum[:, span] * back, cos_ref[:, span], sin_ref[:, span]
                ).astype(LOW)
                out_ref[source, 2] = value_sum[:, span].astype(LOW)

    return call(
        kernel,
        "attend_back",
        ids,
        (length // size,),
        [parts, grads, wide, total, cosines, sines],
        [
            whole(parts.shape),
            pl.BlockSpec((members, HEAD, tokens), lambda i, ids: (0, head, 0)),
            pl.BlockSpec((HEAD, size), lambda i, ids: (0, i)),
            pl.BlockSpec((1, size), lambda i, ids: (0, i)),
            whole(cosines.shape),
            whole(sines.shape),
        ],
        low_array(members, 3, HEAD, tokens),
        whole((members, 3, HEAD, tokens)),
        [
            pltpu.VMEM((length, HEAD), LOW),
            pltpu.VMEM((HEAD + 16, length), LOW),
            pltpu.VMEM((HEAD + 16, length), LOW),
            pltpu.VMEM((HEAD, length), WIDE),
            pltpu.VMEM((HEAD, length), WIDE),
        ],
        after,
        time=26,
    )


def joint_back(
    ids, parts, normed, weight, column, total, core_mask, pairs, into, slot, slots, after=()
):
    members, _, _, tokens = parts.shape
    group = members * HEAD
    width = 3 * group
    quarter = D // (2 * pairs)
    halves = (pairs, quarter, slots * width)
    before = [] if total is None else [total]
    held = [] if into is None else list(into)

    def kernel(ids_ref, part_ref, normed_ref, weight_ref, *refs):
        refs = list(refs)
        total_refs = [refs.pop(0) for _ in before]
        sent_ref, kept_ref, total_ref, across, lined = refs[len(held) :]
        step = pl.program_id(0)

        @pl.when(step == 0)
        def _():
            for member in range(members):
                for kind in range(3):
                    at = kind * group + member * HEAD
                    across[at : at + HEAD, :] = part_ref[member, kind]
            lined[...] = across[...].T

        rows = lined[...]
        put_half(step, pairs, dot(normed_ref[...], rows), sent_ref, kept_ref)
        added = contract(rows, weight_ref[...], 1, 1)
        total_ref[...] = total_refs[0][...] + added if total_refs else added

    def at(i, ids):
        return quarter_at(i, ids, core_mask, pairs)

    strip = pl.BlockSpec((tokens, quarter), lambda i, ids: (0, at(i, ids)))
    first = 4 + len(before)
    return call(
        kernel,
        "joint_back",
        ids,
        (2 * pairs,),
        [parts, normed, weight, *before, *held],
        [
            whole(parts.shape),
            pl.BlockSpec((quarter, tokens), lambda i, ids: (at(i, ids), 0)),
            pl.BlockSpec((quarter, width), lambda i, ids: (at(i, ids), column)),
        ]
        + [strip] * len(before)
        + [anywhere] * len(held),
        [low_array(*halves), wide_array(*halves), wide_array(tokens, D)],
        half_specs(pairs, quarter, width, slot) + [strip],
        [pltpu.VMEM((width, tokens), LOW), pltpu.VMEM((tokens, width), LOW)],
        after,
        aliases={first: 0, first + 1: 1} if held else {},
        time=9,
    )


def tokens_back(ids, gradient, tokens, middle_grad, early, frames, after=()):
    rows = tokens.shape[1]
    size = rows // frames

    def kernel(
        ids_ref, grad_ref, tokens_ref, middle_ref, early_ref, own_ref, other_ref, pieces_ref
    ):
        normed, inverse = norm_parts(tokens_ref[0].astype(WIDE))
        grad, shift_grad, scale_grad = norm_back(
            grad_ref[...], normed, inverse, piece(early_ref, 1, frames)
        )
        grad = grad + middle_ref[...]
        put_piece(pieces_ref, 0, frames, shift_grad)
        put_piece(pieces_ref, 1, frames, scale_grad)

        @pl.when(pl.program_id(0) == ids_ref[1])
        def _():
            own_ref[...] = grad

        @pl.when(pl.program_id(0) != ids_ref[1])
        def _():
            other_ref[...] = grad.astype(LOW)

    def chunk_at(number):
        def index(r, f, ids):
            mine = ids[1] if number == 0 else 1 - ids[1]
            return (jnp.where(r == mine, f, jnp.where(r < mine, 0, frames - 1)), 0)

        return index

    block = row_spec(rows, frames)
    return call(
        kernel,
        "tokens_back",
        ids,
        (2, frames),
        [gradient, tokens, middle_grad, early],
        [block, chunk_spec(rows, frames), block, whole(early.shape)],
        [wide_array(rows, D), low_array(rows, D), wide_array(2 * frames, 2 * D)],
        [
            pl.BlockSpec((size, D), chunk_at(0)),
            pl.BlockSpec((size, D), chunk_at(1)),
            whole((2 * frames, 2 * D)),
        ],
        after=after,
        time=9,
    )


def two_clips(ids, own, others, kind, after=()):
    size = others[0].shape[0] // (2 // len(others))
    if own.ndim == 3:
        own_spec = pl.BlockSpec((1, size, D), lambda r, f, ids: (ids[1], f, 0))
    else:
        own_spec = pl.BlockSpec((size, D), lambda r, f, ids: (f, 0))
    if len(others) == 1:
        other_specs = [pl.BlockSpec((size, D), lambda r, f, ids: (f, 0))]
    else:
        other_specs = [whole((size, D))] * 2

    def kernel(ids_ref, own_ref, *refs):
        *other_refs, out_ref = refs
        mine = pl.program_id(0) == ids_ref[1]

        @pl.when(mine)
        def _():
            out_ref[0] = own_ref[...].reshape(size, D).astype(kind)

        for number, ref in enumerate(other_refs):
            here = pl.program_id(1) == number if len(other_refs) == 2 else True

            @pl.when(jnp.logical_and(jnp.logical_not(mine), here))
            def _(ref=ref):
                out_ref[0] = ref[...].astype(kind)

    return call(
        kernel,
        "two_clips",
        ids,
        (2, 2),
        [own, *others],
        [own_spec, *other_specs],
        jax.ShapeDtypeStruct((2, 2 * size, D), kind),
        pl.BlockSpec((1, size, D), lambda r, f, ids: (r, f, 0)),
        after=after,
        time=4,
    )


def modulation_back(ids, condition, pieces, after=()):
    count, width = pieces.shape
    own = condition.shape[1]
    size = 1024

    def kernel(ids_ref, condition_ref, pieces_ref, out_ref, sum_ref):
        pieces = pieces_ref[...]
        out_ref[...] = lax.dot_general(
            condition_ref[...].astype(WIDE).T,
            pieces,
            (((1,), (0,)), ((), ())),
            precision=highest,
            preferred_element_type=WIDE,
        )
        sum_ref[...] = jnp.sum(pieces, axis=0, keepdims=True)

    return call(
        kernel,
        "modulation_back",
        ids,
        (width // size,),
        [condition, pieces],
        [whole(condition.shape), pl.BlockSpec((count, size), lambda i, ids: (0, i))],
        [wide_array(own, width), wide_array(1, width)],
        [
            pl.BlockSpec((own, size), lambda i, ids: (0, i)),
            pl.BlockSpec((1, size), lambda i, ids: (0, i)),
        ],
        after=after,
        time=4,
    )


def join_and_add(ids, joins, adds, after=()):
    ins, outs = [], []
    for own, arrived, _ in joins:
        ins += [own, arrived]
        pre, post, width = own.shape
        outs.append(jax.ShapeDtypeStruct((pre, 2, post, width), own.dtype))
    for kept, arrived, final in adds:
        ins += [kept, arrived]
        rows, width = kept.shape
        outs += [wide_array(rows, width)] if final else [wide_array(rows // 2, width)] * 2

    def kernel(ids_ref, *refs):
        in_refs, out_refs = list(refs[: len(ins)]), list(refs[len(ins) :])
        for _, _, mask in joins:
            own, arrived, out = in_refs.pop(0), in_refs.pop(0), out_refs.pop(0)
            bit = bit_of(ids_ref[2], mask)
            for row in range(own.shape[0]):
                out[row, pl.ds(bit, 1)] = own[row][None]
                out[row, pl.ds(1 - bit, 1)] = arrived[row][None]
        for _, _, final in adds:
            kept, arrived = in_refs.pop(0), in_refs.pop(0)
            rows = kept.shape[0]
            if final:
                out_refs.pop(0)[...] = kept[...] + arrived[...]
            else:
                for start in (0, rows // 2):
                    span = slice(start, start + rows // 2)
                    out_refs.pop(0)[...] = kept[span] + arrived[span]

    return call(
        kernel,
        "join_and_add",
        ids,
        (1,),
        ins,
        [whole(value.shape) for value in ins],
        outs,
        [whole(out.shape) for out in outs],
        after=after,
        time=3,
    )


def stack_rows(ids, values, after=()):
    count, width = values[0].shape

    def kernel(ids_ref, *refs):
        for number, ref in enumerate(refs[:-1]):
            refs[-1][number * count : (number + 1) * count] = ref[...]

    return call(
        kernel,
        "stack_rows",
        ids,
        (1,),
        values,
        [whole(values[0].shape)] * len(values),
        wide_array(len(values) * count, width),
        whole((len(values) * count, width)),
        after=after,
        time=1,
    )


def fold(ids, kept, arrived, count, after=()):
    rows, width = kept.shape
    part = rows // count

    def kernel(ids_ref, *refs):
        in_refs, out_refs = refs[: 1 + len(arrived)], refs[1 + len(arrived) :]
        for number, out in enumerate(out_refs):
            span = slice(number * part, (number + 1) * part)
            out[...] = sum(ref[span] for ref in in_refs)

    return call(
        kernel,
        "fold",
        ids,
        (1,),
        [kept, *arrived],
        [whole(kept.shape)] * (1 + len(arrived)),
        [wide_array(part, width)] * count,
        [whole((part, width))] * count,
        after=after,
        time=3,
    )


def pack(ids, down, up, output, after=()):
    count = down.shape[0] + up.shape[0] * (up.shape[1] // D) + output.shape[0]

    def kernel(ids_ref, down_ref, up_ref, output_ref, out_ref):
        at = 0
        pieces = [down_ref[...]]
        pieces += [up_ref[:, i * D : (i + 1) * D] for i in range(up.shape[1] // D)]
        for value in pieces + [output_ref[...]]:
            out_ref[at : at + value.shape[0]] = value.astype(LOW)
            at += value.shape[0]

    return call(
        kernel,
        "pack",
        ids,
        (1,),
        [down, up, output],
        [whole(down.shape), whole(up.shape), whole(output.shape)],
        low_array(count, D),
        whole((count, D)),
        after=after,
        time=3,
    )


def other_clip(ids, tokens, frames, after=()):
    rows = tokens.shape[1]
    size = rows // frames

    def kernel(ids_ref, in_ref, out_ref):
        out_ref[...] = in_ref[0]

    return call(
        kernel,
        "other_clip",
        ids,
        (frames,),
        [tokens],
        [pl.BlockSpec((1, size, D), lambda f, ids: (1 - ids[1], f, 0))],
        low_array(rows, D),
        pl.BlockSpec((size, D), lambda f, ids: (f, 0)),
        after=after,
    )


def settle(ids, rows, own_down, blocks, after=()):
    own = (rows.shape[0] - own_down) // (blocks + 1)

    def kernel(ids_ref, rows_ref, down_out, up_out, output_out):
        down_out[...] = rows_ref[:own_down].astype(WIDE)
        for number in range(blocks):
            at = own_down + number * own
            up_out[:, number * D : (number + 1) * D] = rows_ref[at : at + own].astype(WIDE)
        output_out[...] = rows_ref[own_down + blocks * own :].astype(WIDE)

    shapes = [(own_down, D), (own, blocks * D), (own, D)]
    return call(
        kernel,
        "settle",
        ids,
        (1,),
        [rows],
        [whole(rows.shape)],
        [wide_array(*shape) for shape in shapes],
        [whole(shape) for shape in shapes],
        after=after,
    )


def copy_of(ids, value, after=()):
    def kernel(ids_ref, in_ref, out_ref):
        out_ref[...] = in_ref[...]

    return call(
        kernel,
        "copy_of",
        ids,
        (1,),
        [value],
        [whole(value.shape)],
        jax.ShapeDtypeStruct(value.shape, value.dtype),
        whole(value.shape),
        after=after,
    )


def split_four(ids, kept, arrived, blocks_of, masks, after=()):
    rows = kept.shape[1:]
    ins = [kept, *arrived]
    if not masks:

        def add(ids_ref, *refs):
            *in_refs, out_ref = refs
            out_ref[...] = sum(ref[...].astype(WIDE) for ref in in_refs)

        return call(
            add,
            "split_four",
            ids,
            (1,),
            ins,
            [whole(kept.shape)] * len(ins),
            wide_array(*kept.shape),
            whole(kept.shape),
            after=after,
        )
    pre, mid, post = blocks_of
    high, low = masks

    def kernel(ids_ref, *refs):
        in_refs, out_refs = refs[: len(ins)], refs[len(ins) :]
        bits = bit_of(ids_ref[2], high), bit_of(ids_ref[2], low)
        for out, (across, aside) in zip(out_refs, ((0, 0), (1, 0), (0, 1), (1, 1))):
            first = 1 - bits[0] if across else bits[0]
            second = 1 - bits[1] if aside else bits[1]
            for one in range(pre):
                for two in range(post):
                    value = sum(ref[one, first, 0, second, two].astype(WIDE) for ref in in_refs)
                    out[one, 0, two] = value.astype(out.dtype)

    shape = (pre, 2, mid, 2, post) + rows
    lead = (pre, 2, 1, 2, post) + rows
    out_shape = (pre, mid, post) + rows
    zeros = (0,) * len(rows)
    return call(
        kernel,
        "split_four",
        ids,
        (mid,),
        [value.reshape(shape) for value in ins],
        [pl.BlockSpec(lead, lambda i, ids: (0, 0, i, 0, 0) + zeros)] * len(ins),
        [wide_array(*out_shape)] + [low_array(*out_shape)] * 3,
        [pl.BlockSpec((pre, 1, post) + rows, lambda i, ids: (0, i, 0) + zeros)] * 4,
        after=after,
        time=3,
    )


def halve_plain(rank, jobs):
    outs = []
    for kept, arrived, post, mask in jobs:
        value = kept.astype(WIDE) + arrived.astype(WIDE)
        if not post:
            outs.append(value)
            continue
        split = value.reshape((-1, 2, post) + value.shape[1:])
        for side in (1 - bit_of(rank, mask), bit_of(rank, mask)):
            taken = lax.dynamic_index_in_dim(split, side, 1, keepdims=False)
            outs.append(taken.reshape((-1,) + value.shape[1:]))
        outs[-2] = outs[-2].astype(LOW)
    return outs


def per_device(
    clip_size,
    seq_size,
    frames_in,
    noise_level,
    frame_time,
    cotangent,
    joint_weight,
    output_weight,
    up_weight,
    down_weight,
    modulation,
    modulation_bias,
    first_joint,
    first_output,
    first_up,
    first_down,
    first_modulation,
    first_bias,
    second_joint,
    second_output,
    second_up,
    second_down,
    second_modulation,
    second_bias,
):
    devices = clip_size * seq_size
    masters = (joint_weight, output_weight, up_weight, down_weight, modulation, modulation_bias)
    firsts = (first_joint, first_output, first_up, first_down, first_modulation, first_bias)
    seconds = (second_joint, second_output, second_up, second_down, second_modulation, second_bias)
    clip_id, seq_id = lax.axis_index("clip"), lax.axis_index("seq")
    rank = clip_id * seq_size + seq_id
    half = seq_size // 2
    side = seq_id // half
    members = half
    ids = jnp.stack([seq_id % half, side, rank]).astype(jnp.int32)
    head_count = HEADS // members
    group_ids = [[i * half + j for j in range(half)] for i in range(2)]
    last = []

    def swap_with(value, mask):
        return lax.ppermute(value, AXES, [(i, i ^ mask) for i in range(devices)])

    def pick(value, index):
        return lax.dynamic_index_in_dim(value, index, 0, keepdims=False)

    def run(kernel, *args, **options):
        result = kernel(ids, *args, after=tuple(last), **options)
        last[:] = jax.tree.leaves(result)[-1:]
        return result

    clip_masks = [seq_size << bit for bit in range(clip_size.bit_length() - 1)]
    seq_masks = [1 << bit for bit in range(seq_size.bit_length() - 1)]
    order = clip_masks + seq_masks
    core_mask = clip_masks[0]
    pairs = clip_size // 2

    local_rows = frames_in.shape[1]
    frames = max(1, local_rows // PATCHES)
    tokens_here = 2 * local_rows
    pair_ids = [[j, j + half] for j in range(half)]
    tokens = lax.all_to_all(frames_in, "seq", 0, 0, axis_index_groups=pair_ids)

    levels = noise_level.astype(WIDE)[None]
    for mask in clip_masks:
        levels = jnp.concatenate([levels, swap_with(levels, mask)], axis=0)
    all_levels = levels.reshape(-1)
    masks = [0]
    for mask in reversed(order):
        masks = masks + [other ^ mask for other in masks]
    own_width = modulation.shape[0]
    columns = rank * own_width + jnp.arange(own_width, dtype=jnp.int32)
    half_width = D // 2
    frequency = jnp.exp(-math.log(10000.0) * (columns % half_width).astype(WIDE) / half_width)

    def condition_of(targets):
        seq_of = targets % seq_size
        chunk = jnp.stack([seq_of % half, seq_of % half + half], axis=1)
        frame_of = chunk[:, :, None] * local_rows // PATCHES + jnp.arange(frames, dtype=jnp.int32)
        clip_of = (targets // seq_size ^ clip_id) * 2 + seq_of // half
        level_ids = (clip_of[:, None, None] * FRAMES + frame_of).reshape(-1)
        every = jnp.arange(all_levels.shape[0], dtype=jnp.int32)
        level_of = jnp.sum(jnp.where(level_ids[:, None] == every, all_levels, 0.0), axis=1)
        angles = level_of[:, None] * frequency
        wave = jnp.where(columns < half_width, jnp.cos(angles), jnp.sin(angles))
        return jax.nn.silu(wave).astype(LOW)

    condition = condition_of(rank ^ jnp.array(masks, jnp.int32))

    bias_width = modulation_bias.shape[0]
    bias_row = lax.dynamic_update_slice_in_dim(
        jnp.zeros((6 * D,), WIDE), modulation_bias.astype(LOW).astype(WIDE), rank * bias_width, 0
    )
    modulation_low = modulation.astype(LOW)

    class Terms:
        def __init__(self, condition, first, stop):
            terms = dot(condition, modulation_low[:, first:stop]) + bias_row[first:stop]
            middle = terms.shape[0] // 2
            self.kept, self.sent = terms[:middle], terms[middle:]
            self.masks = order[:]
            self.send()

        def send(self):
            self.arrived = swap_with(self.sent, self.masks.pop(0))

        def job(self):
            return (self.kept, self.arrived, not self.masks)

        def take(self, outs):
            self.kept = outs.pop(0)
            if self.masks:
                self.sent = outs.pop(0)
                self.send()

    rows = joint_weight.shape[0]
    joint_low = joint_weight.astype(LOW).reshape(rows, 3, members, head_count, HEAD)
    joint_low = jnp.transpose(joint_low, (0, 3, 1, 2, 4)).reshape(1, rows, 3 * D)
    far = seq_masks[:0:-1]
    routes = [
        far + [seq_masks[0]] + clip_masks[::-1],
        far + clip_masks[:0:-1] + [seq_masks[0], clip_masks[0]],
    ]
    joined = [joint_low]
    early_terms = None
    packed = run(pack, down_weight, up_weight, output_weight)
    packed = lax.all_gather(packed, AXES, axis=0, tiled=False)
    for stage in range(len(order) + 1):
        joins = []
        if stage < len(order):
            if stage == len(far):
                middle_column = joint_low.shape[2] // 2
                joined = [joined[0][..., :middle_column], joined[0][..., middle_column:]]
            for value, route in zip(joined, routes):
                mask, done = route[stage], route[:stage]
                pre = 2 ** sum(1 for other in done if other > mask)
                width = value.shape[-1]
                own = value.reshape(pre, -1, width)
                arrived = swap_with(value, mask).reshape(pre, -1, width)
                joins.append((own, arrived, mask))
        if stage == 1:
            early_terms = Terms(condition, 0, 2 * D)
        adds = [early_terms.job()] if stage else []
        if stage == 3:
            last.append(tokens)
        outs = list(run(join_and_add, joins, adds))
        if stage < len(order):
            joined = [outs.pop(0) for _ in joins]
            joined = [value.reshape(1, -1, value.shape[-1]) for value in joined]
        if stage:
            early_terms.take(outs)
    early = early_terms.kept
    joint_sides = [value[0] for value in joined]
    if head_count % 2:
        joint_sides = [jnp.concatenate(joint_sides, axis=1)]
    heads_aside = head_count // len(joint_sides)

    up_blocks = FF // D
    own_up = up_weight.shape[0]
    own_down = down_weight.shape[0]
    tiled = own_up % 16 == 0
    chunk_rows = 512
    up_first = own_down // own_up
    if tiled:
        chunks_aside = D // chunk_rows
        up_source = (
            packed,
            (devices, own_up, chunk_rows),
            lambda at: (0, up_first + at // chunks_aside, at % chunks_aside),
        )
        output_source = (
            packed,
            pl.BlockSpec((devices, own_up, D), lambda *at: (0, up_first + up_blocks, 0)),
        )
    else:
        upward = packed[:, own_down : own_down + own_up * up_blocks]
        upward = jnp.transpose(
            upward.reshape(devices, up_blocks, own_up, D), (0, 2, 1, 3)
        ).reshape(1, D, FF)
        up_source = (upward, (1, D, chunk_rows), lambda at: (0, 0, at))
        output_full = packed[:, own_down + own_up * up_blocks :].reshape(1, D, D)
        output_source = (output_full, whole((1, D, D)))
    down_source = (packed, (chunk_rows // own_down, own_down, D), lambda at: (at, 0, 0))

    member_seq = side * half + jnp.arange(members, dtype=jnp.int32)
    starts = jnp.stack([member_seq % half, member_seq % half + half], axis=1) * local_rows
    places = (starts[:, :, None] + jnp.arange(local_rows, dtype=jnp.int32)).reshape(-1)
    cosines, sines = rotary_tables(pick(frame_time, side), places)

    normed_across = run(norm_one, tokens, early, frames)

    def exchange(value):
        return lax.all_to_all(value, "seq", 0, 0, axis_index_groups=group_ids)

    class Late:
        def __init__(self, condition):
            terms = dot(condition, modulation_low[:, 2 * D :]) + bias_row[2 * D :]
            self.groups = [(core_mask,)]
            self.groups += [tuple(order[i : i + 2]) for i in range(1, len(order), 2)]
            count = terms.shape[0] // 2
            self.take([terms[:count], terms[count:]])

        def take(self, parts):
            self.kept, *sent = parts
            self.arrived = None
            if sent:
                group = self.groups.pop(0)
                ways = group if len(group) == 1 else (group[1], group[0], group[0] ^ group[1])
                self.arrived = [swap_with(value, mask) for value, mask in zip(sent, ways)]

        def step(self):
            if self.arrived is not None:
                count = 2 ** len(self.groups[0]) if self.groups else 1
                self.take(run(fold, self.kept, self.arrived, count))

    def project_head(head):
        weight, offset = joint_sides[head // heads_aside], head % heads_aside
        return exchange(
            run(project, normed_across, weight, cosines, sines, members, offset)
        )

    parts = {0: project_head(0)}
    late_terms = Late(run(copy_of, condition))
    wide, totals = {}, {}
    front = None
    front_heads = head_count - 1
    for head in range(head_count):
        if head + 1 < head_count:
            parts[head + 1] = project_head(head + 1)
        if head == 0:
            late_terms.step()
        if head < front_heads:
            front, wide[head], totals[head] = run(
                attend, parts[head], front, head, front_heads, False
            )
            if head + 1 == front_heads:
                front = exchange(front)
        else:
            back, wide[head], totals[head] = run(attend, parts[head], None, 0, 1, True)
        if head < 2:
            late_terms.step()
        if head == 0:
            sent = run(other_clip, cotangent, frames)
            cut = local_rows // 2
            pieces = [swap_with(sent[:cut], half), swap_with(sent[cut:], half)]
        if 0 < head < 3:
            last.append(pieces[head - 1])
    while late_terms.arrived is not None:
        late_terms.step()
    late = late_terms.kept
    upstream = (cotangent, jnp.concatenate(pieces))
    backs = [swap_with(back[i], i) if i else back[i] for i in range(members)]

    attended_across, projected, middle, normed_two_low, branch_grad = run(
        middle_part, front, backs, members, output_source, tokens, upstream, late, frames
    )
    branch, normed_two_grad, weight_grads = run(
        feed,
        normed_two_low,
        branch_grad,
        up_source,
        down_source,
        FF,
        devices,
        LOW if tiled else WIDE,
    )

    class Chain:
        def __init__(self, sent, kept):
            self.kept = kept
            self.masks = [clip_masks[1], *seq_masks]
            self.arrived = [swap_with(sent.astype(LOW), core_mask)]

        def step(self):
            if self.arrived is None:
                return
            if not tiled:
                mask = self.masks.pop(0) if self.masks else None
                post = 2 ** sum(1 for other in self.masks if other < mask) if mask else 0
                outs = halve_plain(rank, [(self.kept, self.arrived[0], post, mask)])
                self.arrived = [swap_with(outs[0], mask)] if mask else None
                self.kept = outs[-1]
                return
            rows = self.kept.shape[1:]
            if not self.masks:
                self.kept = run(split_four, self.kept, self.arrived, None, None)
                self.arrived = None
                return
            pair = sorted((self.masks.pop(0), self.masks.pop(0)), reverse=True)
            pre = 2 ** sum(1 for other in self.masks if other > pair[0])
            post = 2 ** sum(1 for other in self.masks if other < pair[1])
            mid = 2 ** len(self.masks) // pre // post
            kept, *sent = run(split_four, self.kept, self.arrived, (pre, mid, post), pair)
            self.kept = kept.reshape((-1,) + rows)
            ways = (*pair, pair[0] ^ pair[1])
            self.arrived = [
                swap_with(value.reshape((-1,) + rows), mask) for value, mask in zip(sent, ways)
            ]

    def owners(value):
        return value.reshape(devices // 2, -1, value.shape[2])

    result, middle_grad, projected_grad, late_rows = run(
        middle_back, middle, branch, normed_two_grad, projected, upstream, late, frames
    )
    weight_grads, *outer = run(
        hand_out, output_source, projected_grad, attended_across, weight_grads, members, 2 * pairs
    )
    weight_sums = lax.psum_scatter(
        weight_grads.astype(LOW), AXES, scatter_dimension=0, tiled=True
    )[0]
    outer_back = exchange(outer[0])
    last.append(outer_back)

    class Frames:
        def __init__(self, rows, groups):
            self.rows, self.groups = rows, list(groups)
            self.send()

        def send(self):
            self.arrived = None
            if self.groups:
                group = self.groups.pop(0)
                masks = group if len(group) == 1 else (*group, group[0] ^ group[1])
                self.arrived = [swap_with(self.rows, mask) for mask in masks]

        def step(self):
            if self.arrived is not None:
                self.rows = run(stack_rows, [self.rows, *self.arrived])
                self.send()

    def ranks_of(groups):
        masks = [0]
        for mask in [mask for group in groups for mask in group]:
            masks = masks + [other ^ mask for other in masks]
        return rank ^ jnp.array(masks, jnp.int32)

    late_frames = Frames(late_rows, [(mask,) for mask in reversed(order)])
    late_frames.step()

    def head_back(head):
        grads, at = (outer_front, head) if head < front_heads else (outer_back, 0)
        return run(
            attend_back, parts[head], grads, at, wide[head], totals[head], cosines, sines
        )

    heads = list(reversed(range(head_count)))
    early_heads = heads[:2] if head_count > 3 else []
    last_heads = heads[len(early_heads) :]

    def head_joint(head, group, total, into):
        weight, offset = joint_sides[head // heads_aside], head % heads_aside
        sent, kept, total = run(
            joint_back,
            joint_parts[head],
            normed_across,
            weight,
            offset,
            total,
            core_mask,
            pairs,
            into,
            group.index(head),
            len(group),
        )
        return total, (sent, kept)

    joint_parts = {}
    total = early_chain = None
    outer_front = exchange(outer[1]) if front_heads else None
    for number, head in enumerate(heads):
        joint_parts[head] = exchange(head_back(head))
        if number < 3:
            late_frames.step()
        if number == 0:
            other_rows = pick(result, 1 - side)
            if head_count > 1:
                other_rows = run(copy_of, other_rows)
            mixed_others = swap_with(other_rows, half)
        if number == 2 and early_heads:
            into = None
            for other in early_heads:
                total, into = head_joint(other, early_heads, total, into)
            early_chain = Chain(owners(into[0]), owners(into[1]))
        if number == 3:
            early_chain.step()
            mixed = run(two_clips, result, [mixed_others], LOW)
            late_frames.step()
        if number == 2 and early_heads:
            early_chain.step()
    into = None
    for head in last_heads:
        total, into = head_joint(head, last_heads, total, into)
        if head == last_heads[0] and early_heads:
            while early_chain.arrived is not None:
                early_chain.step()
    last_chain = Chain(owners(into[0]), owners(into[1]))
    own_rows, other_rows, early_rows = run(
        tokens_back, total, tokens, middle_grad, early, frames
    )
    groups = [tuple(far[i : i + 2]) for i in range(0, len(far), 2)]
    groups += [(core_mask,), (seq_masks[0], clip_masks[1])]
    early_frames = Frames(early_rows, groups)
    middle_row = local_rows // 2
    others = [swap_with(other_rows[:middle_row], half)]
    last_chain.step()
    early_frames.step()
    if head_count < 4:
        mixed = run(two_clips, result, [mixed_others], LOW)
    while late_frames.arrived is not None:
        late_frames.step()
    mod_late, sum_late = run(modulation_back, condition, late_frames.rows)
    down_sum, up_sum, output_sum = run(settle, weight_sums, own_down, up_blocks)
    early_frames.step()
    last_chain.step()
    others.append(swap_with(run(copy_of, other_rows[middle_row:]), half))
    while early_frames.arrived is not None:
        early_frames.step()
    mod_early, sum_early = run(
        modulation_back, condition_of(ranks_of(groups)), early_frames.rows
    )
    while last_chain.arrived is not None:
        last_chain.step()

    joint_heads = {}
    for chain, group in ((early_chain, early_heads), (last_chain, last_heads)):
        for slot, head in enumerate(group):
            width = 3 * D // head_count
            joint_heads[head] = chain.kept[0][:, slot * width : (slot + 1) * width]
    joint_sum = jnp.stack([joint_heads[head] for head in range(head_count)], axis=1)
    joint_sum = joint_sum.reshape(rows, head_count, 3, members, HEAD)
    joint_sum = jnp.transpose(joint_sum, (0, 2, 3, 1, 4)).reshape(rows, 3 * D)
    mod_sum = jnp.concatenate([mod_early, mod_late], axis=1)
    bias_sum = lax.dynamic_slice_in_dim(
        jnp.concatenate([sum_early[0], sum_late[0]]), rank * bias_width, bias_width, 0
    )

    summed = (joint_sum, output_sum, up_sum, down_sum, mod_sum, bias_sum)
    squares = sum(jnp.sum(shard * shard) for shard in summed).reshape(1, 1)
    for first, second in zip(order[::2], order[1::2]):
        squares = (squares + swap_with(squares, first)) + (
            swap_with(squares, second) + swap_with(squares, first ^ second)
        )
        last.append(squares)
    input_grad = run(two_clips, own_rows, others, WIDE)
    if len(order) % 2:
        squares = squares + swap_with(squares, order[-1])
    grad_norm = jnp.sqrt(squares[0, 0])
    factor = jnp.minimum(1.0, clip_limit / (grad_norm + 1e-06))
    step_rates = (
        D ** (-0.5),
        max(1, 2 * D // LENGTH) ** (-0.5),
        D ** (-0.5),
        FF ** (-0.5),
        D ** (-0.5),
        0.5,
    )
    clipped = [shard * factor for shard in summed]
    updates = [
        adam_update(clipped[slot], masters[slot], firsts[slot], seconds[slot], step_rates[slot])
        for slot in range(6)
    ]
    return (
        mixed,
        input_grad,
        *clipped,
        grad_norm,
        *(update[0] for update in updates),
        *(update[1] for update in updates),
        *(update[2] for update in updates),
        *(update[2].astype(LOW) for update in updates),
    )


def solution(mesh):
    tokens = P("clip", "seq", None)
    rows = P(AXES, None)
    weights = (rows, rows, rows, rows, rows, P(AXES))
    in_specs = (tokens, P("clip", None), P("clip", None), tokens) + weights * 3
    out_specs = (tokens, tokens) + weights + (P(),) + weights * 4
    return jax.shard_map(
        partial(per_device, mesh.shape["clip"], mesh.shape["seq"]),
        mesh=mesh,
        in_specs=in_specs,
        out_specs=out_specs,
        check_vma=False,
    )
```

```python
from functools import partial
import math

import jax
import jax.numpy as jnp
from jax import lax
from jax.experimental import pallas as pl
from jax.experimental.pallas import tpu as pltpu
from jax.sharding import PartitionSpec as P

D = 1024
HEADS = 16
HEAD = 64
FF = 4096
FRAMES = 16
GRID_W = 16
STEP = 10
PATCHES = 256
LENGTH = 4096

norm_epsilon = 1e-06
adam_epsilon = 1e-08
first_decay = 0.5
second_decay = 0.5
weight_decay = 0.1
clip_limit = 1.0
highest = lax.Precision.HIGHEST
AXES = ("clip", "seq")
LOW = jnp.bfloat16
WIDE = jnp.float32
SOFT = math.log2(math.e) * HEAD ** (-0.5)


def dot(left, right):
    return jnp.dot(left, right, preferred_element_type=WIDE)


def contract(left, right, left_dim, right_dim):
    return lax.dot_general(
        left, right, (((left_dim,), (right_dim,)), ((), ())), preferred_element_type=WIDE
    )


def normalize(operand):
    centered = operand - jnp.mean(operand, axis=-1, keepdims=True)
    variance = jnp.mean(centered * centered, axis=-1, keepdims=True)
    return centered * lax.rsqrt(variance + norm_epsilon)


def modulate(operand, shift_by, scale_by):
    return normalize(operand) * (1.0 + scale_by) + shift_by


def adam_update(gradient, master, moment_one, moment_two, step_rate):
    moment_one = first_decay * moment_one + (1.0 - first_decay) * gradient
    moment_two = second_decay * moment_two + (1.0 - second_decay) * gradient * gradient
    corrected_one = moment_one / (1.0 - first_decay**STEP)
    corrected_two = moment_two / (1.0 - second_decay**STEP)
    master = master - step_rate * (
        corrected_one / (jnp.sqrt(corrected_two) + adam_epsilon) + weight_decay * master
    )
    return (moment_one, moment_two, master)


def rotary_tables(times, places):
    frame_ids = places // PATCHES
    patch_row = (places % PATCHES // GRID_W).astype(WIDE)
    column = (places % GRID_W).astype(WIDE)
    matches = frame_ids[None, :] == jnp.arange(FRAMES, dtype=jnp.int32)[:, None]
    moment = jnp.sum(jnp.where(matches, times[:, None], 0), axis=0).astype(WIDE)
    time_pairs = HEAD // 8
    grid_pairs = 3 * HEAD // 16
    pair_ids = jnp.arange(HEAD // 2, dtype=jnp.int32)
    second = time_pairs + grid_pairs
    offset = jnp.where(pair_ids < time_pairs, 0, jnp.where(pair_ids < second, time_pairs, second))
    length = jnp.where(pair_ids < time_pairs, time_pairs, grid_pairs)
    frequency = jnp.exp(
        -math.log(10000.0) * (pair_ids - offset).astype(WIDE) / length.astype(WIDE)
    )
    ids = pair_ids[:, None]
    coordinate = jnp.where(
        ids < time_pairs, moment[None], jnp.where(ids < second, patch_row[None], column[None])
    )
    angles = coordinate * frequency[:, None]
    return jnp.cos(angles), jnp.sin(angles)


anywhere = pl.BlockSpec(memory_space=pl.ANY)


def whole(shape):
    return pl.BlockSpec(shape, lambda *ids: (0,) * len(shape))


def call(
    kernel,
    name,
    ids,
    grid,
    ins,
    in_specs,
    outs,
    out_specs,
    scratch=(),
    after=(),
    room=56,
    aliases=None,
    time=2,
):
    count, extra = 1 + len(ins), len(after)

    def body(*refs):
        kernel(*refs[:count], *refs[count + extra :])

    body.__name__ = name
    return pl.pallas_call(
        body,
        grid_spec=pltpu.PrefetchScalarGridSpec(
            num_scalar_prefetch=1,
            grid=grid,
            in_specs=list(in_specs) + [anywhere] * extra,
            out_specs=out_specs,
            scratch_shapes=list(scratch),
        ),
        out_shape=outs,
        input_output_aliases=aliases or {},
        compiler_params=pltpu.CompilerParams(vmem_limit_bytes=room << 20),
        cost_estimate=pl.CostEstimate(
            flops=int(time * 1.15e9), bytes_accessed=int(time * 3e6), transcendentals=0
        ),
        name=name,
    )(ids, *ins, *after)


def low_array(*shape):
    return jax.ShapeDtypeStruct(shape, LOW)


def wide_array(*shape):
    return jax.ShapeDtypeStruct(shape, WIDE)


def bit_of(rank, mask):
    return rank // mask % 2


def chunk_spec(rows, frames):
    return pl.BlockSpec((1, rows // frames, D), lambda r, f, ids: (r, f, 0))


def pair_specs(rows, frames):
    size = rows // frames
    return [
        pl.BlockSpec((1, size, D), lambda r, f, ids: (ids[1], f, 0)),
        pl.BlockSpec((size, D), lambda r, f, ids: (f, 0)),
    ]


def row_spec(rows, frames):
    return pl.BlockSpec((rows // frames, D), lambda r, f, ids: (r * frames + f, 0))


def column_spec(rows, frames):
    return pl.BlockSpec((D, rows // frames), lambda r, f, ids: (0, r * frames + f))


def read_pair(ids_ref, own_ref, other_ref):
    own = pl.program_id(0) == ids_ref[1]
    return jnp.where(own, own_ref[0].astype(WIDE), other_ref[...].astype(WIDE))


def piece(ref, number, frames):
    row = pl.program_id(0) * frames + pl.program_id(1)
    return ref[pl.ds(row, 1), number * D : (number + 1) * D]


def put_piece(ref, number, frames, value):
    row = pl.program_id(0) * frames + pl.program_id(1)
    ref[pl.ds(row, 1), number * D : (number + 1) * D] = value


def norm_parts(operand):
    centered = operand - jnp.mean(operand, axis=-1, keepdims=True)
    variance = jnp.mean(centered * centered, axis=-1, keepdims=True)
    inverse = lax.rsqrt(variance + norm_epsilon)
    return centered * inverse, inverse


def norm_back(gradient, normed, inverse, scale):
    shift_grad = jnp.sum(gradient, axis=0, keepdims=True)
    scale_grad = jnp.sum(gradient * normed, axis=0, keepdims=True)
    inner = gradient * (1.0 + scale)
    mean = jnp.mean(inner, axis=-1, keepdims=True)
    along = jnp.mean(inner * normed, axis=-1, keepdims=True)
    return (inner - mean - normed * along) * inverse, shift_grad, scale_grad


def norm_one(ids, tokens, early, frames, after=()):
    rows = tokens.shape[1]

    def kernel(ids_ref, tokens_ref, early_ref, out_ref):
        normed, _ = norm_parts(tokens_ref[0].astype(WIDE))
        shift, scale = piece(early_ref, 0, frames), piece(early_ref, 1, frames)
        out_ref[...] = (normed * (1.0 + scale) + shift).astype(LOW).T

    return call(
        kernel,
        "norm_one",
        ids,
        (2, frames),
        [tokens, early],
        [chunk_spec(rows, frames), whole(early.shape)],
        low_array(D, 2 * rows),
        column_spec(rows, frames),
        after=after,
        time=5,
    )


def project(ids, rows, weight, cosines, sines, members, first, after=()):
    width, tokens = rows.shape
    columns = members * HEAD
    half = HEAD // 2

    def kernel(ids_ref, rows_ref, weight_ref, cos_ref, sin_ref, out_ref):
        across = dot(weight_ref[...].T, rows_ref[...])
        kind = pl.program_id(0)

        @pl.when(kind == 2)
        def _():
            for member in range(members):
                out_ref[member, 0] = across[member * HEAD : (member + 1) * HEAD].astype(LOW)

        @pl.when(kind < 2)
        def _():
            cosines, sines = cos_ref[...], sin_ref[...]
            for member in range(members):
                one = across[member * HEAD : member * HEAD + half]
                two = across[member * HEAD + half : (member + 1) * HEAD]
                out_ref[member, 0, :half] = (one * cosines - two * sines).astype(LOW)
                out_ref[member, 0, half:] = (two * cosines + one * sines).astype(LOW)

    table = pl.BlockSpec((half, tokens), lambda t, ids: (0, ids[0]))
    return call(
        kernel,
        "project",
        ids,
        (3,),
        [rows, weight, cosines, sines],
        [
            whole((width, tokens)),
            pl.BlockSpec((width, columns), lambda t, ids: (0, first * 3 + t)),
            table,
            table,
        ],
        low_array(members, 3, HEAD, tokens),
        pl.BlockSpec((members, 1, HEAD, tokens), lambda t, ids: (0, t, 0, 0)),
        after=after,
        time=6,
    )


def two_lows(value):
    high = value.astype(LOW)
    return high, (value - high.astype(WIDE)).astype(LOW)


def attend(ids, parts, into, head, heads, relative, after=()):
    members, _, _, tokens = parts.shape
    size, block = min(1024, tokens), min(512, tokens)
    length = members * tokens
    per, count, inside = tokens // size, length // block, tokens // block
    before = [] if into is None else [into]

    def kernel(ids_ref, part_ref, *refs):
        low_ref, wide_ref, total_ref, key_rows, key_top = refs[len(before) :]
        step = pl.program_id(0)

        @pl.when(step == 0)
        def _():
            top = jnp.zeros((1, 1), WIDE)
            for member in range(members):
                keys = part_ref[member, 1].astype(WIDE) * SOFT
                top = jnp.maximum(top, jnp.max(jnp.sum(keys * keys, axis=0, keepdims=True)))
                high, low = two_lows(keys)
                key_rows[member * tokens : (member + 1) * tokens, :] = jnp.concatenate(
                    [high, low], axis=0
                ).T
            key_top[...] = top

        member = step // per
        start = 0 if per == 1 else pl.multiple_of(step % per * size, size)
        queries = part_ref[member, 0, :, pl.ds(start, size)]
        doubled = jnp.concatenate([queries, queries], axis=0)
        wide_queries = queries.astype(WIDE)
        query_top = jnp.max(jnp.sum(wide_queries * wide_queries, axis=0, keepdims=True))
        bounded = query_top * jnp.max(key_top[...]) <= 60.0**2

        def scores_of(number):
            return dot(key_rows[number * block : (number + 1) * block, :], doubled)

        def values_of(number):
            at = number % inside * block
            return part_ref[number // inside, 2, :, at : at + block]

        def finish(gathered, total, top):
            attended = gathered / total
            wide_ref[...] = attended
            total_ref[...] = top + jnp.log2(total)
            target = member ^ ids_ref[0] if relative else member
            low_ref[target, :, pl.ds(start, size)] = attended.astype(LOW)

        @pl.when(bounded)
        def _():
            gathered = jnp.zeros((HEAD, size), WIDE)
            total = jnp.zeros((1, size), WIDE)
            following = scores_of(0)
            for number in range(count):
                scores = following
                if number + 1 < count:
                    following = scores_of(number + 1)
                probs = jnp.exp2(scores)
                total = total + jnp.sum(probs, axis=0, keepdims=True)
                gathered = gathered + dot(values_of(number), probs.astype(LOW))
            finish(gathered, total, 0.0)

        @pl.when(jnp.logical_not(bounded))
        def _():
            gathered = jnp.zeros((HEAD, size), WIDE)
            top = jnp.full((1, size), -1e30, WIDE)
            total = jnp.zeros((1, size), WIDE)
            following = scores_of(0)
            for number in range(count):
                scores = following
                if number + 1 < count:
                    following = scores_of(number + 1)
                raised = jnp.maximum(top, jnp.max(scores, axis=0, keepdims=True))
                shrink = jnp.exp2(top - raised)
                probs = jnp.exp2(scores - raised)
                total = total * shrink + jnp.sum(probs, axis=0, keepdims=True)
                gathered = gathered * shrink + dot(values_of(number), probs.astype(LOW))
                top = raised
            finish(gathered, total, top)

    return call(
        kernel,
        "attend",
        ids,
        (length // size,),
        [parts, *before],
        [whole(parts.shape)] + [anywhere] * len(before),
        [
            low_array(members, heads * HEAD, tokens),
            wide_array(HEAD, length),
            wide_array(1, length),
        ],
        [
            pl.BlockSpec((members, HEAD, tokens), lambda i, ids: (0, head, 0)),
            pl.BlockSpec((HEAD, size), lambda i, ids: (0, i)),
            pl.BlockSpec((1, size), lambda i, ids: (0, i)),
        ],
        [pltpu.VMEM((length, 2 * HEAD), LOW), pltpu.VMEM((1, 1), WIDE)],
        after,
        aliases={2: 0} if before else {},
        time=18,
    )


def middle_part(ids, front, backs, members, weight, tokens, upstream, late, frames, after=()):
    rows = tokens.shape[1]
    size = rows // frames
    group = D // members
    parts = [front] * (front is not None) + list(backs)

    def kernel(ids_ref, *refs):
        part_refs = list(refs[: len(parts)])
        weight_ref, tokens_ref, g_own, g_other, late_ref = refs[len(parts) : len(parts) + 5]
        low_ref, projected_ref, middle_ref, normed_ref, grad_ref, across = refs[len(parts) + 5 :]
        if front is not None:
            front_ref = part_refs.pop(0)
            for member in range(members):
                across[member * group : member * group + group - HEAD, :] = front_ref[member]
        for member, ref in enumerate(part_refs):
            at = pl.multiple_of((ids_ref[0] ^ member) * group + group - HEAD, HEAD)
            across[pl.ds(at, HEAD), :] = ref[...]
        low = across[...]
        low_ref[...] = low
        projected = dot(low.T, weight_ref[...].reshape(D, D))
        projected_ref[...] = projected
        middle = tokens_ref[0].astype(WIDE) + piece(late_ref, 0, frames) * projected
        middle_ref[...] = middle
        normed, _ = norm_parts(middle)
        shift, scale = piece(late_ref, 1, frames), piece(late_ref, 2, frames)
        normed_ref[...] = (normed * (1.0 + scale) + shift).astype(LOW)
        upstream = read_pair(ids_ref, g_own, g_other)
        grad_ref[...] = (piece(late_ref, 3, frames) * upstream).astype(LOW)

    part_specs = [
        pl.BlockSpec(
            part.shape[:-1] + (size,),
            lambda r, f, ids, lead=part.ndim - 1: (0,) * lead + (r * frames + f,),
        )
        for part in parts
    ]
    return call(
        kernel,
        "middle_part",
        ids,
        (2, frames),
        [*parts, weight[0], tokens, *upstream, late],
        part_specs
        + [weight[1], chunk_spec(rows, frames)]
        + pair_specs(rows, frames)
        + [whole(late.shape)],
        [
            low_array(D, 2 * rows),
            wide_array(2 * rows, D),
            wide_array(2 * rows, D),
            low_array(2 * rows, D),
            low_array(2 * rows, D),
        ],
        [column_spec(rows, frames)] + [row_spec(rows, frames)] * 4,
        [pltpu.VMEM((D, size), LOW)],
        after,
        time=12,
    )


def quarter_at(step, ids, core_mask, pairs):
    core = bit_of(ids[2], core_mask)
    return step % pairs * 2 + jnp.where(step < pairs, 1 - core, core)


def feed(ids, rows, grads, up, down, hidden, devices, kind, after=()):
    tokens, width = rows.shape
    chunk = 512
    own_up, own_down = width // devices, hidden // devices
    aside, down_blocks = width // chunk, chunk // own_down
    steps = hidden // chunk
    own_rows = own_down + own_up * (hidden // width) + own_up

    def kernel(
        ids_ref,
        rows_ref,
        grad_ref,
        up_ref,
        down_ref,
        branch_ref,
        back_ref,
        out_ref,
        across,
        down_rows,
        up_rows,
        sems,
    ):
        step = pl.program_id(0)
        slot = step % 2

        def copies(step, slot):
            first = own_down + step // aside * own_up
            return (
                pltpu.make_async_copy(
                    down_rows.at[slot],
                    out_ref.at[pl.ds(step * down_blocks, down_blocks), pl.ds(0, own_down)],
                    sems.at[0, slot],
                ),
                pltpu.make_async_copy(
                    up_rows.at[slot],
                    out_ref.at[
                        :,
                        pl.ds(pl.multiple_of(first, own_up), own_up),
                        pl.ds(pl.multiple_of(step % aside * chunk, chunk), chunk),
                    ],
                    sems.at[1, slot],
                ),
            )

        @pl.when(step == 0)
        def _():
            across[...] = rows_ref[...].T
            branch_ref[...] = jnp.zeros_like(branch_ref)
            back_ref[...] = jnp.zeros_like(back_ref)

        @pl.when(step >= 2)
        def _():
            for copy in copies(step - 2, slot):
                copy.wait()

        grads = grad_ref[...]
        up, down = up_ref[...].reshape(width, chunk), down_ref[...].reshape(chunk, width)
        upper = dot(rows_ref[...], up)
        hidden_grad = dot(grads, down.T)
        root = math.sqrt(2 / math.pi)
        square = upper * upper
        curve = jnp.tanh(upper * (root + root * 0.044715 * square))
        share = 0.5 + 0.5 * curve
        low = (upper * share).astype(LOW)
        slope = share + 0.5 * upper * (1.0 - curve * curve) * (root + 3 * root * 0.044715 * square)
        upper_grad = (hidden_grad * slope).astype(LOW)
        branch_ref[...] += dot(low, down)
        back_ref[...] += dot(upper_grad, up.T)
        down_grad = dot(low.T, grads).astype(kind)
        up_grad = dot(across[...], upper_grad).astype(kind)
        down_rows[slot] = down_grad.reshape(down_rows.shape[1:])
        up_rows[slot] = up_grad.reshape(up_rows.shape[1:])
        for copy in copies(step, slot):
            copy.start()

        @pl.when(step == steps - 1)
        def _():
            for copy in copies(step - 1, 1 - slot) + copies(step, slot):
                copy.wait()

    return call(
        kernel,
        "feed",
        ids,
        (steps,),
        [rows, grads, up[0], down[0]],
        [
            whole((tokens, width)),
            whole((tokens, width)),
            pl.BlockSpec(up[1], lambda step, ids: up[2](step)),
            pl.BlockSpec(down[1], lambda step, ids: down[2](step)),
        ],
        [
            wide_array(tokens, width),
            wide_array(tokens, width),
            jax.ShapeDtypeStruct((devices, own_rows, width), kind),
        ],
        [whole((tokens, width)), whole((tokens, width)), anywhere],
        [
            pltpu.VMEM((width, tokens), LOW),
            pltpu.VMEM((2, down_blocks, own_down, width), kind),
            pltpu.VMEM((2, devices, own_up, chunk), kind),
            pltpu.SemaphoreType.DMA((2, 2)),
        ],
        after,
        room=62,
        time=64,
    )


def middle_back(ids, middle, branch, back, projected, upstream, late, frames, after=()):
    rows = upstream[1].shape[0]

    def kernel(
        ids_ref,
        middle_ref,
        branch_ref,
        back_ref,
        projected_ref,
        g_own,
        g_other,
        late_ref,
        result_ref,
        middle_grad_ref,
        projected_grad_ref,
        pieces_ref,
    ):
        middle, branch = middle_ref[...], branch_ref[...]
        upstream = read_pair(ids_ref, g_own, g_other)
        result_ref[0] = (middle + piece(late_ref, 3, frames) * branch).astype(LOW)
        normed, inverse = norm_parts(middle)
        grad, shift_grad, scale_grad = norm_back(
            back_ref[...], normed, inverse, piece(late_ref, 2, frames)
        )
        grad = grad + upstream
        middle_grad_ref[...] = grad
        projected_grad_ref[...] = (piece(late_ref, 0, frames) * grad).astype(LOW)
        gate_grad = jnp.sum(grad * projected_ref[...], axis=0, keepdims=True)
        put_piece(pieces_ref, 0, frames, gate_grad)
        put_piece(pieces_ref, 1, frames, shift_grad)
        put_piece(pieces_ref, 2, frames, scale_grad)
        put_piece(pieces_ref, 3, frames, jnp.sum(upstream * branch, axis=0, keepdims=True))

    block = row_spec(rows, frames)
    return call(
        kernel,
        "middle_back",
        ids,
        (2, frames),
        [middle, branch, back, projected, *upstream, late],
        [block] * 4 + pair_specs(rows, frames) + [whole(late.shape)],
        [
            low_array(2, rows, D),
            wide_array(2 * rows, D),
            low_array(2 * rows, D),
            wide_array(2 * frames, 4 * D),
        ],
        [chunk_spec(rows, frames)] + [block] * 2 + [whole((2 * frames, 4 * D))],
        after=after,
        time=12,
    )


def put_half(step, pairs, value, sent_ref, kept_ref):
    @pl.when(step < pairs)
    def _():
        sent_ref[0] = value.astype(LOW)

    @pl.when(step >= pairs)
    def _():
        kept_ref[0] = value


def half_specs(pairs, rows, width, slot):
    return [
        pl.BlockSpec((1, rows, width), lambda i, ids: (jnp.minimum(i, pairs - 1), 0, slot)),
        pl.BlockSpec((1, rows, width), lambda i, ids: (jnp.maximum(i - pairs, 0), 0, slot)),
    ]


def hand_out(ids, weight, gradient, attended, into, members, steps, after=()):
    tokens, width = gradient.shape
    quarter = width // steps
    groups = members // steps
    group = width // members
    front = group - HEAD
    devices, own_rows, _ = into.shape
    own = width // devices

    def kernel(ids_ref, weight_ref, grad_ref, attended_ref, into_ref, *refs):
        gradient_ref, *out_refs = refs
        step = pl.program_id(0)
        grads = grad_ref[...]
        if weight_ref.shape[0] == 1:
            taken = weight_ref[0, pl.ds(pl.multiple_of(step * quarter, quarter), quarter), :]
        else:
            blocks = quarter // weight_ref.shape[1]
            taken = weight_ref[pl.ds(step * blocks, blocks)].reshape(quarter, width)
        block = contract(taken, grads, 1, 1).astype(LOW)
        for number in range(groups):
            at = number * group
            out_refs[0][number] = block[at + front : at + group]
            if front:
                out_refs[1][number] = block[at : at + front]
        value = dot(attended_ref[...], grads).astype(into.dtype)
        gradient_ref[...] = value.reshape(gradient_ref.shape)

    shapes = [(members, HEAD, tokens)] + [(members, front, tokens)] * (front > 0)
    return call(
        kernel,
        "hand_out",
        ids,
        (steps,),
        [weight[0], gradient, attended, into],
        [
            weight[1],
            whole(gradient.shape),
            pl.BlockSpec((quarter, tokens), lambda i, ids: (i, 0)),
            anywhere,
        ],
        [jax.ShapeDtypeStruct(into.shape, into.dtype)]
        + [low_array(*shape) for shape in shapes],
        [pl.BlockSpec((quarter // own, own, width), lambda i, ids: (i, own_rows // own - 1, 0))]
        + [pl.BlockSpec((groups,) + shape[1:], lambda i, ids: (i, 0, 0)) for shape in shapes],
        after=after,
        aliases={4: 0},
        time=9,
    )


def turn_back(operand, cosines, sines):
    half = HEAD // 2
    one, two = operand[:half], operand[half:]
    return jnp.concatenate([one * cosines + two * sines, two * cosines - one * sines], axis=0)


def attend_back(ids, parts, grads, head, wide, total, cosines, sines, after=()):
    members, _, _, tokens = parts.shape
    size, block = min(1024, tokens), min(512, tokens)
    length = members * tokens
    per, count = tokens // size, length // block
    back = HEAD ** (-0.5)

    def kernel(
        ids_ref,
        part_ref,
        grad_ref,
        wide_ref,
        total_ref,
        cos_ref,
        sin_ref,
        out_ref,
        key_rows,
        key_more,
        value_more,
        key_sum,
        value_sum,
    ):
        step = pl.program_id(0)

        @pl.when(step == 0)
        def _():
            for member in range(members):
                span = slice(member * tokens, (member + 1) * tokens)
                key_rows[span, :] = part_ref[member, 1].T
                key_more[:HEAD, span] = part_ref[member, 1]
                value_more[:HEAD, span] = part_ref[member, 2]
            key_more[HEAD:, :] = jnp.full((16, length), -1.0, LOW)
            value_more[HEAD:, :] = jnp.full((16, length), -1.0, LOW)
            key_sum[...] = jnp.zeros_like(key_sum)
            value_sum[...] = jnp.zeros_like(value_sum)

        member = step // per
        start = 0 if per == 1 else pl.multiple_of(step % per * size, size)
        queries_across = part_ref[member, 0, :, pl.ds(start, size)]
        grads_across = grad_ref[member, :, pl.ds(start, size)]
        delta = jnp.sum(grads_across.astype(WIDE) * wide_ref[...], axis=0, keepdims=True)

        def less(rows, amount):
            high = amount.astype(LOW)
            middle, low = two_lows(amount - high.astype(WIDE))
            spare = jnp.zeros((13, size), LOW)
            return jnp.concatenate([rows, high, middle, low, spare], axis=0).T

        queries = less(queries_across, total_ref[...] * (1 / SOFT))
        out_grads = less(grads_across, delta)
        query_grad = jnp.zeros((size, HEAD), WIDE)

        def pair(number):
            here = slice(number * block, (number + 1) * block)
            return dot(queries, key_more[:, here]), dot(out_grads, value_more[:, here])

        following = pair(0)
        for number in range(count):
            scores, prob_grad = following
            if number + 1 < count:
                following = pair(number + 1)
            here = slice(number * block, (number + 1) * block)
            probs = jnp.exp2(scores * SOFT)
            score_grad = (probs * prob_grad).astype(LOW)
            value_sum[:, here] += dot(grads_across, probs.astype(LOW))
            key_sum[:, here] += dot(queries_across, score_grad)
            query_grad += dot(score_grad, key_rows[here, :])

        where = pl.multiple_of(step * size, size)
        out_ref[member, 0, :, pl.ds(start, size)] = turn_back(
            query_grad.T * back, cos_ref[:, pl.ds(where, size)], sin_ref[:, pl.ds(where, size)]
        ).astype(LOW)

        @pl.when(step == length // size - 1)
        def _():
            for source in range(members):
                span = slice(source * tokens, (source + 1) * tokens)
                out_ref[source, 1] = turn_back(
                    key_sum[:, span] * back, cos_ref[:, span], sin_ref[:, span]
                ).astype(LOW)
                out_ref[source, 2] = value_sum[:, span].astype(LOW)

    return call(
        kernel,
        "attend_back",
        ids,
        (length // size,),
        [parts, grads, wide, total, cosines, sines],
        [
            whole(parts.shape),
            pl.BlockSpec((members, HEAD, tokens), lambda i, ids: (0, head, 0)),
            pl.BlockSpec((HEAD, size), lambda i, ids: (0, i)),
            pl.BlockSpec((1, size), lambda i, ids: (0, i)),
            whole(cosines.shape),
            whole(sines.shape),
        ],
        low_array(members, 3, HEAD, tokens),
        whole((members, 3, HEAD, tokens)),
        [
            pltpu.VMEM((length, HEAD), LOW),
            pltpu.VMEM((HEAD + 16, length), LOW),
            pltpu.VMEM((HEAD + 16, length), LOW),
            pltpu.VMEM((HEAD, length), WIDE),
            pltpu.VMEM((HEAD, length), WIDE),
        ],
        after,
        time=26,
    )


def joint_back(
    ids, parts, normed, weight, column, total, core_mask, pairs, into, slot, slots, after=()
):
    members, _, _, tokens = parts.shape
    group = members * HEAD
    width = 3 * group
    quarter = D // (2 * pairs)
    halves = (pairs, quarter, slots * width)
    before = [] if total is None else [total]
    held = [] if into is None else list(into)

    def kernel(ids_ref, part_ref, normed_ref, weight_ref, *refs):
        refs = list(refs)
        total_refs = [refs.pop(0) for _ in before]
        sent_ref, kept_ref, total_ref, across, lined = refs[len(held) :]
        step = pl.program_id(0)

        @pl.when(step == 0)
        def _():
            for member in range(members):
                for kind in range(3):
                    at = kind * group + member * HEAD
                    across[at : at + HEAD, :] = part_ref[member, kind]
            lined[...] = across[...].T

        rows = lined[...]
        put_half(step, pairs, dot(normed_ref[...], rows), sent_ref, kept_ref)
        added = contract(rows, weight_ref[...], 1, 1)
        total_ref[...] = total_refs[0][...] + added if total_refs else added

    def at(i, ids):
        return quarter_at(i, ids, core_mask, pairs)

    strip = pl.BlockSpec((tokens, quarter), lambda i, ids: (0, at(i, ids)))
    first = 4 + len(before)
    return call(
        kernel,
        "joint_back",
        ids,
        (2 * pairs,),
        [parts, normed, weight, *before, *held],
        [
            whole(parts.shape),
            pl.BlockSpec((quarter, tokens), lambda i, ids: (at(i, ids), 0)),
            pl.BlockSpec((quarter, width), lambda i, ids: (at(i, ids), column)),
        ]
        + [strip] * len(before)
        + [anywhere] * len(held),
        [low_array(*halves), wide_array(*halves), wide_array(tokens, D)],
        half_specs(pairs, quarter, width, slot) + [strip],
        [pltpu.VMEM((width, tokens), LOW), pltpu.VMEM((tokens, width), LOW)],
        after,
        aliases={first: 0, first + 1: 1} if held else {},
        time=13,
    )


def tokens_back(ids, gradient, tokens, middle_grad, early, frames, after=()):
    rows = tokens.shape[1]
    size = rows // frames

    def kernel(
        ids_ref, grad_ref, tokens_ref, middle_ref, early_ref, own_ref, other_ref, pieces_ref
    ):
        normed, inverse = norm_parts(tokens_ref[0].astype(WIDE))
        grad, shift_grad, scale_grad = norm_back(
            grad_ref[...], normed, inverse, piece(early_ref, 1, frames)
        )
        grad = grad + middle_ref[...]
        put_piece(pieces_ref, 0, frames, shift_grad)
        put_piece(pieces_ref, 1, frames, scale_grad)

        @pl.when(pl.program_id(0) == ids_ref[1])
        def _():
            own_ref[0] = grad

        @pl.when(pl.program_id(0) != ids_ref[1])
        def _():
            other_ref[...] = grad.astype(LOW)

    def chunk_at(number):
        def index(r, f, ids):
            mine = ids[1] if number == 0 else 1 - ids[1]
            return (jnp.where(r == mine, f, jnp.where(r < mine, 0, frames - 1)), 0)

        return index

    block = row_spec(rows, frames)
    return call(
        kernel,
        "tokens_back",
        ids,
        (2, frames),
        [gradient, tokens, middle_grad, early],
        [block, chunk_spec(rows, frames), block, whole(early.shape)],
        [wide_array(2, rows, D), low_array(rows, D), wide_array(2 * frames, 2 * D)],
        [
            pl.BlockSpec((1, size, D), lambda r, f, ids: (ids[1], *chunk_at(0)(r, f, ids))),
            pl.BlockSpec((size, D), chunk_at(1)),
            whole((2 * frames, 2 * D)),
        ],
        after=after,
        time=9,
    )


def fill_clip(ids, held, others, after=()):
    size = held.shape[1] // 2
    if len(others) == 1:
        other_specs = [pl.BlockSpec((size, D), lambda f, ids: (f, 0))]
    else:
        other_specs = [whole((size, D))] * 2

    def kernel(ids_ref, held_ref, *refs):
        *other_refs, out_ref = refs
        for number, ref in enumerate(other_refs):
            here = pl.program_id(0) == number if len(other_refs) == 2 else True

            @pl.when(here)
            def _(ref=ref):
                out_ref[0] = ref[...].astype(held.dtype)

    return call(
        kernel,
        "fill_clip",
        ids,
        (2,),
        [held, *others],
        [anywhere, *other_specs],
        jax.ShapeDtypeStruct(held.shape, held.dtype),
        pl.BlockSpec((1, size, D), lambda f, ids: (1 - ids[1], f, 0)),
        after=after,
        aliases={1: 0},
        time=4,
    )


def modulation_back(ids, condition, pieces, after=()):
    count, width = pieces.shape
    own = condition.shape[1]
    size = 1024

    def kernel(ids_ref, condition_ref, pieces_ref, out_ref, sum_ref):
        pieces = pieces_ref[...]
        out_ref[...] = lax.dot_general(
            condition_ref[...].astype(WIDE).T,
            pieces,
            (((1,), (0,)), ((), ())),
            precision=highest,
            preferred_element_type=WIDE,
        )
        sum_ref[...] = jnp.sum(pieces, axis=0, keepdims=True)

    return call(
        kernel,
        "modulation_back",
        ids,
        (width // size,),
        [condition, pieces],
        [whole(condition.shape), pl.BlockSpec((count, size), lambda i, ids: (0, i))],
        [wide_array(own, width), wide_array(1, width)],
        [
            pl.BlockSpec((own, size), lambda i, ids: (0, i)),
            pl.BlockSpec((1, size), lambda i, ids: (0, i)),
        ],
        after=after,
        time=4,
    )


def join_and_add(ids, joins, adds, after=()):
    ins, outs = [], []
    for own, arrived, _ in joins:
        ins += [own, arrived]
        pre, post, width = own.shape
        outs.append(jax.ShapeDtypeStruct((pre, 2, post, width), own.dtype))
    for kept, arrived, final in adds:
        ins += [kept, arrived]
        rows, width = kept.shape
        outs += [wide_array(rows, width)] if final else [wide_array(rows // 2, width)] * 2

    def kernel(ids_ref, *refs):
        in_refs, out_refs = list(refs[: len(ins)]), list(refs[len(ins) :])
        for _, _, mask in joins:
            own, arrived, out = in_refs.pop(0), in_refs.pop(0), out_refs.pop(0)
            bit = bit_of(ids_ref[2], mask)
            for row in range(own.shape[0]):
                out[row, pl.ds(bit, 1)] = own[row][None]
                out[row, pl.ds(1 - bit, 1)] = arrived[row][None]
        for _, _, final in adds:
            kept, arrived = in_refs.pop(0), in_refs.pop(0)
            rows = kept.shape[0]
            if final:
                out_refs.pop(0)[...] = kept[...] + arrived[...]
            else:
                for start in (0, rows // 2):
                    span = slice(start, start + rows // 2)
                    out_refs.pop(0)[...] = kept[span] + arrived[span]

    return call(
        kernel,
        "join_and_add",
        ids,
        (1,),
        ins,
        [whole(value.shape) for value in ins],
        outs,
        [whole(out.shape) for out in outs],
        after=after,
        time=3,
    )


def stack_rows(ids, values, after=()):
    count, width = values[0].shape

    def kernel(ids_ref, *refs):
        for number, ref in enumerate(refs[:-1]):
            refs[-1][number * count : (number + 1) * count] = ref[...]

    return call(
        kernel,
        "stack_rows",
        ids,
        (1,),
        values,
        [whole(values[0].shape)] * len(values),
        wide_array(len(values) * count, width),
        whole((len(values) * count, width)),
        after=after,
        time=1,
    )


def fold(ids, kept, arrived, count, after=()):
    rows, width = kept.shape
    part = rows // count

    def kernel(ids_ref, *refs):
        in_refs, out_refs = refs[: 1 + len(arrived)], refs[1 + len(arrived) :]
        for number, out in enumerate(out_refs):
            span = slice(number * part, (number + 1) * part)
            out[...] = sum(ref[span] for ref in in_refs)

    return call(
        kernel,
        "fold",
        ids,
        (1,),
        [kept, *arrived],
        [whole(kept.shape)] * (1 + len(arrived)),
        [wide_array(part, width)] * count,
        [whole((part, width))] * count,
        after=after,
        time=3,
    )


def pack(ids, down, up, output, after=()):
    count = down.shape[0] + up.shape[0] * (up.shape[1] // D) + output.shape[0]

    def kernel(ids_ref, down_ref, up_ref, output_ref, out_ref):
        at = 0
        pieces = [down_ref[...]]
        pieces += [up_ref[:, i * D : (i + 1) * D] for i in range(up.shape[1] // D)]
        for value in pieces + [output_ref[...]]:
            out_ref[at : at + value.shape[0]] = value.astype(LOW)
            at += value.shape[0]

    return call(
        kernel,
        "pack",
        ids,
        (1,),
        [down, up, output],
        [whole(down.shape), whole(up.shape), whole(output.shape)],
        low_array(count, D),
        whole((count, D)),
        after=after,
        time=3,
    )


def other_clip(ids, tokens, frames, after=()):
    rows = tokens.shape[1]
    size = rows // frames

    def kernel(ids_ref, in_ref, out_ref):
        out_ref[...] = in_ref[0]

    return call(
        kernel,
        "other_clip",
        ids,
        (frames,),
        [tokens],
        [pl.BlockSpec((1, size, D), lambda f, ids: (1 - ids[1], f, 0))],
        low_array(rows, D),
        pl.BlockSpec((size, D), lambda f, ids: (f, 0)),
        after=after,
    )


def settle(ids, rows, own_down, blocks, after=()):
    own = (rows.shape[0] - own_down) // (blocks + 1)

    def kernel(ids_ref, rows_ref, down_out, up_out, output_out):
        down_out[...] = rows_ref[:own_down].astype(WIDE)
        for number in range(blocks):
            at = own_down + number * own
            up_out[:, number * D : (number + 1) * D] = rows_ref[at : at + own].astype(WIDE)
        output_out[...] = rows_ref[own_down + blocks * own :].astype(WIDE)

    shapes = [(own_down, D), (own, blocks * D), (own, D)]
    return call(
        kernel,
        "settle",
        ids,
        (1,),
        [rows],
        [whole(rows.shape)],
        [wide_array(*shape) for shape in shapes],
        [whole(shape) for shape in shapes],
        after=after,
    )


def copy_of(ids, value, after=()):
    def kernel(ids_ref, in_ref, out_ref):
        out_ref[...] = in_ref[...]

    return call(
        kernel,
        "copy_of",
        ids,
        (1,),
        [value],
        [whole(value.shape)],
        jax.ShapeDtypeStruct(value.shape, value.dtype),
        whole(value.shape),
        after=after,
    )


def split_four(ids, kept, arrived, blocks_of, masks, after=()):
    rows = kept.shape[1:]
    ins = [kept, *arrived]
    if not masks:

        def add(ids_ref, *refs):
            *in_refs, out_ref = refs
            out_ref[...] = sum(ref[...].astype(WIDE) for ref in in_refs)

        return call(
            add,
            "split_four",
            ids,
            (1,),
            ins,
            [whole(kept.shape)] * len(ins),
            wide_array(*kept.shape),
            whole(kept.shape),
            after=after,
        )
    pre, mid, post = blocks_of
    high, low = masks

    def kernel(ids_ref, *refs):
        in_refs, out_refs = refs[: len(ins)], refs[len(ins) :]
        bits = bit_of(ids_ref[2], high), bit_of(ids_ref[2], low)
        for out, (across, aside) in zip(out_refs, ((0, 0), (1, 0), (0, 1), (1, 1))):
            first = 1 - bits[0] if across else bits[0]
            second = 1 - bits[1] if aside else bits[1]
            for one in range(pre):
                for two in range(post):
                    value = sum(ref[one, first, 0, second, two].astype(WIDE) for ref in in_refs)
                    out[one, 0, two] = value.astype(out.dtype)

    shape = (pre, 2, mid, 2, post) + rows
    lead = (pre, 2, 1, 2, post) + rows
    out_shape = (pre, mid, post) + rows
    zeros = (0,) * len(rows)
    return call(
        kernel,
        "split_four",
        ids,
        (mid,),
        [value.reshape(shape) for value in ins],
        [pl.BlockSpec(lead, lambda i, ids: (0, 0, i, 0, 0) + zeros)] * len(ins),
        [wide_array(*out_shape)] + [low_array(*out_shape)] * 3,
        [pl.BlockSpec((pre, 1, post) + rows, lambda i, ids: (0, i, 0) + zeros)] * 4,
        after=after,
        time=3,
    )


def halve_plain(rank, jobs):
    outs = []
    for kept, arrived, post, mask in jobs:
        value = kept.astype(WIDE) + arrived.astype(WIDE)
        if not post:
            outs.append(value)
            continue
        split = value.reshape((-1, 2, post) + value.shape[1:])
        for side in (1 - bit_of(rank, mask), bit_of(rank, mask)):
            taken = lax.dynamic_index_in_dim(split, side, 1, keepdims=False)
            outs.append(taken.reshape((-1,) + value.shape[1:]))
        outs[-2] = outs[-2].astype(LOW)
    return outs


def per_device(
    clip_size,
    seq_size,
    frames_in,
    noise_level,
    frame_time,
    cotangent,
    joint_weight,
    output_weight,
    up_weight,
    down_weight,
    modulation,
    modulation_bias,
    first_joint,
    first_output,
    first_up,
    first_down,
    first_modulation,
    first_bias,
    second_joint,
    second_output,
    second_up,
    second_down,
    second_modulation,
    second_bias,
):
    devices = clip_size * seq_size
    masters = (joint_weight, output_weight, up_weight, down_weight, modulation, modulation_bias)
    firsts = (first_joint, first_output, first_up, first_down, first_modulation, first_bias)
    seconds = (second_joint, second_output, second_up, second_down, second_modulation, second_bias)
    clip_id, seq_id = lax.axis_index("clip"), lax.axis_index("seq")
    rank = clip_id * seq_size + seq_id
    half = seq_size // 2
    side = seq_id // half
    members = half
    ids = jnp.stack([seq_id % half, side, rank]).astype(jnp.int32)
    head_count = HEADS // members
    group_ids = [[i * half + j for j in range(half)] for i in range(2)]
    last = []

    def swap_with(value, mask):
        return lax.ppermute(value, AXES, [(i, i ^ mask) for i in range(devices)])

    def pick(value, index):
        return lax.dynamic_index_in_dim(value, index, 0, keepdims=False)

    def run(kernel, *args, **options):
        result = kernel(ids, *args, after=tuple(last), **options)
        last[:] = jax.tree.leaves(result)[-1:]
        return result

    clip_masks = [seq_size << bit for bit in range(clip_size.bit_length() - 1)]
    seq_masks = [1 << bit for bit in range(seq_size.bit_length() - 1)]
    order = clip_masks + seq_masks
    core_mask = clip_masks[0]
    pairs = clip_size // 2

    local_rows = frames_in.shape[1]
    frames = max(1, local_rows // PATCHES)
    tokens_here = 2 * local_rows
    pair_ids = [[j, j + half] for j in range(half)]
    tokens = lax.all_to_all(frames_in, "seq", 0, 0, axis_index_groups=pair_ids)

    levels = noise_level.astype(WIDE)[None]
    for mask in clip_masks:
        levels = jnp.concatenate([levels, swap_with(levels, mask)], axis=0)
    all_levels = levels.reshape(-1)
    masks = [0]
    for mask in reversed(order):
        masks = masks + [other ^ mask for other in masks]
    own_width = modulation.shape[0]
    columns = rank * own_width + jnp.arange(own_width, dtype=jnp.int32)
    half_width = D // 2
    frequency = jnp.exp(-math.log(10000.0) * (columns % half_width).astype(WIDE) / half_width)

    def condition_of(targets):
        seq_of = targets % seq_size
        chunk = jnp.stack([seq_of % half, seq_of % half + half], axis=1)
        frame_of = chunk[:, :, None] * local_rows // PATCHES + jnp.arange(frames, dtype=jnp.int32)
        clip_of = (targets // seq_size ^ clip_id) * 2 + seq_of // half
        level_ids = (clip_of[:, None, None] * FRAMES + frame_of).reshape(-1)
        every = jnp.arange(all_levels.shape[0], dtype=jnp.int32)
        level_of = jnp.sum(jnp.where(level_ids[:, None] == every, all_levels, 0.0), axis=1)
        angles = level_of[:, None] * frequency
        wave = jnp.where(columns < half_width, jnp.cos(angles), jnp.sin(angles))
        return jax.nn.silu(wave).astype(LOW)

    condition = condition_of(rank ^ jnp.array(masks, jnp.int32))

    bias_width = modulation_bias.shape[0]
    bias_row = lax.dynamic_update_slice_in_dim(
        jnp.zeros((6 * D,), WIDE), modulation_bias.astype(LOW).astype(WIDE), rank * bias_width, 0
    )
    modulation_low = modulation.astype(LOW)

    class Terms:
        def __init__(self, condition, first, stop):
            terms = dot(condition, modulation_low[:, first:stop]) + bias_row[first:stop]
            middle = terms.shape[0] // 2
            self.kept, self.sent = terms[:middle], terms[middle:]
            self.masks = order[:]
            self.send()

        def send(self):
            self.arrived = swap_with(self.sent, self.masks.pop(0))

        def job(self):
            return (self.kept, self.arrived, not self.masks)

        def take(self, outs):
            self.kept = outs.pop(0)
            if self.masks:
                self.sent = outs.pop(0)
                self.send()

    rows = joint_weight.shape[0]
    joint_low = joint_weight.astype(LOW).reshape(rows, 3, members, head_count, HEAD)
    joint_low = jnp.transpose(joint_low, (0, 3, 1, 2, 4)).reshape(1, rows, 3 * D)
    far = seq_masks[:0:-1]
    routes = [
        far + [seq_masks[0]] + clip_masks[::-1],
        far + clip_masks[:0:-1] + [seq_masks[0], clip_masks[0]],
    ]
    joined = [joint_low]
    early_terms = None
    packed = run(pack, down_weight, up_weight, output_weight)
    packed = lax.all_gather(packed, AXES, axis=0, tiled=False)
    for stage in range(len(order) + 1):
        joins = []
        if stage < len(order):
            if stage == len(far):
                middle_column = joint_low.shape[2] // 2
                joined = [joined[0][..., :middle_column], joined[0][..., middle_column:]]
            for value, route in zip(joined, routes):
                mask, done = route[stage], route[:stage]
                pre = 2 ** sum(1 for other in done if other > mask)
                width = value.shape[-1]
                own = value.reshape(pre, -1, width)
                arrived = swap_with(value, mask).reshape(pre, -1, width)
                joins.append((own, arrived, mask))
        if stage == 1:
            early_terms = Terms(condition, 0, 2 * D)
        adds = [early_terms.job()] if stage else []
        if stage == 3:
            last.append(tokens)
        outs = list(run(join_and_add, joins, adds))
        if stage < len(order):
            joined = [outs.pop(0) for _ in joins]
            joined = [value.reshape(1, -1, value.shape[-1]) for value in joined]
        if stage:
            early_terms.take(outs)
    early = early_terms.kept
    joint_sides = [value[0] for value in joined]
    if head_count % 2:
        joint_sides = [jnp.concatenate(joint_sides, axis=1)]
    heads_aside = head_count // len(joint_sides)

    up_blocks = FF // D
    own_up = up_weight.shape[0]
    own_down = down_weight.shape[0]
    tiled = own_up % 16 == 0
    chunk_rows = 512
    up_first = own_down // own_up
    if tiled:
        chunks_aside = D // chunk_rows
        up_source = (
            packed,
            (devices, own_up, chunk_rows),
            lambda at: (0, up_first + at // chunks_aside, at % chunks_aside),
        )
        output_source = (
            packed,
            pl.BlockSpec((devices, own_up, D), lambda *at: (0, up_first + up_blocks, 0)),
        )
    else:
        upward = packed[:, own_down : own_down + own_up * up_blocks]
        upward = jnp.transpose(
            upward.reshape(devices, up_blocks, own_up, D), (0, 2, 1, 3)
        ).reshape(1, D, FF)
        up_source = (upward, (1, D, chunk_rows), lambda at: (0, 0, at))
        output_full = packed[:, own_down + own_up * up_blocks :].reshape(1, D, D)
        output_source = (output_full, whole((1, D, D)))
    down_source = (packed, (chunk_rows // own_down, own_down, D), lambda at: (at, 0, 0))

    member_seq = side * half + jnp.arange(members, dtype=jnp.int32)
    starts = jnp.stack([member_seq % half, member_seq % half + half], axis=1) * local_rows
    places = (starts[:, :, None] + jnp.arange(local_rows, dtype=jnp.int32)).reshape(-1)
    cosines, sines = rotary_tables(pick(frame_time, side), places)

    normed_across = run(norm_one, tokens, early, frames)

    def exchange(value):
        return lax.all_to_all(value, "seq", 0, 0, axis_index_groups=group_ids)

    class Late:
        def __init__(self, condition):
            terms = dot(condition, modulation_low[:, 2 * D :]) + bias_row[2 * D :]
            self.groups = [(core_mask,)]
            self.groups += [tuple(order[i : i + 2]) for i in range(1, len(order), 2)]
            count = terms.shape[0] // 2
            self.take([terms[:count], terms[count:]])

        def take(self, parts):
            self.kept, *sent = parts
            self.arrived = None
            if sent:
                group = self.groups.pop(0)
                ways = group if len(group) == 1 else (group[1], group[0], group[0] ^ group[1])
                self.arrived = [swap_with(value, mask) for value, mask in zip(sent, ways)]

        def step(self):
            if self.arrived is not None:
                count = 2 ** len(self.groups[0]) if self.groups else 1
                self.take(run(fold, self.kept, self.arrived, count))

    def project_head(head):
        weight, offset = joint_sides[head // heads_aside], head % heads_aside
        return exchange(
            run(project, normed_across, weight, cosines, sines, members, offset)
        )

    parts = {0: project_head(0)}
    late_terms = Late(run(copy_of, condition))
    wide, totals = {}, {}
    front = None
    front_heads = head_count - 1
    for head in range(head_count):
        if head + 1 < head_count:
            parts[head + 1] = project_head(head + 1)
        if head == 0:
            late_terms.step()
        if head < front_heads:
            front, wide[head], totals[head] = run(
                attend, parts[head], front, head, front_heads, False
            )
            if head + 1 == front_heads:
                front = exchange(front)
        else:
            back, wide[head], totals[head] = run(attend, parts[head], None, 0, 1, True)
        if head < 2:
            late_terms.step()
        if head == 0:
            sent = run(other_clip, cotangent, frames)
            cut = local_rows // 2
            pieces = [swap_with(sent[:cut], half), swap_with(sent[cut:], half)]
        if 0 < head < 3:
            last.append(pieces[head - 1])
    while late_terms.arrived is not None:
        late_terms.step()
    late = late_terms.kept
    upstream = (cotangent, jnp.concatenate(pieces))
    backs = [swap_with(back[i], i) if i else back[i] for i in range(members)]

    attended_across, projected, middle, normed_two_low, branch_grad = run(
        middle_part, front, backs, members, output_source, tokens, upstream, late, frames
    )
    branch, normed_two_grad, weight_grads = run(
        feed,
        normed_two_low,
        branch_grad,
        up_source,
        down_source,
        FF,
        devices,
        LOW if tiled else WIDE,
    )

    class Chain:
        def __init__(self, sent, kept):
            self.kept = kept
            self.masks = [clip_masks[1], *seq_masks]
            self.arrived = [swap_with(sent.astype(LOW), core_mask)]

        def step(self):
            if self.arrived is None:
                return
            if not tiled:
                mask = self.masks.pop(0) if self.masks else None
                post = 2 ** sum(1 for other in self.masks if other < mask) if mask else 0
                outs = halve_plain(rank, [(self.kept, self.arrived[0], post, mask)])
                self.arrived = [swap_with(outs[0], mask)] if mask else None
                self.kept = outs[-1]
                return
            rows = self.kept.shape[1:]
            if not self.masks:
                self.kept = run(split_four, self.kept, self.arrived, None, None)
                self.arrived = None
                return
            pair = sorted((self.masks.pop(0), self.masks.pop(0)), reverse=True)
            pre = 2 ** sum(1 for other in self.masks if other > pair[0])
            post = 2 ** sum(1 for other in self.masks if other < pair[1])
            mid = 2 ** len(self.masks) // pre // post
            kept, *sent = run(split_four, self.kept, self.arrived, (pre, mid, post), pair)
            self.kept = kept.reshape((-1,) + rows)
            ways = (*pair, pair[0] ^ pair[1])
            self.arrived = [
                swap_with(value.reshape((-1,) + rows), mask) for value, mask in zip(sent, ways)
            ]

    def owners(value):
        return value.reshape(devices // 2, -1, value.shape[2])

    result, middle_grad, projected_grad, late_rows = run(
        middle_back, middle, branch, normed_two_grad, projected, upstream, late, frames
    )
    weight_grads, *outer = run(
        hand_out, output_source, projected_grad, attended_across, weight_grads, members, 2 * pairs
    )
    weight_sums = lax.psum_scatter(
        weight_grads.astype(LOW), AXES, scatter_dimension=0, tiled=True
    )[0]
    outer_back = exchange(outer[0])
    last.append(outer_back)

    class Frames:
        def __init__(self, rows, groups):
            self.rows, self.groups = rows, list(groups)
            self.send()

        def send(self):
            self.arrived = None
            if self.groups:
                group = self.groups.pop(0)
                masks = group if len(group) == 1 else (*group, group[0] ^ group[1])
                self.arrived = [swap_with(self.rows, mask) for mask in masks]

        def step(self):
            if self.arrived is not None:
                self.rows = run(stack_rows, [self.rows, *self.arrived])
                self.send()

    def ranks_of(groups):
        masks = [0]
        for mask in [mask for group in groups for mask in group]:
            masks = masks + [other ^ mask for other in masks]
        return rank ^ jnp.array(masks, jnp.int32)

    groups = [tuple(far[i : i + 2]) for i in range(0, len(far), 2)]
    groups += [(core_mask,), (seq_masks[0], clip_masks[1])]
    frames_condition = condition_of(ranks_of(groups))
    late_frames = Frames(late_rows, groups)
    late_frames.step()

    def head_back(head):
        grads, at = (outer_front, head) if head < front_heads else (outer_back, 0)
        return run(
            attend_back, parts[head], grads, at, wide[head], totals[head], cosines, sines
        )

    heads = list(reversed(range(head_count)))
    early_heads = heads[:2] if head_count > 3 else []
    last_heads = heads[len(early_heads) :]

    def head_joint(head, group, total, into):
        weight, offset = joint_sides[head // heads_aside], head % heads_aside
        sent, kept, total = run(
            joint_back,
            joint_parts[head],
            normed_across,
            weight,
            offset,
            total,
            core_mask,
            pairs,
            into,
            group.index(head),
            len(group),
        )
        return total, (sent, kept)

    joint_parts = {}
    total = early_chain = None
    outer_front = exchange(outer[1]) if front_heads else None
    for number, head in enumerate(heads):
        joint_parts[head] = exchange(head_back(head))
        if number < 3:
            late_frames.step()
        if number == 0:
            mixed_others = swap_with(pick(result, 1 - side), half)
        if number == 2 and early_heads:
            into = None
            for other in early_heads:
                total, into = head_joint(other, early_heads, total, into)
            early_chain = Chain(owners(into[0]), owners(into[1]))
        if number == 3:
            early_chain.step()
            mixed = run(fill_clip, result, [mixed_others])
            late_frames.step()
        if number == 2 and early_heads:
            early_chain.step()
    into = None
    for head in last_heads:
        total, into = head_joint(head, last_heads, total, into)
        if head == last_heads[0] and early_heads:
            while early_chain.arrived is not None:
                early_chain.step()
    last_chain = Chain(owners(into[0]), owners(into[1]))
    own_rows, other_rows, early_rows = run(
        tokens_back, total, tokens, middle_grad, early, frames
    )
    early_frames = Frames(early_rows, groups)
    middle_row = local_rows // 2
    others = [swap_with(other_rows[:middle_row], half)]
    last_chain.step()
    early_frames.step()
    if head_count < 4:
        mixed = run(fill_clip, result, [mixed_others])
    while late_frames.arrived is not None:
        late_frames.step()
    mod_late, sum_late = run(modulation_back, frames_condition, late_frames.rows)
    down_sum, up_sum, output_sum = run(settle, weight_sums, own_down, up_blocks)
    early_frames.step()
    last_chain.step()
    others.append(swap_with(run(copy_of, other_rows[middle_row:]), half))
    while early_frames.arrived is not None:
        early_frames.step()
    mod_early, sum_early = run(modulation_back, frames_condition, early_frames.rows)
    while last_chain.arrived is not None:
        last_chain.step()

    joint_heads = {}
    for chain, group in ((early_chain, early_heads), (last_chain, last_heads)):
        for slot, head in enumerate(group):
            width = 3 * D // head_count
            joint_heads[head] = chain.kept[0][:, slot * width : (slot + 1) * width]
    joint_sum = jnp.stack([joint_heads[head] for head in range(head_count)], axis=1)
    joint_sum = joint_sum.reshape(rows, head_count, 3, members, HEAD)
    joint_sum = jnp.transpose(joint_sum, (0, 2, 3, 1, 4)).reshape(rows, 3 * D)
    mod_sum = jnp.concatenate([mod_early, mod_late], axis=1)
    bias_sum = lax.dynamic_slice_in_dim(
        jnp.concatenate([sum_early[0], sum_late[0]]), rank * bias_width, bias_width, 0
    )

    summed = (joint_sum, output_sum, up_sum, down_sum, mod_sum, bias_sum)
    squares = sum(jnp.sum(shard * shard) for shard in summed).reshape(1, 1)
    for first, second in zip(order[::2], order[1::2]):
        squares = (squares + swap_with(squares, first)) + (
            swap_with(squares, second) + swap_with(squares, first ^ second)
        )
        last.append(squares)
    input_grad = run(fill_clip, own_rows, others)
    if len(order) % 2:
        squares = squares + swap_with(squares, order[-1])
    grad_norm = jnp.sqrt(squares[0, 0])
    factor = jnp.minimum(1.0, clip_limit / (grad_norm + 1e-06))
    step_rates = (
        D ** (-0.5),
        max(1, 2 * D // LENGTH) ** (-0.5),
        D ** (-0.5),
        FF ** (-0.5),
        D ** (-0.5),
        0.5,
    )
    clipped = [shard * factor for shard in summed]
    updates = [
        adam_update(clipped[slot], masters[slot], firsts[slot], seconds[slot], step_rates[slot])
        for slot in range(6)
    ]
    return (
        mixed,
        input_grad,
        *clipped,
        grad_norm,
        *(update[0] for update in updates),
        *(update[1] for update in updates),
        *(update[2] for update in updates),
        *(update[2].astype(LOW) for update in updates),
    )


def solution(mesh):
    tokens = P("clip", "seq", None)
    rows = P(AXES, None)
    weights = (rows, rows, rows, rows, rows, P(AXES))
    in_specs = (tokens, P("clip", None), P("clip", None), tokens) + weights * 3
    out_specs = (tokens, tokens) + weights + (P(),) + weights * 4
    return jax.shard_map(
        partial(per_device, mesh.shape["clip"], mesh.shape["seq"]),
        mesh=mesh,
        in_specs=in_specs,
        out_specs=out_specs,
        check_vma=False,
    )
```
